128 devices in a mesh: dp: 4 (over y), fsdp: 32 (over x, z, core).
Axes of the slice: x: 4, y: 4, z: 4, core: 2. Of those that a mesh axis runs over, the one named last changes fastest.
Arguments:
- tokens: bfloat16 [65536, 768], P(('dp', 'fsdp')), may hold values from -24 to 24
- segment_ids: int32 [128, 512], P(('dp', 'fsdp')), may hold values from 0 to 2, never falling along the last dimension, each value on 1 to 384 neighbouring positions
- qkv_weight: bfloat16 [768, 576], P(('dp', 'fsdp')), may hold values from -0.4375 to 0.4375
- out_weight: bfloat16 [768, 768], P(('dp', 'fsdp')), may hold values from -1.75 to 1.75
- up_weight: bfloat16 [768, 768], P(('dp', 'fsdp')), may hold values from -0.4375 to 0.4375
- down_weight: bfloat16 [3072, 192], P(('dp', 'fsdp')), may hold values from -0.21875 to 0.21875
- qv_bias: bfloat16 [2, 768], P(None, ('dp', 'fsdp')), may hold values from -3 to 3
- out_bias: bfloat16 [2, 768], P(None, ('dp', 'fsdp')), may hold values from -3 to 3
- up_bias: bfloat16 [3072], P(('dp', 'fsdp')), may hold values from -3 to 3
- norm_gain: bfloat16 [2, 768], P(None, ('dp', 'fsdp')), may hold values from 0.099609375 to 1.8984375
- norm_shift: bfloat16 [2, 768], P(None, ('dp', 'fsdp')), may hold values from -3 to 3
- cotangent: bfloat16 [65536, 768], P(('dp', 'fsdp')), may hold values from -6 to 6
Outputs:
- output: bfloat16 [65536, 768], P(('dp', 'fsdp'))
- grad_tokens: float32 [65536, 768], P(('dp', 'fsdp'))
- grad_qkv_weight: float32 [768, 576], P(('dp', 'fsdp'))
- grad_out_weight: float32 [768, 768], P(('dp', 'fsdp'))
- grad_up_weight: float32 [768, 768], P(('dp', 'fsdp'))
- grad_down_weight: float32 [3072, 192], P(('dp', 'fsdp'))
- grad_qv_bias: float32 [2, 768], P(None, ('dp', 'fsdp'))
- grad_out_bias: float32 [2, 768], P(None, ('dp', 'fsdp'))
- grad_up_bias: float32 [3072], P(('dp', 'fsdp'))
- grad_norm_gain: float32 [2, 768], P(None, ('dp', 'fsdp'))
- grad_norm_shift: float32 [2, 768], P(None, ('dp', 'fsdp'))
The draws below stay inside these ranges and needn't reach their ends.
Inputs may be any that keep to these rules, and one draw needn't show every extreme that they name: `segment_ids`: each row holds one device's tokens; ids never fall along a row, each of the ids 0, 1, 2 covers 1 to 384 tokens of every row, and one sequence of every row has exactly that many.
All inputs are finite; a program needn't handle non-finite values.
Results may differ from the reference program's by a relative error of at most 0.012.
The reference program's roundings to bfloat16 on the way count: a program that leaves them out, or rounds other values in their place, can miss the bound.
Values may be sent and summed in bfloat16 or wider, within the bound.
No kernel may reach another device: no remote copies, remote signals or barrier semaphores. Data moves between devices by JAX's collectives and lax.ppermute only.
A program may use at most 128 MiB of HBM per device.

```python
import math
from functools import partial
import jax
import jax.numpy as jnp
import numpy as np
from jax import lax

D = 768
HEADS = 12
F = 3072
G = 4
TOK_DEV = 512
HEAD = 64
DG = 192
FG = 768
TOKENS = 65536
N_DP = 4
N_FSDP = 32


def with_spikes(drawn, rng, source, target, blocks, factor):
    owner, partner = [(jnp.arange(drawn.shape[dim]) // (drawn.shape[dim] // blocks)).reshape([-1 if axis == dim else 1 for axis in range(drawn.ndim)]) for dim in (source, target)]
    chosen = jax.random.permutation(rng, blocks)[partner]
    strong = (owner == chosen) | (owner == (partner + blocks // 2) % blocks)
    return jnp.where(strong, factor * drawn, drawn)


def shard_levels(rng, shape, cuts, least, largest):
    loudness, own = 1.0, jax.random.fold_in(rng, 6)
    for position, blocks in cuts:
        draws = jnp.exp(jax.random.uniform(jax.random.fold_in(own, position), (blocks,), jnp.float32, least / len(cuts), largest / len(cuts)))
        loudness = loudness * jnp.repeat(draws, shape[position] // blocks).reshape([-1 if axis == position else 1 for axis in range(len(shape))])
    return loudness


def length_profile(amount, total, limit, lean):
    loads = [(1 << 20) // math.isqrt(rank ** lean) + 1 for rank in range(2, amount + 1)]
    surplus, counts = total - limit - (amount - 1), [1] * (amount - 1)
    while surplus > 0:
        free = [i for i in range(amount - 1) if counts[i] < limit]
        pool, budget = sum([loads[i] for i in free]), surplus
        for i in free:
            extra = min(limit - counts[i], max(1, budget * loads[i] // pool), surplus)
            counts[i] = counts[i] + extra
            surplus = surplus - extra
    return np.array([limit] + counts)


def ragged_sizes(stream_key, count, total, most, lean):
    if count == 2:
        one = jax.random.randint(stream_key, (), max(1, total - most), min(most, total - 1) + 1)
        return jnp.stack([one, total - one])
    sizes = jnp.asarray(length_profile(count, total, most, lean), jnp.int32)
    twos = (count - 1) // 2
    giver, sink = sizes[1:1 + 2 * twos:2], sizes[2:2 + 2 * twos:2]
    slack = jnp.minimum(giver - 1, most - sink)
    moved = jax.random.randint(jax.random.fold_in(stream_key, 1), (twos,), 0, 1 << 20) % (slack + 1)
    sizes = sizes.at[1:1 + 2 * twos:2].set(giver - moved).at[2:2 + 2 * twos:2].set(sink + moved)
    return sizes[jax.random.permutation(jax.random.fold_in(stream_key, 2), count)]


def noise(rng, dims, scale, reach, pieces=(), dtype=jnp.bfloat16):
    drawn = jax.random.normal(rng, dims, jnp.float32) * scale
    if len(pieces) > 0:
        drawn = shard_levels(rng, dims, pieces, -0.22, 0.18) * drawn
    return jnp.clip(drawn, min=-reach, max=reach).astype(dtype)


def noise_with(own_key, extent, deviation, most, split, heavy, held_as=jnp.bfloat16):
    entries = deviation * jax.random.normal(own_key, extent, jnp.float32)
    if split:
        entries = entries * shard_levels(own_key, extent, split, -0.22, 0.18)
    return jnp.clip(with_spikes(entries, jax.random.fold_in(own_key, 3), *heavy), -most, most).astype(held_as)


def setup_inputs(seed: int = 0) -> dict:
    seeds = jax.random.split(jax.random.key(seed), 13)
    tokens = noise_with(seeds[0], (TOKENS, D), 1.0, 24.0, ((0, 128),), (0, 1, 128, 5.5))
    segment_ids = jax.vmap(lambda own: jnp.searchsorted(jnp.cumsum(ragged_sizes(own, 3, TOK_DEV, TOK_DEV - TOK_DEV // 4, 2)), jnp.arange(TOK_DEV), side="right"))(jax.random.split(seeds[1], (N_DP * N_FSDP))).reshape((N_DP * N_FSDP, TOK_DEV)).astype(jnp.int32)
    qkv_weight = noise(seeds[2], (D, 3 * DG), DG ** -0.5, 0.4375, ((0, 128),))
    out_weight = noise(seeds[3], (D, D), (D // 64) ** -0.5, 1.75, ((0, 128),))
    up_weight = noise(seeds[4], (D, FG), DG ** -0.5, 0.4375, ((0, 128),))
    down_weight = noise(seeds[5], (F, DG), FG ** -0.5, 0.21875, ((0, 128),))
    qv_bias = noise(seeds[6], (2, D), 0.5, 3.0, ((1, 128),))
    out_bias = noise(seeds[7], (2, D), 0.5, 3.0, ((1, 128),))
    up_bias = noise(seeds[8], (F,), 0.5, 3.0, ((0, 128),))
    norm_gain = jnp.clip(1.0 + 0.18 * jax.random.normal(seeds[9], (2, D), jnp.float32), 0.099609375, 1.8984375).astype(jnp.bfloat16)
    norm_shift = noise(seeds[10], (2, D), 0.5, 3.0, ((1, 128),))
    cotangent = noise(seeds[11], (TOKENS, D), 1.0, 6.0, ((0, 128),))
    return {"tokens": tokens, "segment_ids": segment_ids, "qkv_weight": qkv_weight, "out_weight": out_weight, "up_weight": up_weight, "down_weight": down_weight, "qv_bias": qv_bias, "out_bias": out_bias, "up_bias": up_bias, "norm_gain": norm_gain, "norm_shift": norm_shift, "cotangent": cotangent}


@jax.custom_vjp
def low(v):
    return lax.optimization_barrier(v.astype(jnp.bfloat16)).astype(jnp.float32)

@jax.custom_vjp
def low_back(v):
    return v

def low_keep(v):
    return (low(v), None)

def low_pass(kept, grad):
    return (grad,)

def back_keep(v):
    return (v, None)

def back_low(kept, grad):
    return (low(grad),)
low.defvjp(low_keep, low_pass)
low_back.defvjp(back_keep, back_low)
precise = lax.Precision.HIGHEST

def grouped(inputs, weight):
    row_count = inputs.shape[0]
    out_width = weight.shape[1]
    grouped_in = inputs.reshape(row_count, G, -1)
    block_weights = weight.reshape(G, -1, out_width)
    product = jnp.einsum('tgi,gic->tgc', grouped_in, block_weights, precision=precise)
    return product.reshape(row_count, G * out_width)

def normalize(rows_in, gain_row, shift_row):
    centered = rows_in - lax.optimization_barrier(jnp.mean(rows_in, axis=-1, keepdims=True))
    spread = lax.optimization_barrier(jnp.mean(centered * centered, axis=-1, keepdims=True))
    return centered * lax.rsqrt(spread + 1e-05) * gain_row + shift_row

def gelu_exact(values):
    return jax.nn.gelu(values, approximate=False)

def attend(block):
    queries, keys_low, values, segment = block
    parts = segment.shape[0]
    row_count = segment.shape[1]
    query_heads = queries.reshape(parts, row_count, HEADS, HEAD)
    key_heads = keys_low.reshape(parts, row_count, HEADS, HEAD)
    value_heads = values.reshape(parts, row_count, HEADS, HEAD)
    scores = jnp.einsum('pqhd,pkhd->phqk', query_heads, key_heads, precision=precise) * HEAD ** (-0.5)
    scores = low_back(scores)
    same_seq = segment[:, None, :, None] == segment[:, None, None, :]
    scores = jnp.where(same_seq, scores, -1000000000.0)
    row_max = lax.optimization_barrier(jnp.max(scores, axis=-1, keepdims=True))
    exponent = jnp.exp(scores - row_max)
    attn_probs = low(exponent / lax.optimization_barrier(jnp.sum(exponent, axis=-1, keepdims=True)))
    context = jnp.einsum('phqk,pkhd->pqhd', attn_probs, value_heads, precision=precise)
    return context.reshape(parts, row_count, D)

def forward(segment_ids, inputs, qkv_weight, out_weight, up_weight, down_weight, qv_bias, out_bias, up_bias, norm_gain, norm_shift):
    row_count = inputs.shape[0]
    packed = grouped(inputs, qkv_weight).reshape(row_count, G, 3, DG)
    queries = low(low_back(packed[:, :, 0].reshape(row_count, D) + qv_bias[0]))
    keys_low = low(low_back(packed[:, :, 1].reshape(row_count, D)))
    values = low(low_back(packed[:, :, 2].reshape(row_count, D) + qv_bias[1]))
    devices = N_DP * N_FSDP
    per_block = math.gcd(devices, max(1, 4096 // TOK_DEV))
    block_shape = (devices // per_block, per_block, TOK_DEV)
    context = lax.map(jax.checkpoint(attend), (queries.reshape(block_shape + (D,)), keys_low.reshape(block_shape + (D,)), values.reshape(block_shape + (D,)), segment_ids.reshape(block_shape)))
    context = low(low_back(context.reshape(row_count, D)))
    attended = low_back(jnp.dot(context, out_weight, precision=precise, preferred_element_type=jnp.float32) + out_bias[0])
    first_norm = normalize(inputs + attended, norm_gain[0], norm_shift[0])
    upper_in = low_back(grouped(low(first_norm), up_weight) + up_bias)
    active = low(gelu_exact(upper_in))
    branch = low_back(grouped(active, down_weight) + out_bias[1])
    return normalize(first_norm + branch, norm_gain[1], norm_shift[1])

def reference(tokens, segment_ids, qkv_weight, out_weight, up_weight, down_weight, qv_bias, out_bias, up_bias, norm_gain, norm_shift, cotangent):
    result, pullback = jax.vjp(partial(forward, segment_ids), tokens.astype(jnp.float32), qkv_weight.astype(jnp.float32), out_weight.astype(jnp.float32), up_weight.astype(jnp.float32), down_weight.astype(jnp.float32), qv_bias.astype(jnp.float32), out_bias.astype(jnp.float32), up_bias.astype(jnp.float32), norm_gain.astype(jnp.float32), norm_shift.astype(jnp.float32))
    grads = pullback(cotangent.astype(jnp.float32))
    return (result.astype(jnp.bfloat16), grads[0], grads[1], grads[2], grads[3], grads[4], grads[5], grads[6], grads[7], grads[8], grads[9])
```

```python
import jax
import jax.numpy as jnp
import numpy as np
from jax import lax
from jax.experimental import pallas as pl
from jax.experimental.pallas import tpu as pltpu
from jax.sharding import PartitionSpec as P

AXES = ("dp", "fsdp")
D = 768
F = 3072
G = 4
DG = 192
QKV = 3 * DG
HEADS = 12
HEAD = 64
TOK = 512
LONG = 384
CHIPS = 64
ROWS = 24
EPS = 1e-05
BAND = 64
BANDS = D // BAND
BF = jnp.bfloat16
F32 = jnp.float32
MIB = 1 << 20

SIDE = 18
CUT = 576
UP_AT = 64
OUT_AT = 320


def orders():
    weights, downs, hidden = (np.zeros((2, 192, 192), np.float32) for _ in range(3))
    for core in range(2):
        for device in range(8):
            chip, half = device // 2, device % 2
            base = (half != core) * 96 + chip * ROWS
            for row in range(6):
                for kind in range(4):
                    weights[core, kind * 48 + device * 6 + row, base + kind * 6 + row] = 1
            for row in range(ROWS):
                downs[core, device * ROWS + row, base + row] = 1
                hidden[core, device * ROWS + row, base + SIDE + row // 4] = 1
    return np.concatenate([weights, downs, hidden], axis=1)


def dot(left, right, over_left, over_right):
    return lax.dot_general(
        left, right, (((over_left,), (over_right,)), ((), ())), preferred_element_type=F32
    )


def iota(shape, axis):
    return lax.broadcasted_iota(jnp.int32, shape, axis)


def pack_kernel(qkv, out, up, down, qv, outb, upb, gain, shift, packed, tile, square):
    tile[...] = jnp.zeros_like(tile)
    tile[0:6, 0:CUT] = qkv[...].astype(F32)
    tile[6:12, 0:CUT] = out[:, 0:CUT].astype(F32)
    tile[12:18, 0:CUT] = up[:, 0:CUT].astype(F32)
    square[...] = jnp.zeros_like(square)
    for place, rows in enumerate((qv, outb, gain, shift)):
        square[2 * place : 2 * place + 2, 0:6] = rows[...].astype(F32)
    columns = square[...].T
    spread = jnp.where(iota((8, ROWS), 1) // 4 == iota((8, ROWS), 0), upb[...].astype(F32), 0.0)
    lanes = (iota((ROWS, 128), 1) - 8 == iota((ROWS, 128), 0) % 4).astype(F32)
    hidden = jnp.dot(spread, lanes, preferred_element_type=F32)
    tile[SIDE:ROWS, 0:128] = (columns[0:8] + hidden)[0:6]
    tile[SIDE:ROWS, UP_AT : UP_AT + DG] = up[:, CUT:D].astype(F32)
    tile[SIDE:ROWS, OUT_AT : OUT_AT + DG] = out[:, CUT:D].astype(F32)
    tile[:, CUT:D] = down[...].astype(F32)
    whole = tile[...].astype(BF)
    twice = jnp.concatenate([whole, whole], axis=0)
    for pair in range(CHIPS // 2):
        packed[2 * ROWS * pair : 2 * ROWS * (pair + 1), :] = twice


def each(count, step):
    def body(i, nothing):
        step(i)
        return nothing

    lax.fori_loop(0, count, body, 0)


def part(i, size):
    return pl.ds(pl.multiple_of(i * size, size), size)


def halves(chunk):
    return jnp.sum(chunk.reshape(BAND // 8, 8, TOK), axis=0)


def means(count, bands):
    def body(i, sums):
        return tuple(kept + halves(chunk) for kept, chunk in zip(sums, bands(part(i, BAND)), strict=True))

    sums = lax.fori_loop(0, BANDS, body, (jnp.zeros((8, TOK), F32),) * count)
    return [jnp.sum(total, axis=0, keepdims=True) * (1.0 / D) for total in sums]


def lane_sum(chunk):
    return jnp.sum(chunk, axis=1, keepdims=True)


def main_kernel(
    tokens, segments, cotangent, mine, other, order,
    output, grad_tokens, keep, send,
    w_qkv, w_out, w_up, w_down, side, up_bias,
    turn, x_t, c_t, q_t, k_t, v_t, ctx_t, low_t, probs, probs_small,
    first_low, hat, active, slope, second, branch_pad, packed_t,
    g_qkv, g_out, g_up, g_down, g_side,
):
    core = lax.rem(lax.axis_index("fsdp"), 2)
    lane48 = iota((48, 128), 1)

    def place_block(i):
        rows = part(i, 96)
        both = jnp.concatenate([mine[rows, :], other[rows, :]], axis=0)
        placed = jnp.dot(order[core, 0:192, :], both[:, 0:640], preferred_element_type=F32).astype(BF)
        down_rows = jnp.dot(order[core, 192:384, :], both[:, 512:768], preferred_element_type=F32)
        units = part(i, 192)
        w_down[units, :] = down_rows.astype(BF)
        hidden = jnp.dot(order[core, 384:576, :], both[:, 0:128], preferred_element_type=F32)
        pick = iota((192, 128), 1) - 8 == iota((192, 128), 0) % 4
        up_bias[units, :] = lane_sum(jnp.where(pick, hidden, 0.0))
        here = part(i, 48)
        last = placed[144:192]
        w_qkv[here, :] = placed[0:48, 0:CUT]
        w_out[here, 0:512] = placed[48:96, 0:512]
        w_out[here, 512:640] = jnp.where(lane48 < 64, placed[48:96, 512:640], last[:, 256:384])
        w_out[here, 640:768] = last[:, 384:512]
        w_up[here, 0:512] = placed[96:144, 0:512]
        w_up[here, 512:640] = jnp.where(lane48 < 64, placed[96:144, 512:640], last[:, 0:128])
        w_up[here, 640:768] = last[:, 128:256]
        side[here, :] = last[:, 0:128].astype(F32)

    each(16, place_block)

    ids = segments[...]
    count0 = jnp.sum((ids == 0).astype(jnp.int32))
    count1 = jnp.sum((ids == 1).astype(jnp.int32))
    count2 = TOK - count0 - count1
    start = jnp.where(count0 == LONG, 0, jnp.where(count1 == LONG, count0, count0 + count1))
    border = jnp.where(count0 == LONG, count1, jnp.where(count1 == LONG, count2, count0))

    def turn_rows(i):
        place = iota((64, TOK), 1) + start
        place = jnp.where(place >= TOK, place - TOK, place)
        turn[part(i, 64), :] = jnp.where(iota((64, TOK), 0) + i * 64 == place, 1.0, 0.0).astype(BF)

    each(8, turn_rows)

    def turn_features(i):
        x_t[part(i, 256), :] = dot(tokens[:, part(i, 256)], turn[...], 0, 0).astype(BF)
        c_t[part(i, 256), :] = dot(cotangent[:, part(i, 256)], turn[...], 0, 0).astype(BF)

    each(3, turn_features)

    together = (iota((128, 128), 0) < border) == (iota((128, 128), 1) < border)
    spans = ((slice(0, LONG), probs), (slice(LONG, TOK), probs_small))

    def attend(g):
        rows = part(g, DG)
        packed = dot(w_qkv[rows, :], x_t[rows, :], 0, 0)
        q_t[rows, :] = ((packed[0:DG] + side[rows, 0:1]).astype(BF).astype(F32) * 0.125).astype(BF)
        k_t[rows, :] = packed[DG : 2 * DG].astype(BF)
        v_t[rows, :] = (packed[2 * DG :] + side[rows, 1:2]).astype(BF)
        for third in range(3):
            head = g * 3 + third
            rows = part(head, HEAD)
            for cols, kept in spans:
                scores = dot(k_t[rows, cols], q_t[rows, cols], 0, 0)
                if kept is probs_small:
                    scores = jnp.where(together, scores, -1000000000.0)
                power = jnp.exp(scores - jnp.max(scores, axis=0, keepdims=True))
                share = power * (1.0 / jnp.sum(power, axis=0, keepdims=True))
                kept[head] = share
                ctx_t[rows, cols] = dot(v_t[rows, cols], share.astype(BF), 1, 0).astype(BF)

    each(G, attend)

    def project(i):
        rows = part(i, 128)
        attended = dot(w_out[:, rows], ctx_t[...], 0, 0) + side[rows, 2:3]
        second[rows, :] = x_t[rows, :].astype(F32) + attended

    each(6, project)
    (mean_one,) = means(1, lambda rows: (second[rows, :],))
    (spread_one,) = means(1, lambda rows: ((second[rows, :] - mean_one) ** 2,))
    rs_one = lax.rsqrt(spread_one + EPS)

    def norm_one(i):
        rows = part(i, BAND)
        hats = (second[rows, :] - mean_one) * rs_one
        hat[rows, :] = hats
        result = hats * side[rows, 4:5] + side[rows, 6:7]
        second[rows, :] = result
        first_low[rows, :] = result.astype(BF)

    each(BANDS, norm_one)

    def feed(g):
        rows = part(g, DG)
        for third in range(3):
            units = part(g * 3 + third, 256)
            upper = dot(w_up[rows, 256 * third : 256 * third + 256], first_low[rows, :], 0, 0) + up_bias[units, :]
            below = 0.5 + 0.5 * lax.erf(upper * 0.7071067811865476)
            density = jnp.exp(-0.5 * upper * upper) * 0.3989422804014327
            active[units, :] = (upper * below).astype(BF)
            slope[units, :] = below + upper * density
        units = part(g, D)
        branch = dot(w_down[units, :], active[units, :], 0, 0)[64:256]
        second[rows, :] += branch + side[rows, 3:4]

    each(G, feed)

    (mean_two,) = means(1, lambda rows: (second[rows, :],))
    (spread_two,) = means(1, lambda rows: ((second[rows, :] - mean_two) ** 2,))
    rs_two = lax.rsqrt(spread_two + EPS)

    def norm_two(rows):
        hats = (second[rows, :] - mean_two) * rs_two
        second[rows, :] = hats
        low_t[rows, :] = (hats * side[rows, 5:6] + side[rows, 7:8]).astype(BF)
        slopes = c_t[rows, :].astype(F32)
        g_side[rows, 5:6] = lane_sum(slopes * hats)
        g_side[rows, 7:8] = lane_sum(slopes)
        slopes = slopes * side[rows, 5:6]
        return slopes, slopes * hats

    lean, tilt = means(2, norm_two)

    def write_output(i):
        output[:, part(i, 256)] = dot(turn[...], low_t[part(i, 256), :], 1, 1).astype(BF)

    each(3, write_output)

    def norm_two_back(i):
        rows = part(i, BAND)
        slopes = c_t[rows, :].astype(F32) * side[rows, 5:6]
        back = rs_two * (slopes - lean - second[rows, :] * tilt)
        second[rows, :] = back
        low = back.astype(BF)
        g_side[rows, 3:4] = lane_sum(low.astype(F32))
        low_t[rows, :] = low

    each(BANDS, norm_two_back)
    for g in range(G):
        branch_pad[g, 0:64, :] = jnp.zeros((64, TOK), BF)
        branch_pad[g, 64:256, :] = low_t[DG * g : DG * (g + 1), :]

    def feed_back(g):
        rows = part(g, DG)
        for third in range(3):
            units = part(g * 3 + third, 256)
            span = slice(256 * third, 256 * third + 256)
            d_active = dot(w_down[units, :], branch_pad[g], 1, 0)
            d_upper = (d_active * slope[units, :]).astype(BF)
            up_bias[units, :] = lane_sum(d_upper.astype(F32))
            g_down[units, :] = dot(active[units, :], branch_pad[g], 1, 1).astype(BF)
            g_up[rows, span] = dot(first_low[rows, :], d_upper, 1, 1).astype(BF)
            active[units, :] = d_upper
        second[rows, :] += dot(w_up[rows, :], active[part(g, D), :], 1, 0)

    each(G, feed_back)

    def norm_one_sums(rows):
        slopes, hats = second[rows, :], hat[rows, :]
        g_side[rows, 4:5] = lane_sum(slopes * hats)
        g_side[rows, 6:7] = lane_sum(slopes)
        slopes = slopes * side[rows, 4:5]
        return slopes, slopes * hats

    lean_one, tilt_one = means(2, norm_one_sums)

    def norm_one_back(i):
        rows = part(i, BAND)
        back = rs_one * (second[rows, :] * side[rows, 4:5] - lean_one - hat[rows, :] * tilt_one)
        second[rows, :] = back
        low = back.astype(BF)
        g_side[rows, 2:3] = lane_sum(low.astype(F32))
        low_t[rows, :] = low

    each(BANDS, norm_one_back)

    def project_back(i):
        rows = part(i, 128)
        g_out[rows, :] = dot(ctx_t[rows, :], low_t[...], 1, 1).astype(BF)
        c_t[rows, :] = dot(w_out[rows, :], low_t[...], 1, 0).astype(BF)

    each(6, project_back)

    def attend_back(g):
        for third in range(3):
            head = g * 3 + third
            rows = part(head, HEAD)
            at = HEAD * third
            for cols, kept in spans:
                d_out = c_t[rows, cols]
                share = kept[head]
                d_share = dot(v_t[rows, cols], d_out, 0, 0)
                packed_t[2 * DG + at : 2 * DG + at + HEAD, cols] = dot(d_out, share.astype(BF), 1, 1).astype(BF)
                d_scores = share * (d_share - jnp.sum(d_share * share, axis=0, keepdims=True))
                d_scores = d_scores.astype(BF)
                packed_t[at : at + HEAD, cols] = (0.125 * dot(k_t[rows, cols], d_scores, 1, 0)).astype(BF)
                packed_t[DG + at : DG + at + HEAD, cols] = dot(q_t[rows, cols], d_scores, 1, 1).astype(BF)
        rows = part(g, DG)
        g_qkv[rows, :] = dot(x_t[rows, :], packed_t[...], 1, 1).astype(BF)
        total = second[rows, :] + dot(w_qkv[rows, :], packed_t[...], 1, 0)
        g_side[rows, 0:1] = lane_sum(packed_t[0:DG, :].astype(F32))
        g_side[rows, 1:2] = lane_sum(packed_t[2 * DG :, :].astype(F32))
        high = total.astype(BF)
        low_t[rows, :] = high
        first_low[rows, :] = (total - high.astype(F32)).astype(BF)

    each(G, attend_back)

    def write_grad(i):
        rows = part(i, 256)
        grad_tokens[:, rows] = dot(turn[...], low_t[rows, :], 1, 1) + dot(turn[...], first_low[rows, :], 1, 1)

    each(3, write_grad)

    def tile_block(i):
        here = part(i, 48)
        units = part(i, 192)
        pick = iota((192, 128), 1) - 8 == iota((192, 128), 0) % 4
        hidden = jnp.where(pick, up_bias[units, :], 0.0).astype(BF)
        bias = jnp.where(lane48 < 8, g_side[here, :], 0.0).astype(BF)
        zero = jnp.zeros((48, 128), BF)
        out_cut, up_cut = g_out[here, 512:640], g_up[here, 512:640]
        last = jnp.concatenate(
            [
                jnp.where(lane48 < 64, bias, up_cut),
                g_up[here, 640:768],
                jnp.where(lane48 < 64, zero, out_cut),
                g_out[here, 640:768],
                zero,
            ],
            axis=1,
        )
        stacked = jnp.concatenate(
            [
                jnp.concatenate([g_qkv[here, :], zero[:, 0:64]], axis=1),
                jnp.concatenate([g_out[here, 0:512], jnp.where(lane48 < 64, out_cut, zero)], axis=1),
                jnp.concatenate([g_up[here, 0:512], jnp.where(lane48 < 64, up_cut, zero)], axis=1),
                last,
            ],
            axis=0,
        )
        placed = dot(order[core, 0:192, :], stacked, 0, 0)
        downs = dot(order[core, 192:384, :], g_down[units, :], 0, 0)
        biases = dot(order[core, 384:576, :], hidden, 0, 0)
        rows = part(i, 96)
        for target, begin in ((keep, 0), (send, 96)):
            span = slice(begin, begin + 96)
            target[rows, 0:128] = (placed[span, 0:128] + biases[span]).astype(BF)
            target[rows, 128:512] = placed[span, 128:512].astype(BF)
            target[rows, 512:640] = (placed[span, 512:640] + downs[span, 0:128]).astype(BF)
            target[rows, 640:768] = downs[span, 128:256].astype(BF)

    each(16, tile_block)


def add_kernel(left, right, total):
    total[...] = (left[...].astype(F32) + right[...].astype(F32)).astype(BF)


def sum_kernel(parts, qkv, out, up, down, qv, outb, upb, gain, shift, square):
    total = jnp.zeros((2 * ROWS, D), F32)
    for pair in range(CHIPS // 2):
        total += parts[2 * ROWS * pair : 2 * ROWS * (pair + 1), :].astype(F32)
    total = total[0:ROWS] + total[ROWS:]
    qkv[...] = total[0:6, 0:CUT]
    out[:, 0:CUT] = total[6:12, 0:CUT]
    out[:, CUT:D] = total[SIDE:ROWS, OUT_AT : OUT_AT + DG]
    up[:, 0:CUT] = total[12:18, 0:CUT]
    up[:, CUT:D] = total[SIDE:ROWS, UP_AT : UP_AT + DG]
    down[...] = total[:, CUT:D]
    square[...] = jnp.zeros_like(square)
    square[0:6, :] = total[SIDE:ROWS, 0:128]
    columns = square[...].T
    for place, rows in enumerate((qv, outb, gain, shift)):
        rows[...] = columns[2 * place : 2 * place + 2, 0:6]
    lanes = (iota((128, ROWS), 0) - 8 == iota((128, ROWS), 1) % 4).astype(F32)
    spread = jnp.dot(square[0:8, :], lanes, preferred_element_type=F32, precision=lax.Precision.HIGHEST)
    spread = jnp.where(iota((8, ROWS), 1) // 4 == iota((8, ROWS), 0), spread, 0.0)
    upb[...] = jnp.sum(spread, axis=0, keepdims=True)


def call(kernel, shapes, scratch, limit, name):
    return pl.pallas_call(
        kernel,
        out_shape=[jax.ShapeDtypeStruct(*shape) for shape in shapes],
        scratch_shapes=[pltpu.VMEM(*shape) for shape in scratch],
        compiler_params=pltpu.CompilerParams(vmem_limit_bytes=limit * MIB),
        name=name,
    )


def same_core(n_dp, n_fsdp):
    return [[y * n_fsdp + i for y in range(n_dp) for i in range(core, n_fsdp, 2)] for core in range(2)]


def swap(array):
    return lax.ppermute(array, "fsdp", [(i, i ^ 1) for i in range(32)])


def local(
    tokens, segment_ids, qkv_weight, out_weight, up_weight, down_weight,
    qv_bias, out_bias, up_bias, norm_gain, norm_shift, cotangent,
):
    groups = same_core(4, 32)
    wide = (CHIPS * ROWS, D)
    packed = call(
        pack_kernel, [(wide, BF)], [((ROWS, D), F32), ((128, 128), F32)], 32, "pack"
    )(qkv_weight, out_weight, up_weight, down_weight, qv_bias, out_bias, up_bias.reshape(1, ROWS),
      norm_gain, norm_shift)[0]
    mine = lax.all_to_all(packed, AXES, 0, 0, axis_index_groups=groups, tiled=True)
    other = swap(mine)
    order = jnp.asarray(orders(), BF)
    square = (D, TOK)
    output, grad_tokens, keep, send = call(
        main_kernel,
        [((TOK, D), BF), ((TOK, D), F32), (wide, BF), (wide, BF)],
        [
            ((D, QKV), BF), ((D, D), BF), ((D, D), BF), ((F, 256), BF), ((D, 128), F32), ((F, 1), F32),
            ((TOK, TOK), BF), (square, BF), (square, BF), (square, BF), (square, BF), (square, BF), (square, BF),
            (square, BF), ((HEADS, LONG, LONG), F32), ((HEADS, 128, 128), F32),
            (square, BF), (square, F32), ((F, TOK), BF), ((F, TOK), F32), (square, F32),
            ((G, 256, TOK), BF), ((QKV, TOK), BF),
            ((D, QKV), BF), ((D, D), BF), ((D, D), BF), ((F, 256), BF), ((D, 128), F32),
        ],
        64,
        "layer",
    )(tokens, segment_ids, cotangent, mine, other, order)
    chip = call(add_kernel, [(wide, BF)], [], 32, "chip_sum")(keep, swap(send))[0]
    parts = lax.all_to_all(chip, AXES, 0, 0, axis_index_groups=groups, tiled=True)
    qkv, out, up, down, qv, outb, upb, gain, shift = call(
        sum_kernel,
        [((6, QKV), F32), ((6, D), F32), ((6, D), F32), ((ROWS, DG), F32), ((2, 6), F32), ((2, 6), F32),
         ((1, ROWS), F32), ((2, 6), F32), ((2, 6), F32)],
        [((128, 128), F32)],
        32,
        "slice_sum",
    )(parts)
    return output, grad_tokens, qkv, out, up, down, qv, outb, upb.reshape(ROWS), gain, shift


def solution(mesh):
    rows, columns, flat = P(AXES, None), P(None, AXES), P(AXES)
    in_specs = (rows, rows, rows, rows, rows, rows, columns, columns, flat, columns, columns, rows)
    out_specs = (rows, rows, rows, rows, rows, rows, columns, columns, flat, columns, columns)
    return jax.shard_map(local, mesh=mesh, in_specs=in_specs, out_specs=out_specs, check_vma=False)
```

```python
import jax
import jax.numpy as jnp
from jax import lax
from jax.experimental import pallas as pl
from jax.experimental.pallas import tpu as pltpu
from jax.sharding import PartitionSpec as P

AXES = ("dp", "fsdp")
D = 768
F = 3072
G = 4
DG = 192
QKV = 3 * DG
HEADS = 12
HEAD = 64
TOK = 512
LONG = 384
CHIPS = 64
ROWS = 24
EPS = 1e-05
BAND = 64
BANDS = D // BAND
BF = jnp.bfloat16
F32 = jnp.float32
MIB = 1 << 20

SIDE = 18
WIDE = 2 * DG
TILES = CHIPS * ROWS


def dot(left, right, over_left, over_right):
    return lax.dot_general(
        left, right, (((over_left,), (over_right,)), ((), ())), preferred_element_type=F32
    )


def iota(shape, axis):
    return lax.broadcasted_iota(jnp.int32, shape, axis)


def each(count, step, unroll=1):
    def body(i, nothing):
        step(i)
        return nothing

    lax.fori_loop(0, count, body, 0, unroll=unroll)


def part(i, size):
    return pl.ds(pl.multiple_of(i * size, size), size)


def halves(chunk):
    return jnp.sum(chunk.reshape(BAND // 8, 8, TOK), axis=0)


def means(count, bands):
    def body(i, sums):
        return tuple(kept + halves(chunk) for kept, chunk in zip(sums, bands(part(i, BAND)), strict=True))

    sums = lax.fori_loop(0, BANDS, body, (jnp.zeros((8, TOK), F32),) * count, unroll=2)
    return [jnp.sum(total, axis=0, keepdims=True) * (1.0 / D) for total in sums]


def lane_sum(chunk):
    return jnp.sum(chunk, axis=1, keepdims=True)


def pick_hidden():
    return iota((192, 128), 1) - 8 == (iota((192, 128), 0) & 3)


def arrival(core, by_device, axis):
    sorted_row = iota((192, 1) if axis == 0 else (1, 192), axis)
    if by_device:
        device = (sorted_row * 2731) >> 16
        row = sorted_row - device * ROWS
    else:
        block = (sorted_row * 1366) >> 16
        sixth = (sorted_row * 10923) >> 16
        device = sixth - block * 8
        row = block * 6 + sorted_row - sixth * 6
    return jnp.where((device & 1) == core, 0, 96) + (device >> 1) * ROWS + row


def sorter(core, by_device=False):
    return (arrival(core, by_device, 0) == iota((192, 192), 1)).astype(F32).astype(BF)


def unsorter(core, by_device=False):
    return (arrival(core, by_device, 1) == iota((192, 192), 0)).astype(F32).astype(BF)


def grower():
    return ((iota((192, 48), 0) >> 2) == iota((192, 48), 1)).astype(F32).astype(BF)


def low_lanes():
    return iota((48, 128), 1) < 64


def repeat(tile, target):
    whole = tile[...].astype(BF)
    twice = jnp.concatenate([whole, whole], axis=0)

    def copy(pair):
        target[part(pair, 2 * ROWS), :] = twice

    each(CHIPS // 2, copy, unroll=4)


def pack_attention_kernel(*refs):
    far, packed, near, (tile, square, arrive) = refs[:7], refs[7], refs[8:15], refs[15:]
    arriving = moves(zip(far, near, strict=True), arrive)
    start(*arriving)
    wait(*arriving)
    qkv, out, qv, outb, upb, gain, shift = near
    square[...] = jnp.zeros_like(square)
    for place, rows in enumerate((qv, outb, gain, shift)):
        square[2 * place : 2 * place + 2, 0:6] = rows[...].astype(F32)
    columns = square[...].T
    grown = jnp.where(iota((8, ROWS), 1) // 4 == iota((8, ROWS), 0), upb[...].astype(F32), 0.0)
    lanes = (iota((ROWS, 128), 1) - 8 == iota((ROWS, 128), 0) % 4).astype(F32)
    hidden = jnp.dot(grown, lanes, preferred_element_type=F32)
    tile[...] = jnp.zeros_like(tile)
    for block in range(4):
        rows, lanes = slice(6 * block, 6 * block + 6), slice(DG * block, DG * block + DG)
        here, there = (slice(0, DG), slice(DG, WIDE))[:: 1 - 2 * (block % 2)]
        tile[rows, here] = out[:, lanes].astype(F32)
        if block < 3:
            tile[rows, there] = qkv[:, lanes].astype(F32)
    tile[SIDE:ROWS, 0:128] = (columns[0:8] + hidden)[0:6]
    repeat(tile, packed)


def pack_feed_kernel(up_far, down_far, packed, up, down, tile, arrive):
    arriving = moves([(up_far, up), (down_far, down)], arrive)
    start(*arriving)
    wait(*arriving)
    for block in range(4):
        rows, lanes = slice(6 * block, 6 * block + 6), slice(DG * block, DG * block + DG)
        tile[rows, 0:DG] = up[:, lanes].astype(F32)
    tile[:, DG:WIDE] = down[...].astype(F32)
    repeat(tile, packed)


def turn_kernel(tokens, segments, cotangent, turn, x_t, c_t):
    ids = segments[...]
    count0 = jnp.sum((ids == 0).astype(jnp.int32))
    count1 = jnp.sum((ids == 1).astype(jnp.int32))
    start = jnp.where(count0 == LONG, 0, jnp.where(count1 == LONG, count0, count0 + count1))

    def turn_rows(i):
        place = iota((64, TOK), 1) + start
        place = jnp.where(place >= TOK, place - TOK, place)
        turn[part(i, 64), :] = jnp.where(iota((64, TOK), 0) + i * 64 == place, 1.0, 0.0).astype(BF)

    each(8, turn_rows)

    def turn_features(i):
        x_t[part(i, 256), :] = dot(tokens[:, part(i, 256)], turn[...], 0, 0).astype(BF)
        c_t[part(i, 256), :] = dot(cotangent[:, part(i, 256)], turn[...], 0, 0).astype(BF)

    each(3, turn_features)


def moves(pairs, sems):
    return [pltpu.make_async_copy(source, target, sems.at[i]) for i, (source, target) in enumerate(pairs)]


def start(*copies):
    for copy in copies:
        copy.start()


def wait(*copies):
    for copy in copies:
        copy.wait()


def own_core():
    return lax.rem(lax.axis_index("fsdp"), 2)


SPANS = (slice(0, LONG), slice(LONG, TOK))


def attention_kernel(
    segments, mine, other, x_far,
    w_qkv_far, w_out_far, side_far, q_far, k_far, v_far, ctx_far, probs_far, small_far, hat_far, scale,
    x_t, w_qkv, w_out, side, q_t, k_t, v_t, ctx_t, probs, probs_small, first, hat, arrive, leave,
):
    halves_of_hat = [(hat.at[part(i, D // 2), :], hat_far.at[part(i, D // 2), :]) for i in range(2)]
    (arriving,) = moves([(x_far, x_t)], arrive)
    leaving = moves(
        [(w_qkv, w_qkv_far), (w_out, w_out_far), (side, side_far), (q_t, q_far), (k_t, k_far), (v_t, v_far),
         (ctx_t, ctx_far), (probs, probs_far), (probs_small, small_far), *halves_of_hat],
        leave,
    )
    start(arriving)
    sort = sorter(own_core())

    def place_block(i):
        rows = part(i, 96)
        both = jnp.concatenate([mine[rows, :], other[rows, :]], axis=0)
        placed = jnp.dot(sort, both, preferred_element_type=F32).astype(BF)
        here = part(i, 48)
        blocks = [placed[48 * block : 48 * block + 48] for block in range(4)]
        for begin, target, left, right in (
            (0, w_out, 0, 1), (WIDE, w_out, 2, 3), (0, w_qkv, 1, 0), (WIDE, w_qkv, 3, 2),
        ):
            target[here, begin : begin + 128] = blocks[left][:, 0:128]
            target[here, begin + 128 : begin + 256] = jnp.where(
                low_lanes(), blocks[left][:, 128:256], blocks[right][:, 128:256]
            )
            target[here, begin + 256 : begin + 384] = blocks[right][:, 256:384]
        side[here, :] = blocks[3][:, 0:128].astype(F32)

    each(16, place_block, unroll=4)
    start(*leaving[:3])
    wait(arriving)

    ids = segments[...]
    count0 = jnp.sum((ids == 0).astype(jnp.int32))
    count1 = jnp.sum((ids == 1).astype(jnp.int32))
    count2 = TOK - count0 - count1
    border = jnp.where(count0 == LONG, count1, jnp.where(count1 == LONG, count2, count0))
    together = (iota((128, 128), 0) < border) == (iota((128, 128), 1) < border)

    def attend(g):
        rows = part(g, DG)
        packed = dot(w_qkv[rows, 0:WIDE], x_t[rows, :], 0, 0)
        k_t[rows, :] = packed[0:DG].astype(BF)
        q_t[rows, :] = ((packed[DG:WIDE] + side[rows, 0:1]).astype(BF).astype(F32) * 0.125).astype(BF)
        packed = dot(w_qkv[rows, 512:768], x_t[rows, :], 0, 0)
        v_t[rows, :] = (packed[64:256] + side[rows, 1:2]).astype(BF)
        for third in range(3):
            head = g * 3 + third
            rows = part(head, HEAD)
            for cols, kept in zip(SPANS, (probs, probs_small), strict=True):
                scores = dot(k_t[rows, cols], q_t[rows, cols], 0, 0)
                if kept is probs_small:
                    scores = jnp.where(together, scores, -1000000000.0)
                power = jnp.exp(scores - jnp.max(scores, axis=0, keepdims=True))
                share = (power * (1.0 / jnp.sum(power, axis=0, keepdims=True))).astype(BF)
                kept[head] = share
                ctx_t[rows, cols] = dot(v_t[rows, cols], share, 1, 0).astype(BF)

    each(G, attend)
    start(*leaving[3:9])

    def project(i):
        rows = part(i, 128)
        attended = dot(w_out[:, rows], ctx_t[...], 0, 0) + side[rows, 2:3]
        first[rows, :] = x_t[rows, :].astype(F32) + attended

    each(6, project)
    (mean,) = means(1, lambda rows: (first[rows, :],))
    (variance,) = means(1, lambda rows: ((first[rows, :] - mean) ** 2,))
    scale[...] = lax.rsqrt(variance + EPS)

    def norm(i):
        rows = part(i, BAND)
        hat[rows, :] = (first[rows, :] - mean) * scale[...]

    each(BANDS // 2, norm, unroll=3)
    start(leaving[9])
    each(BANDS // 2, lambda i: norm(i + BANDS // 2), unroll=3)
    start(leaving[10])
    wait(*leaving)


def feed_kernel(
    mine, other, side_far, hat_far, c_far,
    result_far, d_first_far, g_side_far, keep, send,
    side, hat, c_t, result, d_first, g_side,
    w_up, w_down, up_bias, first_low, active, slope, low_t, branch_pad, g_up, g_down, arrive, leave,
):
    arriving = moves([(side_far, side), (hat_far, hat), (c_far, c_t)], arrive)
    leaving = moves([(result, result_far), (d_first, d_first_far), (g_side, g_side_far)], leave)
    start(*arriving)
    core = own_core()
    sort, sort_devices, grow = sorter(core), sorter(core, True), grower()

    def place_block(i):
        rows = part(i, 96)
        both = jnp.concatenate([mine[rows, :], other[rows, :]], axis=0)
        placed = jnp.dot(sort, both[:, 0:256], preferred_element_type=F32).astype(BF)
        units = part(i, 192)
        w_down[units, :] = jnp.dot(sort_devices, both[:, 128:384], preferred_element_type=F32).astype(BF)
        here = part(i, 48)
        for block in range(4):
            w_up[here, DG * block : DG * block + DG] = placed[48 * block : 48 * block + 48, 0:DG]
        hidden = jnp.dot(grow, side[here, :].astype(BF), preferred_element_type=F32)
        up_bias[units, :] = lane_sum(jnp.where(pick_hidden(), hidden, 0.0))

    wait(arriving[0])
    each(16, place_block, unroll=4)
    wait(*arriving[1:])

    def first_norm(i):
        rows = part(i, BAND)
        first = hat[rows, :] * side[rows, 4:5] + side[rows, 6:7]
        d_first[rows, :] = first
        first_low[rows, :] = first.astype(BF)

    each(BANDS, first_norm, unroll=2)

    def feed(g):
        rows = part(g, DG)
        for third in range(3):
            units = part(g * 3 + third, 256)
            upper = dot(w_up[rows, 256 * third : 256 * third + 256], first_low[rows, :], 0, 0) + up_bias[units, :]
            below = 0.5 + 0.5 * lax.erf(upper * 0.7071067811865476)
            density = jnp.exp(-0.5 * upper * upper) * 0.3989422804014327
            active[units, :] = (upper * below).astype(BF)
            slope[units, :] = below + upper * density
        units = part(g, D)
        branch = dot(w_down[units, :], active[units, :], 0, 0)[64:256]
        d_first[rows, :] += branch + side[rows, 3:4]

    each(G, feed)

    (mean,) = means(1, lambda rows: (d_first[rows, :],))
    (variance,) = means(1, lambda rows: ((d_first[rows, :] - mean) ** 2,))
    scale = lax.rsqrt(variance + EPS)

    def norm(rows):
        hats = (d_first[rows, :] - mean) * scale
        d_first[rows, :] = hats
        result[rows, :] = (hats * side[rows, 5:6] + side[rows, 7:8]).astype(BF)
        slopes = c_t[rows, :].astype(F32)
        g_side[rows, :] = jnp.zeros((BAND, 128), F32)
        g_side[rows, 5:6] = lane_sum(slopes * hats)
        g_side[rows, 7:8] = lane_sum(slopes)
        slopes = slopes * side[rows, 5:6]
        return slopes, slopes * hats

    lean, tilt = means(2, norm)
    start(leaving[0])

    def norm_back(i):
        rows = part(i, BAND)
        slopes = c_t[rows, :].astype(F32) * side[rows, 5:6]
        back = scale * (slopes - lean - d_first[rows, :] * tilt)
        d_first[rows, :] = back
        low = back.astype(BF)
        g_side[rows, 3:4] = lane_sum(low.astype(F32))
        low_t[rows, :] = low

    each(BANDS, norm_back, unroll=2)
    for g in range(G):
        branch_pad[g, 0:64, :] = jnp.zeros((64, TOK), BF)
        branch_pad[g, 64:256, :] = low_t[DG * g : DG * (g + 1), :]

    def feed_back(g):
        rows = part(g, DG)
        for third in range(3):
            units = part(g * 3 + third, 256)
            span = slice(256 * third, 256 * third + 256)
            d_active = dot(w_down[units, :], branch_pad[g], 1, 0)
            d_upper = (d_active * slope[units, :]).astype(BF)
            up_bias[units, :] = lane_sum(d_upper.astype(F32))
            g_down[units, :] = dot(active[units, :], branch_pad[g], 1, 1).astype(BF)
            g_up[rows, span] = dot(first_low[rows, :], d_upper, 1, 1).astype(BF)
            active[units, :] = d_upper
        d_first[rows, :] += dot(w_up[rows, :], active[part(g, D), :], 1, 0)

    each(G, feed_back)
    start(leaving[1])
    unsort, unsort_devices = unsorter(core), unsorter(core, True)

    def tile_block(i):
        here, units, rows = part(i, 48), part(i, 192), part(i, 96)
        hidden = jnp.where(pick_hidden(), up_bias[units, :], 0.0)
        g_side[here, :] += dot(grow.astype(F32), hidden, 0, 0)
        ups = jnp.concatenate([g_up[here, DG * block : DG * block + DG] for block in range(4)], axis=0)
        ups = jnp.concatenate([ups, jnp.zeros((192, 64), BF)], axis=1)
        placed = dot(unsort, ups, 1, 0)
        downs = dot(unsort_devices, g_down[units, :], 1, 0)
        for target, begin in ((keep, 0), (send, 96)):
            span = slice(begin, begin + 96)
            target[rows, 0:128] = placed[span, 0:128].astype(BF)
            target[rows, 128:256] = (placed[span, 128:256] + downs[span, 0:128]).astype(BF)
            target[rows, 256:384] = downs[span, 128:256].astype(BF)

    each(16, tile_block, unroll=4)
    start(leaving[2])
    wait(*leaving)


def attention_back_kernel(
    d_first_far, hat_far, side_far, g_feed_far, w_out_far, ctx_far, q_far, k_far, v_far, probs_far, small_far, x_far,
    scale,
    d_sum_far, packed_far, keep, send,
    d_first, hat, side, g_feed, w_out, ctx_t, q_t, k_t, v_t, probs, probs_small, x_t,
    d_sum, packed_t, low_t, d_ctx, g_side, g_qkv, g_out, arrive, leave,
):
    arriving = moves(
        [(d_first_far, d_first), (hat_far, hat), (side_far, side), (g_feed_far, g_feed), (w_out_far, w_out),
         (ctx_far, ctx_t), (q_far, q_t), (k_far, k_t), (v_far, v_t), (probs_far, probs), (small_far, probs_small),
         (x_far, x_t)],
        arrive,
    )
    leaving = moves([(d_sum, d_sum_far), (packed_t, packed_far)], leave)
    start(*arriving)
    wait(*arriving[:4])

    def norm_sums(rows):
        slopes, hats = d_first[rows, :], hat[rows, :]
        g_side[rows, :] = g_feed[rows, :]
        g_side[rows, 4:5] = lane_sum(slopes * hats)
        g_side[rows, 6:7] = lane_sum(slopes)
        slopes = slopes * side[rows, 4:5]
        return slopes, slopes * hats

    lean, tilt = means(2, norm_sums)

    def norm_back(i):
        rows = part(i, BAND)
        back = scale[...] * (d_first[rows, :] * side[rows, 4:5] - lean - hat[rows, :] * tilt)
        d_sum[rows, :] = back
        low = back.astype(BF)
        g_side[rows, 2:3] = lane_sum(low.astype(F32))
        low_t[rows, :] = low

    each(BANDS, norm_back, unroll=2)

    start(leaving[0])
    wait(*arriving[4:6])

    def project_back(i):
        rows = part(i, 128)
        g_out[rows, :] = dot(ctx_t[rows, :], low_t[...], 1, 1).astype(BF)
        d_ctx[rows, :] = dot(w_out[rows, :], low_t[...], 1, 0).astype(BF)

    each(6, project_back)
    wait(*arriving[6:])

    def attend_back(g):
        for third in range(3):
            head = g * 3 + third
            rows = part(head, HEAD)
            at = HEAD * third
            for cols, kept in zip(SPANS, (probs, probs_small), strict=True):
                d_out = d_ctx[rows, cols]
                share_low = kept[head]
                share = share_low.astype(F32)
                d_share = dot(v_t[rows, cols], d_out, 0, 0)
                packed_t[g, 3 * DG + at : 3 * DG + at + HEAD, cols] = dot(d_out, share_low, 1, 1).astype(BF)
                d_scores = share * (d_share - jnp.sum(d_share * share, axis=0, keepdims=True))
                d_scores = d_scores.astype(BF)
                packed_t[g, DG + at : DG + at + HEAD, cols] = (0.125 * dot(k_t[rows, cols], d_scores, 1, 0)).astype(BF)
                packed_t[g, at : at + HEAD, cols] = dot(q_t[rows, cols], d_scores, 1, 1).astype(BF)
        rows = part(g, DG)
        packed_t[g, WIDE : 3 * DG, :] = jnp.zeros((DG, TOK), BF)
        g_qkv[rows, 0:WIDE] = dot(x_t[rows, :], packed_t[g, 0:WIDE, :], 1, 1).astype(BF)
        g_qkv[rows, 512:768] = dot(x_t[rows, :], packed_t[g, 512:768, :], 1, 1).astype(BF)
        g_side[rows, 0:1] = lane_sum(packed_t[g, DG:WIDE, :].astype(F32))
        g_side[rows, 1:2] = lane_sum(packed_t[g, 3 * DG :, :].astype(F32))

    each(G, attend_back)
    start(leaving[1])
    unsort = unsorter(own_core())

    def tile_block(i):
        here, rows = part(i, 48), part(i, 96)
        blocks = []
        for begin in (0, WIDE):
            mixed_out, mixed_qkv = g_out[here, begin + 128 : begin + 256], g_qkv[here, begin + 128 : begin + 256]
            blocks.append(
                [
                    g_out[here, begin : begin + 128],
                    jnp.where(low_lanes(), mixed_out, mixed_qkv),
                    g_qkv[here, begin + 256 : begin + 384],
                ]
            )
            blocks.append(
                [
                    g_qkv[here, 0:128] if begin == 0 else g_side[here, :].astype(BF),
                    jnp.where(low_lanes(), mixed_qkv, mixed_out),
                    g_out[here, begin + 256 : begin + 384],
                ]
            )
        both = jnp.concatenate([jnp.concatenate(block, axis=1) for block in blocks], axis=0)
        placed = dot(unsort, both, 1, 0).astype(BF)
        keep[rows, :] = placed[0:96]
        send[rows, :] = placed[96:192]

    each(16, tile_block, unroll=4)
    wait(*leaving)


def token_kernel(w_qkv, packed_t, d_sum, turn, result, grad_tokens, output, high, low):
    def total(g):
        rows = part(g, DG)
        back = dot(w_qkv[rows, 0:WIDE], packed_t[g, 0:WIDE, :], 1, 0)
        whole = d_sum[rows, :] + back + dot(w_qkv[rows, 512:768], packed_t[g, 512:768, :], 1, 0)
        high[rows, :] = whole.astype(BF)
        low[rows, :] = (whole - high[rows, :].astype(F32)).astype(BF)

    each(G, total)

    def write(i):
        rows = part(i, 256)
        grad_tokens[:, rows] = dot(turn[...], high[rows, :], 1, 1) + dot(turn[...], low[rows, :], 1, 1)
        output[:, rows] = dot(turn[...], result[rows, :], 1, 1).astype(BF)

    each(3, write)


def add_kernel(left, right, total):
    total[...] = (left[...].astype(F32) + right[...].astype(F32)).astype(BF)


def tile_sum(parts):
    total = jnp.zeros((2 * ROWS, WIDE), F32)
    for pair in range(CHIPS // 2):
        total += parts[2 * ROWS * pair : 2 * ROWS * (pair + 1), :].astype(F32)
    return total[0:ROWS] + total[ROWS:]


def sum_feed_kernel(parts, up, down):
    total = tile_sum(parts)
    for block in range(4):
        up[:, DG * block : DG * block + DG] = total[6 * block : 6 * block + 6, 0:DG]
    down[...] = total[:, DG:WIDE]


def sum_attention_kernel(parts, qkv, out, qv, outb, upb, gain, shift, square):
    total = tile_sum(parts)
    for block in range(4):
        rows, lanes = slice(6 * block, 6 * block + 6), slice(DG * block, DG * block + DG)
        here, there = (slice(0, DG), slice(DG, WIDE))[:: 1 - 2 * (block % 2)]
        out[:, lanes] = total[rows, here]
        if block < 3:
            qkv[:, lanes] = total[rows, there]
    square[...] = jnp.zeros_like(square)
    square[0:6, :] = total[SIDE:ROWS, 0:128]
    columns = square[...].T
    for place, rows in enumerate((qv, outb, gain, shift)):
        rows[...] = columns[2 * place : 2 * place + 2, 0:6]
    lanes = (iota((128, ROWS), 0) - 8 == iota((128, ROWS), 1) % 4).astype(F32)
    grown = jnp.dot(square[0:8, :], lanes, preferred_element_type=F32, precision=lax.Precision.HIGHEST)
    grown = jnp.where(iota((8, ROWS), 1) // 4 == iota((8, ROWS), 0), grown, 0.0)
    upb[...] = jnp.sum(grown, axis=0, keepdims=True)


FAR = pl.BlockSpec(memory_space=pl.ANY)
NEAR = pl.BlockSpec(memory_space=pltpu.VMEM)


def call(kernel, shapes, scratch, name, limit, flops=0, near=(), sems=()):
    scratch = [pltpu.VMEM(*shape) for shape in scratch] + [pltpu.SemaphoreType.DMA((count,)) for count in sems]

    def specs(count, base):
        return [NEAR if not sems or base + i in near else FAR for i in range(count)]

    def run(*inputs):
        if sems:
            inputs = [x if i in near else pltpu.with_memory_space_constraint(x, pltpu.HBM) for i, x in enumerate(inputs)]
        return pl.pallas_call(
            kernel,
            in_specs=specs(len(inputs), 0),
            out_specs=specs(len(shapes), len(inputs)),
            out_shape=[
                pltpu.HBM(*shape) if sems and len(inputs) + i not in near else jax.ShapeDtypeStruct(*shape)
                for i, shape in enumerate(shapes)
            ],
            scratch_shapes=scratch,
            compiler_params=pltpu.CompilerParams(vmem_limit_bytes=limit * MIB),
            cost_estimate=pl.CostEstimate(flops=flops, bytes_accessed=0, transcendentals=0),
            name=name,
        )(*inputs)

    return run


def exchange(array):
    groups = [[y * 32 + i for y in range(4) for i in range(core, 32, 2)] for core in range(2)]
    return lax.all_to_all(array, AXES, 0, 0, axis_index_groups=groups, tiled=True)


def swap(array):
    return lax.ppermute(array, "fsdp", [(i, i ^ 1) for i in range(32)])


def local(
    tokens, segment_ids, qkv_weight, out_weight, up_weight, down_weight,
    qv_bias, out_bias, up_bias, norm_gain, norm_shift, cotangent,
):
    tile, probs = ((TILES, WIDE), BF), ((HEADS, LONG, LONG), BF)
    full, low, square, side = ((D, TOK), F32), ((D, TOK), BF), ((D, D), BF), ((D, 128), F32)
    small, packed, row = ((HEADS, 128, 128), BF), ((G, D, TOK), BF), ((1, TOK), F32)
    one_tile = ((ROWS, WIDE), F32)
    shards = (qkv_weight, out_weight, qv_bias, out_bias, up_bias.reshape(1, ROWS), norm_gain, norm_shift)
    pack_a = call(
        pack_attention_kernel, [tile], [*((x.shape, x.dtype) for x in shards), one_tile, ((128, 128), F32)],
        "pack_attention", 12, near=(7,), sems=(7,),
    )(*shards)[0]
    mine_a = exchange(pack_a)
    pack_f = call(
        pack_feed_kernel, [tile], [((6, D), BF), ((ROWS, DG), BF), one_tile],
        "pack_feed", 12, flops=10**9, near=(2,), sems=(2,),
    )(up_weight, down_weight)[0]
    turn, x_t, c_t = call(
        turn_kernel, [((TOK, TOK), BF), low, low], [], "turn", 60, flops=2 * 2 * TOK * TOK * D
    )(tokens, segment_ids, cotangent)
    mine_a, pack_f, x_t = lax.optimization_barrier((mine_a, pack_f, x_t))
    mine_f = exchange(pack_f)
    w_qkv, w_out, sides, q_t, k_t, v_t, ctx_t, shares, shares_small, hat, scale = call(
        attention_kernel,
        [square, square, side, low, low, low, low, probs, small, full, row],
        [low, square, square, side, low, low, low, low, probs, small, full, full],
        "attention", 44, flops=15 * 10**9, near=(0, 1, 2, 14), sems=(1, 11),
    )(segment_ids, mine_a, swap(mine_a), x_t)
    mine_f, hat = lax.optimization_barrier((mine_f, hat))
    result, d_first, g_side, keep_f, send_f = call(
        feed_kernel,
        [low, full, side, tile, tile],
        [side, full, low, low, full, side,
         square, ((F, 256), BF), ((F, 1), F32), low, ((F, TOK), BF), ((F, TOK), F32), low,
         ((G, 256, TOK), BF), square, ((F, 256), BF)],
        "feed", 44, flops=20 * 10**9, near=(0, 1, 8, 9), sems=(3, 3),
    )(mine_f, swap(mine_f), sides, hat, c_t)
    chip_f = call(add_kernel, [tile], [], "chip_sum_feed", 12)(keep_f, swap(send_f))[0]
    chip_f, d_first = lax.optimization_barrier((chip_f, d_first))
    parts_f = exchange(chip_f)
    d_sum, d_packed, keep_a, send_a = call(
        attention_back_kernel,
        [full, packed, tile, tile],
        [full, full, side, side, square, low, low, low, low, probs, small, low,
         full, packed, low, low, side, square, square],
        "attention_back", 44, flops=20 * 10**9, near=(12, 15, 16), sems=(12, 2),
    )(d_first, hat, sides, g_side, w_out, ctx_t, q_t, k_t, v_t, shares, shares_small, x_t, scale)
    keep_a, send_a, parts_f = lax.optimization_barrier((keep_a, send_a, parts_f))
    chip_a = call(add_kernel, [tile], [], "chip_sum_attention", 12)(keep_a, swap(send_a))[0]
    chip_a, d_sum, parts_f = lax.optimization_barrier((chip_a, d_sum, parts_f))
    parts_a = exchange(chip_a)
    grad_tokens, output = call(
        token_kernel, [((TOK, D), F32), ((TOK, D), BF)], [low, low], "token_gradient", 60, flops=4 * 2 * TOK * TOK * D
    )(w_qkv, d_packed, d_sum, turn, result)
    up, down = call(sum_feed_kernel, [((6, D), F32), ((ROWS, DG), F32)], [], "sum_feed", 12, flops=10**9)(parts_f)
    qkv, out, qv, outb, upb, gain, shift = call(
        sum_attention_kernel,
        [((6, QKV), F32), ((6, D), F32), ((2, 6), F32), ((2, 6), F32), ((1, ROWS), F32), ((2, 6), F32), ((2, 6), F32)],
        [((128, 128), F32)], "sum_attention", 12,
    )(parts_a)
    return output, grad_tokens, qkv, out, up, down, qv, outb, upb.reshape(ROWS), gain, shift


def solution(mesh):
    rows, columns, flat = P(AXES, None), P(None, AXES), P(AXES)
    in_specs = (rows, rows, rows, rows, rows, rows, columns, columns, flat, columns, columns, rows)
    out_specs = (rows, rows, rows, rows, rows, rows, columns, columns, flat, columns, columns)
    return jax.shard_map(local, mesh=mesh, in_specs=in_specs, out_specs=out_specs, check_vma=False)
```

```python
import jax
import jax.numpy as jnp
from jax import lax
from jax.experimental import pallas as pl
from jax.experimental.pallas import tpu as pltpu
from jax.sharding import PartitionSpec as P

AXES = ("dp", "fsdp")
D = 768
F = 3072
G = 4
DG = 192
QKV = 3 * DG
HEADS = 12
HEAD = 64
TOK = 512
LONG = 384
CHIPS = 64
ROWS = 24
EPS = 1e-05
BAND = 64
BANDS = D // BAND
BF = jnp.bfloat16
F32 = jnp.float32
MIB = 1 << 20

SIDE = 18
WIDE = 2 * DG
TILES = CHIPS * ROWS


def dot(left, right, over_left, over_right):
    return lax.dot_general(
        left, right, (((over_left,), (over_right,)), ((), ())), preferred_element_type=F32
    )


def iota(shape, axis):
    return lax.broadcasted_iota(jnp.int32, shape, axis)


def each(count, step):
    for i in range(count):
        step(i)


def part(i, size):
    return slice(i * size, (i + 1) * size)


def halves(chunk):
    return jnp.sum(chunk.reshape(BAND // 8, 8, TOK), axis=0)


def means(count, bands):
    sums = [jnp.zeros((8, TOK), F32)] * count
    for i in range(BANDS):
        sums = [kept + halves(chunk) for kept, chunk in zip(sums, bands(part(i, BAND)), strict=True)]
    return [jnp.sum(total, axis=0, keepdims=True) * (1.0 / D) for total in sums]


def lane_sum(chunk):
    return jnp.sum(chunk, axis=1, keepdims=True)


def pick_hidden():
    return iota((192, 128), 1) - 8 == (iota((192, 128), 0) & 3)


def arrival(core, by_device, axis):
    sorted_row = iota((192, 1) if axis == 0 else (1, 192), axis)
    if by_device:
        device = (sorted_row * 2731) >> 16
        row = sorted_row - device * ROWS
    else:
        block = (sorted_row * 1366) >> 16
        sixth = (sorted_row * 10923) >> 16
        device = sixth - block * 8
        row = block * 6 + sorted_row - sixth * 6
    return jnp.where((device & 1) == core, 0, 96) + (device >> 1) * ROWS + row


def sorter(core, by_device=False):
    return (arrival(core, by_device, 0) == iota((192, 192), 1)).astype(F32).astype(BF)


def unsorter(core, by_device=False):
    return (arrival(core, by_device, 1) == iota((192, 192), 0)).astype(F32).astype(BF)


def grower():
    return ((iota((192, 48), 0) >> 2) == iota((192, 48), 1)).astype(F32).astype(BF)


def low_lanes():
    return iota((48, 128), 1) < 64


def pack_kernel(*refs):
    far, packed, near, (tile, square, twice, arrive, leave) = refs[:9], refs[9], refs[10:19], refs[19:]
    arriving = moves(zip(far, near, strict=True), arrive)
    start(*arriving)
    wait(*arriving)
    qkv, out, up, down, qv, outb, upb, gain, shift = near
    square[...] = jnp.zeros_like(square)
    for place, rows in enumerate((qv, outb, gain, shift)):
        square[2 * place : 2 * place + 2, 0:6] = rows[...].astype(F32)
    columns = square[...].T
    grown = jnp.where(iota((8, ROWS), 1) // 4 == iota((8, ROWS), 0), upb[...].astype(F32), 0.0)
    lanes = (iota((ROWS, 128), 1) - 8 == iota((ROWS, 128), 0) % 4).astype(F32)
    hidden = jnp.dot(grown, lanes, preferred_element_type=F32)
    tile[...] = jnp.zeros_like(tile)
    for block in range(4):
        rows, lanes = slice(6 * block, 6 * block + 6), slice(DG * block, DG * block + DG)
        here, there = (slice(0, DG), slice(DG, WIDE))[:: 1 - 2 * (block % 2)]
        tile[rows, here] = out[:, lanes].astype(F32)
        if block < 3:
            tile[rows, there] = qkv[:, lanes].astype(F32)
        tile[rows, WIDE : WIDE + DG] = up[:, lanes].astype(F32)
    tile[SIDE:ROWS, 0:128] = (columns[0:8] + hidden)[0:6]
    tile[:, WIDE + DG : D] = down[...].astype(F32)
    twice[0:ROWS, :] = tile[...].astype(BF)
    twice[ROWS:, :] = tile[...].astype(BF)
    pairs = [(twice, packed.at[2 * ROWS * pair : 2 * ROWS * (pair + 1), :]) for pair in range(CHIPS // 2)]
    leaving = moves(pairs, leave)
    start(*leaving)
    wait(*leaving)


def turn_kernel(tokens, segments, cotangent, turn, x_t, c_t):
    ids = segments[...]
    count0 = jnp.sum((ids == 0).astype(jnp.int32))
    count1 = jnp.sum((ids == 1).astype(jnp.int32))
    start = jnp.where(count0 == LONG, 0, jnp.where(count1 == LONG, count0, count0 + count1))

    def turn_rows(i):
        place = iota((64, TOK), 1) + start
        place = jnp.where(place >= TOK, place - TOK, place)
        turn[part(i, 64), :] = jnp.where(iota((64, TOK), 0) + i * 64 == place, 1.0, 0.0).astype(BF)

    each(8, turn_rows)

    def turn_features(i):
        x_t[part(i, 256), :] = dot(tokens[:, part(i, 256)], turn[...], 0, 0).astype(BF)
        c_t[part(i, 256), :] = dot(cotangent[:, part(i, 256)], turn[...], 0, 0).astype(BF)

    each(3, turn_features)


def moves(pairs, sems):
    return [pltpu.make_async_copy(source, target, sems.at[i]) for i, (source, target) in enumerate(pairs)]


def start(*copies):
    for copy in copies:
        copy.start()


def wait(*copies):
    for copy in copies:
        copy.wait()


def own_core():
    return lax.rem(lax.axis_index("fsdp"), 2)


SPANS = (slice(0, LONG), slice(LONG, TOK))


def layer_kernel(
    segments, mine_far, other, x_far, c_far,
    w_qkv_far, result_far, d_sum_far, packed_far, keep_far, send_far,
    mine, send, x_t, c_t, w_qkv, w_out, w_up, w_down, side, up_bias, q_t, k_t, v_t, ctx_t, probs, probs_small,
    first_low, hat, hat_two, active, slope, stream, d_first, d_upper, d_ctx, result, low_t, branch_pad, packed_t,
    g_qkv, g_out, g_up, g_down, g_side, arrive, leave,
):
    core = own_core()
    quarters = [slice(TILES // 4 * i, TILES // 4 * (i + 1)) for i in range(4)]
    arriving = moves(
        [(mine_far.at[rows, :], mine.at[rows, :]) for rows in quarters] + [(x_far, x_t), (c_far, c_t)],
        arrive,
    )
    leaving = moves(
        [(w_qkv, w_qkv_far), (result, result_far), (stream, d_sum_far)]
        + [(packed_t.at[g], packed_far.at[g]) for g in range(G)]
        + [
            (near.at[rows, :], far.at[rows, :])
            for rows in quarters
            for near, far in ((mine, keep_far), (send, send_far))
        ],
        leave,
    )
    start(*arriving)
    sort, sort_devices, grow = sorter(core), sorter(core, True), grower()

    def both(i, lanes):
        rows = part(i, 96)
        return jnp.concatenate([mine[rows, lanes], other[rows, lanes]], axis=0)

    def place_attention(i):
        here = part(i, 48)
        placed = jnp.dot(sort, both(i, slice(0, WIDE)), preferred_element_type=F32).astype(BF)
        blocks = [placed[48 * block : 48 * block + 48] for block in range(4)]
        for begin, target, left, right in (
            (0, w_out, 0, 1), (WIDE, w_out, 2, 3), (0, w_qkv, 1, 0), (WIDE, w_qkv, 3, 2),
        ):
            target[here, begin : begin + 128] = blocks[left][:, 0:128]
            target[here, begin + 128 : begin + 256] = jnp.where(
                low_lanes(), blocks[left][:, 128:256], blocks[right][:, 128:256]
            )
            target[here, begin + 256 : begin + 384] = blocks[right][:, 256:384]
        side[here, :] = blocks[3][:, 0:128].astype(F32)

    def place_feed(i):
        here, units = part(i, 48), part(i, 192)
        placed = jnp.dot(sort, both(i, slice(WIDE, WIDE + 256)), preferred_element_type=F32).astype(BF)
        for block in range(4):
            w_up[here, DG * block : DG * block + DG] = placed[48 * block : 48 * block + 48, 0:DG]
        rows = jnp.dot(sort_devices, both(i, slice(512, 768)), preferred_element_type=F32)
        w_down[units, :] = rows.astype(BF)
        hidden = jnp.dot(grow, side[here, :].astype(BF), preferred_element_type=F32)
        up_bias[units, :] = lane_sum(jnp.where(pick_hidden(), hidden, 0.0))

    for quarter in range(4):
        wait(arriving[quarter])
        each(4, lambda i, quarter=quarter: place_attention(i + 4 * quarter))
    start(leaving[0])
    wait(arriving[4])

    ids = segments[...]
    count0 = jnp.sum((ids == 0).astype(jnp.int32))
    count1 = jnp.sum((ids == 1).astype(jnp.int32))
    count2 = TOK - count0 - count1
    border = jnp.where(count0 == LONG, count1, jnp.where(count1 == LONG, count2, count0))
    together = (iota((128, 128), 0) < border) == (iota((128, 128), 1) < border)

    def attend(g):
        rows = part(g, DG)
        packed = dot(w_qkv[rows, 0:WIDE], x_t[rows, :], 0, 0)
        k_t[rows, :] = packed[0:DG].astype(BF)
        q_t[rows, :] = ((packed[DG:WIDE] + side[rows, 0:1]).astype(BF).astype(F32) * 0.125).astype(BF)
        packed = dot(w_qkv[rows, 512:768], x_t[rows, :], 0, 0)
        v_t[rows, :] = (packed[64:256] + side[rows, 1:2]).astype(BF)
        for third in range(3):
            head = g * 3 + third
            rows = part(head, HEAD)
            for cols, kept in zip(SPANS, (probs, probs_small), strict=True):
                scores = dot(k_t[rows, cols], q_t[rows, cols], 0, 0)
                if kept is probs_small:
                    scores = jnp.where(together, scores, -1000000000.0)
                power = jnp.exp(scores - jnp.max(scores, axis=0, keepdims=True))
                share = (power * (1.0 / jnp.sum(power, axis=0, keepdims=True))).astype(BF)
                kept[head] = share
                ctx_t[rows, cols] = dot(v_t[rows, cols], share, 1, 0).astype(BF)

    each(G, attend)

    def project(i):
        rows = part(i, 128)
        attended = dot(w_out[:, rows], ctx_t[...], 0, 0) + side[rows, 2:3]
        stream[rows, :] = x_t[rows, :].astype(F32) + attended

    each(6, project)
    (mean_one,) = means(1, lambda rows: (stream[rows, :],))

    def spread_one(rows):
        place_feed(rows.start // BAND)
        return ((stream[rows, :] - mean_one) ** 2,)

    (variance,) = means(1, spread_one)
    scale_one = lax.rsqrt(variance + EPS)

    def norm_one(i):
        rows = part(i, BAND)
        hats = (stream[rows, :] - mean_one) * scale_one
        hat[rows, :] = hats
        first = hats * side[rows, 4:5] + side[rows, 6:7]
        stream[rows, :] = first
        first_low[rows, :] = first.astype(BF)
        if i % 3 == 0:
            place_feed(BANDS + i // 3)

    each(BANDS, norm_one)

    def feed(g):
        rows = part(g, DG)
        for third in range(3):
            units = part(g * 3 + third, 256)
            upper = dot(w_up[rows, 256 * third : 256 * third + 256], first_low[rows, :], 0, 0) + up_bias[units, :]
            below = 0.5 + 0.5 * lax.erf(upper * 0.7071067811865476)
            density = jnp.exp(-0.5 * upper * upper) * 0.3989422804014327
            active[units, :] = (upper * below).astype(BF)
            slope[units, :] = below + upper * density
        units = part(g, D)
        branch = dot(w_down[units, :], active[units, :], 0, 0)[64:256]
        stream[rows, :] += branch + side[rows, 3:4]

    each(G, feed)
    wait(arriving[5])

    (mean_two,) = means(1, lambda rows: (stream[rows, :],))
    (variance,) = means(1, lambda rows: ((stream[rows, :] - mean_two) ** 2,))
    scale_two = lax.rsqrt(variance + EPS)

    def norm_two(rows):
        hats = (stream[rows, :] - mean_two) * scale_two
        hat_two[rows, :] = hats
        result[rows, :] = (hats * side[rows, 5:6] + side[rows, 7:8]).astype(BF)
        slopes = c_t[rows, :].astype(F32) * side[rows, 5:6]
        return slopes, slopes * hats

    lean_two, tilt_two = means(2, norm_two)
    start(leaving[1])
    for g in range(G):
        branch_pad[g, 0:64, :] = jnp.zeros((64, TOK), BF)

    def norm_two_back(i):
        rows = part(i, BAND)
        slopes = c_t[rows, :].astype(F32) * side[rows, 5:6]
        back = scale_two * (slopes - lean_two - hat_two[rows, :] * tilt_two)
        stream[rows, :] = back
        branch_pad[i // 3, 64 + BAND * (i % 3) : 128 + BAND * (i % 3), :] = back.astype(BF)

    each(BANDS, norm_two_back)

    def feed_back(g):
        rows = part(g, DG)
        for third in range(3):
            units = part(g * 3 + third, 256)
            d_active = dot(w_down[units, :], branch_pad[g], 1, 0)
            d_upper[units, :] = (d_active * slope[units, :]).astype(BF)
        d_first[rows, :] = stream[rows, :] + dot(w_up[rows, :], d_upper[part(g, D), :], 1, 0)

    each(G, feed_back)

    def norm_one_sums(rows):
        i = rows.start // BAND
        units = part(i, 256)
        g_down[units, :] = dot(active[units, :], branch_pad[i // 3], 1, 1).astype(BF)
        slopes = d_first[rows, :] * side[rows, 4:5]
        return slopes, slopes * hat[rows, :]

    lean_one, tilt_one = means(2, norm_one_sums)

    def norm_one_back(i):
        rows, units = part(i, BAND), part(i, 256)
        back = scale_one * (d_first[rows, :] * side[rows, 4:5] - lean_one - hat[rows, :] * tilt_one)
        stream[rows, :] = back
        low_t[rows, :] = back.astype(BF)
        span = slice(256 * (i % 3), 256 * (i % 3) + 256)
        g_up[part(i // 3, DG), span] = dot(first_low[part(i // 3, DG), :], d_upper[units, :], 1, 1).astype(BF)

    each(BANDS, norm_one_back)
    start(leaving[2])

    def project_back(i):
        rows = part(i, 128)
        d_ctx[rows, :] = dot(w_out[rows, :], low_t[...], 1, 0).astype(BF)
        g_out[rows, :] = dot(ctx_t[rows, :], low_t[...], 1, 1).astype(BF)

    each(6, project_back)

    unsort, unsort_devices = unsorter(core), unsorter(core, True)

    def side_sums(i):
        rows = part(i, BAND)
        g_side[rows, :] = jnp.zeros((BAND, 128), F32)
        slopes = c_t[rows, :].astype(F32)
        g_side[rows, 5:6] = lane_sum(slopes * hat_two[rows, :])
        g_side[rows, 7:8] = lane_sum(slopes)
        slopes = d_first[rows, :]
        g_side[rows, 4:5] = lane_sum(slopes * hat[rows, :])
        g_side[rows, 6:7] = lane_sum(slopes)
        g_side[rows, 2:3] = lane_sum(low_t[rows, :].astype(F32))
        branch = branch_pad[i // 3, 64 + BAND * (i % 3) : 128 + BAND * (i % 3), :]
        g_side[rows, 3:4] = lane_sum(branch.astype(F32))
        units = part(i, 256)
        up_bias[units, :] = lane_sum(d_upper[units, :].astype(F32))

    def tile_feed(i):
        here, units, rows = part(i, 48), part(i, 192), part(i, 96)
        zero = jnp.zeros((48, 64), BF)
        ups = [jnp.concatenate([g_up[here, DG * block : DG * block + DG], zero], axis=1) for block in range(4)]
        placed = dot(unsort, jnp.concatenate(ups, axis=0), 1, 0)
        downs = dot(unsort_devices, g_down[units, :], 1, 0)
        for target, begin in ((mine, 0), (send, 96)):
            span = slice(begin, begin + 96)
            target[rows, 384:512] = placed[span, 0:128].astype(BF)
            target[rows, 512:640] = (placed[span, 128:256] + downs[span, 0:128]).astype(BF)
            target[rows, 640:768] = downs[span, 128:256].astype(BF)

    def attend_back(g):
        for third in range(3):
            head = g * 3 + third
            rows = part(head, HEAD)
            at = HEAD * third
            for cols, kept in zip(SPANS, (probs, probs_small), strict=True):
                d_out = d_ctx[rows, cols]
                share_low = kept[head]
                share = share_low.astype(F32)
                d_share = dot(v_t[rows, cols], d_out, 0, 0)
                packed_t[g, 3 * DG + at : 3 * DG + at + HEAD, cols] = dot(d_out, share_low, 1, 1).astype(BF)
                d_scores = share * (d_share - jnp.sum(d_share * share, axis=0, keepdims=True))
                d_scores = d_scores.astype(BF)
                packed_t[g, DG + at : DG + at + HEAD, cols] = (0.125 * dot(k_t[rows, cols], d_scores, 1, 0)).astype(BF)
                packed_t[g, at : at + HEAD, cols] = dot(q_t[rows, cols], d_scores, 1, 1).astype(BF)
            side_sums(head)
            tile_feed(head)
        rows = part(g, DG)
        packed_t[g, WIDE : 3 * DG, :] = jnp.zeros((DG, TOK), BF)
        start(leaving[3 + g])
        g_qkv[rows, 0:WIDE] = dot(x_t[rows, :], packed_t[g, 0:WIDE, :], 1, 1).astype(BF)
        g_qkv[rows, 512:768] = dot(x_t[rows, :], packed_t[g, 512:768, :], 1, 1).astype(BF)
        g_side[rows, 0:1] = lane_sum(packed_t[g, DG:WIDE, :].astype(F32))
        g_side[rows, 1:2] = lane_sum(packed_t[g, 3 * DG :, :].astype(F32))
        tile_feed(12 + g)

    each(G, attend_back)

    def tile_attention(i):
        here, units, rows = part(i, 48), part(i, 192), part(i, 96)
        hidden = jnp.where(pick_hidden(), up_bias[units, :], 0.0).astype(BF)
        bias = (g_side[here, :] + dot(grow, hidden, 0, 0)).astype(BF)
        blocks = []
        for begin in (0, WIDE):
            mixed_out, mixed_qkv = g_out[here, begin + 128 : begin + 256], g_qkv[here, begin + 128 : begin + 256]
            for odd in range(2):
                first = (g_qkv[here, 0:128] if begin == 0 else bias) if odd else g_out[here, begin : begin + 128]
                left, right = (mixed_qkv, mixed_out) if odd else (mixed_out, mixed_qkv)
                last = (g_out if odd else g_qkv)[here, begin + 256 : begin + 384]
                blocks.append(jnp.concatenate([first, jnp.where(low_lanes(), left, right), last], axis=1))
        placed = dot(unsort, jnp.concatenate(blocks, axis=0), 1, 0).astype(BF)
        mine[rows, 0:WIDE] = placed[0:96]
        send[rows, 0:WIDE] = placed[96:192]

    for quarter in range(4):
        each(4, lambda i, quarter=quarter: tile_attention(i + 4 * quarter))
        start(*leaving[7 + 2 * quarter : 9 + 2 * quarter])
    wait(*leaving)


def token_kernel(w_qkv, packed_t, d_sum, turn, result, grad_tokens, output, high, low):
    def total(g):
        rows = part(g, DG)
        back = dot(w_qkv[rows, 0:WIDE], packed_t[g, 0:WIDE, :], 1, 0)
        whole = d_sum[rows, :] + back + dot(w_qkv[rows, 512:768], packed_t[g, 512:768, :], 1, 0)
        high[rows, :] = whole.astype(BF)
        low[rows, :] = (whole - high[rows, :].astype(F32)).astype(BF)

    each(G, total)

    def write(i):
        rows = part(i, 256)
        grad_tokens[:, rows] = dot(turn[...], high[rows, :], 1, 1) + dot(turn[...], low[rows, :], 1, 1)
        output[:, rows] = dot(turn[...], result[rows, :], 1, 1).astype(BF)

    each(3, write)


def add_kernel(left_far, right, total_far, left, total, arrive, leave):
    count = 8
    size = TILES // count
    rows = [part(i, size) for i in range(count)]
    arriving = moves([(left_far.at[span, :], left.at[span, :]) for span in rows], arrive)
    leaving = moves([(total.at[span, :], total_far.at[span, :]) for span in rows], leave)
    start(*arriving)
    for i, span in enumerate(rows):
        wait(arriving[i])
        total[span, :] = (left[span, :].astype(F32) + right[span, :].astype(F32)).astype(BF)
        start(leaving[i])
    wait(*leaving)


def sum_kernel(parts, qkv, out, up, down, qv, outb, upb, gain, shift, square):
    total = jnp.zeros((2 * ROWS, D), F32)
    for pair in range(CHIPS // 2):
        total += parts[part(pair, 2 * ROWS), :].astype(F32)
    total = total[0:ROWS] + total[ROWS:]
    for block in range(4):
        rows, lanes = slice(6 * block, 6 * block + 6), slice(DG * block, DG * block + DG)
        here, there = (slice(0, DG), slice(DG, WIDE))[:: 1 - 2 * (block % 2)]
        out[:, lanes] = total[rows, here]
        if block < 3:
            qkv[:, lanes] = total[rows, there]
        up[:, lanes] = total[rows, WIDE : WIDE + DG]
    down[...] = total[:, WIDE + DG : D]
    square[...] = jnp.zeros_like(square)
    square[0:6, :] = total[SIDE:ROWS, 0:128]
    columns = square[...].T
    for place, rows in enumerate((qv, outb, gain, shift)):
        rows[...] = columns[2 * place : 2 * place + 2, 0:6]
    lanes = (iota((128, ROWS), 0) - 8 == iota((128, ROWS), 1) % 4).astype(F32)
    grown = jnp.dot(square[0:8, :], lanes, preferred_element_type=F32, precision=lax.Precision.HIGHEST)
    grown = jnp.where(iota((8, ROWS), 1) // 4 == iota((8, ROWS), 0), grown, 0.0)
    upb[...] = jnp.sum(grown, axis=0, keepdims=True)


FAR = pl.BlockSpec(memory_space=pl.ANY)
NEAR = pl.BlockSpec(memory_space=pltpu.VMEM)


def call(kernel, shapes, scratch, name, limit, flops=0, near=(), sems=(), aliases=()):
    scratch = [pltpu.VMEM(*shape) for shape in scratch] + [pltpu.SemaphoreType.DMA((count,)) for count in sems]

    def specs(count, base):
        return [NEAR if not sems or base + i in near else FAR for i in range(count)]

    def run(*inputs):
        if sems:
            inputs = [x if i in near else pltpu.with_memory_space_constraint(x, pltpu.HBM) for i, x in enumerate(inputs)]
        return pl.pallas_call(
            kernel,
            in_specs=specs(len(inputs), 0),
            out_specs=specs(len(shapes), len(inputs)),
            out_shape=[
                pltpu.HBM(*shape) if sems and len(inputs) + i not in near else jax.ShapeDtypeStruct(*shape)
                for i, shape in enumerate(shapes)
            ],
            scratch_shapes=scratch,
            input_output_aliases=dict(aliases),
            compiler_params=pltpu.CompilerParams(vmem_limit_bytes=limit * MIB),
            cost_estimate=pl.CostEstimate(flops=flops, bytes_accessed=0, transcendentals=0),
            name=name,
        )(*inputs)

    return run


def exchange(array):
    groups = [[y * 32 + i for y in range(4) for i in range(core, 32, 2)] for core in range(2)]
    return lax.all_to_all(array, AXES, 0, 0, axis_index_groups=groups, tiled=True)


def swap(array):
    return lax.ppermute(array, "fsdp", [(i, i ^ 1) for i in range(32)])


def local(
    tokens, segment_ids, qkv_weight, out_weight, up_weight, down_weight,
    qv_bias, out_bias, up_bias, norm_gain, norm_shift, cotangent,
):
    tile, full, low, square, side = ((TILES, D), BF), ((D, TOK), F32), ((D, TOK), BF), ((D, D), BF), ((D, 128), F32)
    probs, small, packed = ((HEADS, LONG, LONG), BF), ((HEADS, 128, 128), BF), ((G, D, TOK), BF)
    units = ((F, 256), BF)
    shards = (
        qkv_weight, out_weight, up_weight, down_weight, qv_bias, out_bias, up_bias.reshape(1, ROWS),
        norm_gain, norm_shift,
    )
    gathered = call(
        pack_kernel, [tile], [*((x.shape, x.dtype) for x in shards), ((ROWS, D), F32), ((128, 128), F32), ((2 * ROWS, D), BF)],
        "pack", 12, sems=(9, CHIPS // 2),
    )(*shards)[0]
    mine = exchange(gathered)
    turn, x_t, c_t = call(
        turn_kernel, [((TOK, TOK), BF), low, low], [], "turn", 60, flops=2 * 2 * TOK * TOK * D
    )(tokens, segment_ids, cotangent)
    mine, x_t = lax.optimization_barrier((mine, x_t))
    w_qkv, result, d_sum, d_packed, keep, send = call(
        layer_kernel,
        [square, low, full, packed, tile, tile],
        [tile, tile, low, low, square, square, square, units, side, ((F, 1), F32), low, low, low, low, probs, small,
         low, full, full, ((F, TOK), BF), ((F, TOK), F32), full, full, ((F, TOK), BF), low, low, low,
         ((G, 256, TOK), BF), packed,
         square, square, square, units, side],
        "layer", 53, flops=40 * 10**9, near=(0, 2), sems=(6, 15),
    )(segment_ids, mine, pltpu.with_memory_space_constraint(swap(mine), pltpu.VMEM), x_t, c_t)
    chip = call(add_kernel, [tile], [tile, tile], "chip_sum", 20, near=(1,), sems=(8, 8))(keep, swap(send))[0]
    chip, d_packed = lax.optimization_barrier((chip, d_packed))
    parts = exchange(chip)
    grad_tokens, output = call(
        token_kernel, [((TOK, D), F32), ((TOK, D), BF)], [low, low], "token_gradient", 60,
        flops=4 * 2 * TOK * TOK * D,
    )(w_qkv, d_packed, d_sum, turn, result)
    qkv, out, up, down, qv, outb, upb, gain, shift = call(
        sum_kernel,
        [((6, QKV), F32), ((6, D), F32), ((6, D), F32), ((ROWS, DG), F32), ((2, 6), F32), ((2, 6), F32),
         ((1, ROWS), F32), ((2, 6), F32), ((2, 6), F32)],
        [((128, 128), F32)], "slice_sum", 12,
    )(parts)
    return output, grad_tokens, qkv, out, up, down, qv, outb, upb.reshape(ROWS), gain, shift


def solution(mesh):
    rows, columns, flat = P(AXES, None), P(None, AXES), P(AXES)
    in_specs = (rows, rows, rows, rows, rows, rows, columns, columns, flat, columns, columns, rows)
    out_specs = (rows, rows, rows, rows, rows, rows, columns, columns, flat, columns, columns)
    return jax.shard_map(local, mesh=mesh, in_specs=in_specs, out_specs=out_specs, check_vma=False)
```

```python
import jax
import jax.numpy as jnp
from jax import lax
from jax.experimental import pallas as pl
from jax.experimental.pallas import tpu as pltpu
from jax.sharding import PartitionSpec as P

AXES = ("dp", "fsdp")
D = 768
F = 3072
G = 4
DG = 192
QKV = 3 * DG
HEADS = 12
HEAD = 64
TOK = 512
LONG = 384
CHIPS = 64
ROWS = 24
EPS = 1e-05
BAND = 64
BANDS = D // BAND
BF = jnp.bfloat16
F32 = jnp.float32
MIB = 1 << 20

SIDE = 18
WIDE = 2 * DG
TILES = CHIPS * ROWS


def dot(left, right, over_left, over_right):
    return lax.dot_general(
        left, right, (((over_left,), (over_right,)), ((), ())), preferred_element_type=F32
    )


def iota(shape, axis):
    return lax.broadcasted_iota(jnp.int32, shape, axis)


def each(count, step):
    for i in range(count):
        step(i)


def part(i, size):
    return slice(i * size, (i + 1) * size)


def halves(chunk):
    return jnp.sum(chunk.reshape(chunk.shape[0] // 8, 8, TOK), axis=0)


def means(count, bands):
    sums = [jnp.zeros((8, TOK), F32)] * count
    for i in range(BANDS):
        sums = [kept + halves(chunk) for kept, chunk in zip(sums, bands(part(i, BAND)), strict=True)]
    return [jnp.sum(total, axis=0, keepdims=True) * (1.0 / D) for total in sums]


class Moments:
    def add(self, chunk):
        if not hasattr(self, "near"):
            self.near = jnp.mean(chunk, axis=0, keepdims=True)
            self.sums = [jnp.zeros((8, TOK), F32)] * 2
        off = chunk - self.near
        self.sums = [self.sums[0] + halves(off), self.sums[1] + halves(off * off)]

    def result(self):
        off, square = (jnp.sum(total, axis=0, keepdims=True) * (1.0 / D) for total in self.sums)
        return self.near + off, lax.rsqrt(square - off * off + EPS)


def lane_sum(chunk):
    return jnp.sum(chunk, axis=1, keepdims=True)


def pick_hidden():
    return iota((192, 128), 1) - 8 == (iota((192, 128), 0) & 3)


def arrival(core, by_device, axis):
    sorted_row = iota((192, 1) if axis == 0 else (1, 192), axis)
    if by_device:
        device = (sorted_row * 2731) >> 16
        row = sorted_row - device * ROWS
    else:
        block = (sorted_row * 1366) >> 16
        sixth = (sorted_row * 10923) >> 16
        device = sixth - block * 8
        row = block * 6 + sorted_row - sixth * 6
    return jnp.where((device & 1) == core, 0, 96) + (device >> 1) * ROWS + row


def sorter(core, by_device=False):
    return (arrival(core, by_device, 0) == iota((192, 192), 1)).astype(F32).astype(BF)


def unsorter(core, by_device=False):
    return (arrival(core, by_device, 1) == iota((192, 192), 0)).astype(F32).astype(BF)


def grower():
    return ((iota((192, 48), 0) >> 2) == iota((192, 48), 1)).astype(F32).astype(BF)


def low_lanes():
    return iota((48, 128), 1) < 64


def pack_kernel(*refs):
    far, packed, near, (tile, square, twice, arrive, leave) = refs[:9], refs[9], refs[10:19], refs[19:]
    arriving = moves(zip(far, near, strict=True), arrive)
    start(*arriving)
    wait(*arriving)
    qkv, out, up, down, qv, outb, upb, gain, shift = near
    square[...] = jnp.zeros_like(square)
    for place, rows in enumerate((qv, outb, gain, shift)):
        square[2 * place : 2 * place + 2, 0:6] = rows[...].astype(F32)
    columns = square[...].T
    grown = jnp.where(iota((8, ROWS), 1) // 4 == iota((8, ROWS), 0), upb[...].astype(F32), 0.0)
    lanes = (iota((ROWS, 128), 1) - 8 == iota((ROWS, 128), 0) % 4).astype(F32)
    hidden = jnp.dot(grown, lanes, preferred_element_type=F32)
    tile[...] = jnp.zeros_like(tile)
    for block in range(4):
        rows, lanes = slice(6 * block, 6 * block + 6), slice(DG * block, DG * block + DG)
        here, there = (slice(0, DG), slice(DG, WIDE))[:: 1 - 2 * (block % 2)]
        tile[rows, here] = out[:, lanes].astype(F32)
        if block < 3:
            tile[rows, there] = qkv[:, lanes].astype(F32)
        tile[rows, WIDE : WIDE + DG] = up[:, lanes].astype(F32)
    tile[SIDE:ROWS, 0:128] = (columns[0:8] + hidden)[0:6]
    tile[:, WIDE + DG : D] = down[...].astype(F32)
    twice[0:ROWS, :] = tile[...].astype(BF)
    twice[ROWS:, :] = tile[...].astype(BF)
    pairs = [(twice, packed.at[2 * ROWS * pair : 2 * ROWS * (pair + 1), :]) for pair in range(CHIPS // 2)]
    leaving = moves(pairs, leave)
    start(*leaving)
    wait(*leaving)


def turn_kernel(tokens, segments, cotangent, turn, x_t, c_t):
    ids = segments[...]
    count0 = jnp.sum((ids == 0).astype(jnp.int32))
    count1 = jnp.sum((ids == 1).astype(jnp.int32))
    start = jnp.where(count0 == LONG, 0, jnp.where(count1 == LONG, count0, count0 + count1))

    def turn_rows(i):
        place = iota((64, TOK), 1) + start
        place = jnp.where(place >= TOK, place - TOK, place)
        turn[part(i, 64), :] = jnp.where(iota((64, TOK), 0) + i * 64 == place, 1.0, 0.0).astype(BF)

    each(8, turn_rows)

    def turn_features(i):
        x_t[part(i, 256), :] = dot(tokens[:, part(i, 256)], turn[...], 0, 0).astype(BF)
        c_t[part(i, 256), :] = dot(cotangent[:, part(i, 256)], turn[...], 0, 0).astype(BF)

    each(3, turn_features)


def moves(pairs, sems):
    return [pltpu.make_async_copy(source, target, sems.at[i]) for i, (source, target) in enumerate(pairs)]


def start(*copies):
    for copy in copies:
        copy.start()


def wait(*copies):
    for copy in copies:
        copy.wait()


def start_behind(core, *copies):
    def body(i, nothing):
        start(*copies)
        return nothing

    lax.fori_loop(0, 1 + (core >> 1), body, 0)


def own_core():
    return lax.rem(lax.axis_index("fsdp"), 2)


SPANS = (slice(0, LONG), slice(LONG, TOK))


def layer_kernel(
    segments, mine_far, other, x_far, c_far,
    w_qkv_far, result_far, d_sum_far, packed_far, keep_far, send_far,
    mine, send, x_t, c_t, w_qkv, w_out, w_up, w_down, side, up_bias, q_t, k_t, v_t, ctx_t, probs, probs_small,
    first_low, hat, hat_two, active, slope, stream, d_first, d_upper, d_ctx, result, low_t, branch_pad, packed_t,
    g_qkv, g_out, g_up, g_down, g_side, scores, d_scores, d_few, work, arrive, leave,
):
    core = own_core()
    quarters = [slice(TILES // 4 * i, TILES // 4 * (i + 1)) for i in range(4)]
    arriving = moves(
        [(mine_far.at[rows, :], mine.at[rows, :]) for rows in quarters] + [(x_far, x_t), (c_far, c_t)],
        arrive,
    )
    leaving = moves(
        [(w_qkv, w_qkv_far), (result, result_far), (stream, d_sum_far)]
        + [(packed_t.at[g], packed_far.at[g]) for g in range(G)]
        + [
            (near.at[rows, :], far.at[rows, :])
            for rows in quarters
            for near, far in ((mine, keep_far), (send, send_far))
        ],
        leave,
    )
    start(*arriving)
    sort, sort_devices, grow = sorter(core), sorter(core, True), grower()

    def both(i, lanes):
        rows = part(i, 96)
        return jnp.concatenate([mine[rows, lanes], other[rows, lanes]], axis=0)

    def place_attention(i):
        here = part(i, 48)
        placed = jnp.dot(sort, both(i, slice(0, WIDE)), preferred_element_type=F32).astype(BF)
        blocks = [placed[48 * block : 48 * block + 48] for block in range(4)]
        for begin, target, left, right in (
            (0, w_out, 0, 1), (WIDE, w_out, 2, 3), (0, w_qkv, 1, 0), (WIDE, w_qkv, 3, 2),
        ):
            target[here, begin : begin + 128] = blocks[left][:, 0:128]
            target[here, begin + 128 : begin + 256] = jnp.where(
                low_lanes(), blocks[left][:, 128:256], blocks[right][:, 128:256]
            )
            target[here, begin + 256 : begin + 384] = blocks[right][:, 256:384]
        side[here, :] = blocks[3][:, 0:128].astype(F32)

    def place_feed(i):
        here, units = part(i, 48), part(i, 192)
        placed = jnp.dot(sort, both(i, slice(WIDE, WIDE + 256)), preferred_element_type=F32).astype(BF)
        for block in range(4):
            w_up[here, DG * block : DG * block + DG] = placed[48 * block : 48 * block + 48, 0:DG]
        rows = jnp.dot(sort_devices, both(i, slice(512, 768)), preferred_element_type=F32)
        w_down[units, :] = rows.astype(BF)
        hidden = jnp.dot(grow, side[here, :].astype(BF), preferred_element_type=F32)
        up_bias[units, :] = lane_sum(jnp.where(pick_hidden(), hidden, 0.0))

    wait(arriving[0])
    each(4, place_attention)
    wait(arriving[4])

    ids = segments[...]
    count0 = jnp.sum((ids == 0).astype(jnp.int32))
    count1 = jnp.sum((ids == 1).astype(jnp.int32))
    count2 = TOK - count0 - count1
    border = jnp.where(count0 == LONG, count1, jnp.where(count1 == LONG, count2, count0))
    together = (iota((128, 128), 0) < border) == (iota((128, 128), 1) < border)

    def project_in(g):
        rows = part(g, DG)
        packed = dot(w_qkv[rows, 0:WIDE], x_t[rows, :], 0, 0)
        k_t[rows, :] = packed[0:DG].astype(BF)
        q_t[rows, :] = ((packed[DG:WIDE] + side[rows, 0:1]).astype(BF).astype(F32) * 0.125).astype(BF)
        packed = dot(w_qkv[rows, 512:768], x_t[rows, :], 0, 0)
        v_t[rows, :] = (packed[64:256] + side[rows, 1:2]).astype(BF)

    def score(head):
        if head % 3 == 0:
            project_in(head // 3)
        rows = part(head, HEAD)
        scores[head % 2] = dot(k_t[rows, 0:LONG], q_t[rows, 0:LONG], 0, 0)

    def shares(logits):
        power = jnp.exp(logits - jnp.max(logits, axis=0, keepdims=True))
        return (power * (1.0 / jnp.sum(power, axis=0, keepdims=True))).astype(BF)

    def attend(head):
        for third in range(3):
            cols = part(third, 128)
            probs[head, :, cols] = shares(scores[head % 2, :, cols])
        rows = part(head, HEAD)
        few = dot(k_t[rows, LONG:TOK], q_t[rows, LONG:TOK], 0, 0)
        probs_small[head] = shares(jnp.where(together, few, -1000000000.0))

    def mix(head):
        rows = part(head, HEAD)
        ctx_t[rows, 0:LONG] = dot(v_t[rows, 0:LONG], probs[head], 1, 0).astype(BF)
        ctx_t[rows, LONG:TOK] = dot(v_t[rows, LONG:TOK], probs_small[head], 1, 0).astype(BF)

    meanwhile = ((4, 5), (6, 7), (8,), (9,), (10, 11), (12,), (13,), (14, 15), (), (), (), ())
    score(0)
    for head in range(HEADS):
        if head + 1 < HEADS:
            score(head + 1)
        if head > 0:
            mix(head - 1)
        attend(head)
        if head in (0, 2, 5):
            wait(arriving[(head + 4) // 3])
        each(len(meanwhile[head]), lambda i, blocks=meanwhile[head]: place_attention(blocks[i]))
    mix(HEADS - 1)

    moments_one = Moments()

    def project(i):
        rows = part(i, 128)
        attended = dot(w_out[:, rows], ctx_t[...], 0, 0) + side[rows, 2:3]
        total = x_t[rows, :].astype(F32) + attended
        stream[rows, :] = total
        moments_one.add(total)

    each(6, project)
    mean_one, scale_one = moments_one.result()

    def norm_one(i):
        rows = part(i, BAND)
        hats = (stream[rows, :] - mean_one) * scale_one
        hat[rows, :] = hats
        first = hats * side[rows, 4:5] + side[rows, 6:7]
        stream[rows, :] = first
        first_low[rows, :] = first.astype(BF)
        place_feed(i)
        if i % 3 == 2:
            place_feed(BANDS + i // 3)

    each(BANDS, norm_one)

    def raise_up(i):
        g, third = i // 3, i % 3
        rows = part(g, DG)
        work[i % 2] = dot(w_up[rows, 256 * third : 256 * third + 256], first_low[rows, :], 0, 0)

    def activate(i):
        for quarter in range(4):
            units = part(4 * i + quarter, 64)
            upper = work[i % 2, part(quarter, 64), :] + up_bias[units, :]
            below = 0.5 + 0.5 * lax.erf(upper * 0.7071067811865476)
            density = jnp.exp(-0.5 * upper * upper) * 0.3989422804014327
            active[units, :] = (upper * below).astype(BF)
            slope[units, :] = below + upper * density

    def bring_down(g):
        rows, units = part(g, DG), part(g, D)
        branch = dot(w_down[units, :], active[units, :], 0, 0)[64:256]
        total = stream[rows, :] + branch + side[rows, 3:4]
        stream[rows, :] = total
        moments_two.add(total)

    moments_two = Moments()
    raise_up(0)
    for i in range(12):
        if i + 1 < 12:
            raise_up(i + 1)
        if i % 3 == 0 and i > 0:
            bring_down(i // 3 - 1)
        activate(i)
    bring_down(3)
    wait(arriving[5])

    mean_two, scale_two = moments_two.result()

    def norm_two(rows):
        hats = (stream[rows, :] - mean_two) * scale_two
        hat_two[rows, :] = hats
        result[rows, :] = (hats * side[rows, 5:6] + side[rows, 7:8]).astype(BF)
        slopes = c_t[rows, :].astype(F32) * side[rows, 5:6]
        return slopes, slopes * hats

    lean_two, tilt_two = means(2, norm_two)
    for g in range(G):
        branch_pad[g, 0:64, :] = jnp.zeros((64, TOK), BF)

    def norm_two_back(i):
        rows = part(i, BAND)
        slopes = c_t[rows, :].astype(F32) * side[rows, 5:6]
        back = scale_two * (slopes - lean_two - hat_two[rows, :] * tilt_two)
        stream[rows, :] = back
        branch_pad[i // 3, 64 + BAND * (i % 3) : 128 + BAND * (i % 3), :] = back.astype(BF)

    each(BANDS, norm_two_back)

    def raise_back(i):
        work[i % 2] = dot(w_down[part(i, 256), :], branch_pad[i // 3], 1, 0)

    def activate_back(i):
        for quarter in range(4):
            units = part(4 * i + quarter, 64)
            d_upper[units, :] = (work[i % 2, part(quarter, 64), :] * slope[units, :]).astype(BF)

    def bring_back(g):
        rows = part(g, DG)
        slopes = stream[rows, :] + dot(w_up[rows, :], d_upper[part(g, D), :], 1, 0)
        d_first[rows, :] = slopes
        slopes = slopes * side[rows, 4:5]
        sums_one[:] = [sums_one[0] + halves(slopes), sums_one[1] + halves(slopes * hat[rows, :])]

    sums_one = [jnp.zeros((8, TOK), F32)] * 2
    raise_back(0)
    for i in range(12):
        if i + 1 < 12:
            raise_back(i + 1)
        if i % 3 == 0 and i > 0:
            bring_back(i // 3 - 1)
        activate_back(i)
    bring_back(3)

    lean_one, tilt_one = (jnp.sum(total, axis=0, keepdims=True) * (1.0 / D) for total in sums_one)

    def norm_one_back(i):
        rows, units = part(i, BAND), part(i, 256)
        back = scale_one * (d_first[rows, :] * side[rows, 4:5] - lean_one - hat[rows, :] * tilt_one)
        stream[rows, :] = back
        low_t[rows, :] = back.astype(BF)
        span = slice(256 * (i % 3), 256 * (i % 3) + 256)
        g_up[part(i // 3, DG), span] = dot(first_low[part(i // 3, DG), :], d_upper[units, :], 1, 1).astype(BF)
        g_down[units, :] = dot(active[units, :], branch_pad[i // 3], 1, 1).astype(BF)

    each(BANDS, norm_one_back)
    start_behind(core, *leaving[0:3])

    def project_back(i):
        rows = part(i, 128)
        d_ctx[rows, :] = dot(w_out[rows, :], low_t[...], 1, 0).astype(BF)
        g_out[rows, :] = dot(ctx_t[rows, :], low_t[...], 1, 1).astype(BF)

    each(6, project_back)

    unsort, unsort_devices = unsorter(core), unsorter(core, True)

    def side_sums(i):
        rows = part(i, BAND)
        g_side[rows, :] = jnp.zeros((BAND, 128), F32)
        slopes = c_t[rows, :].astype(F32)
        g_side[rows, 5:6] = lane_sum(slopes * hat_two[rows, :])
        g_side[rows, 7:8] = lane_sum(slopes)
        slopes = d_first[rows, :]
        g_side[rows, 4:5] = lane_sum(slopes * hat[rows, :])
        g_side[rows, 6:7] = lane_sum(slopes)
        g_side[rows, 2:3] = lane_sum(low_t[rows, :].astype(F32))
        branch = branch_pad[i // 3, 64 + BAND * (i % 3) : 128 + BAND * (i % 3), :]
        g_side[rows, 3:4] = lane_sum(branch.astype(F32))
        units = part(i, 256)
        up_bias[units, :] = lane_sum(d_upper[units, :].astype(F32))

    def tile_feed(i):
        here, units, rows = part(i, 48), part(i, 192), part(i, 96)
        zero = jnp.zeros((48, 64), BF)
        ups = [jnp.concatenate([g_up[here, DG * block : DG * block + DG], zero], axis=1) for block in range(4)]
        placed = dot(unsort, jnp.concatenate(ups, axis=0), 1, 0)
        downs = dot(unsort_devices, g_down[units, :], 1, 0)
        for target, begin in ((mine, 0), (send, 96)):
            span = slice(begin, begin + 96)
            target[rows, 384:512] = placed[span, 0:128].astype(BF)
            target[rows, 512:640] = (placed[span, 128:256] + downs[span, 0:128]).astype(BF)
            target[rows, 640:768] = downs[span, 128:256].astype(BF)

    def score_back(head):
        rows = part(head, HEAD)
        scores[head % 2] = dot(v_t[rows, 0:LONG], d_ctx[rows, 0:LONG], 0, 0)

    def shares_back(share, d_share):
        return (share * (d_share - jnp.sum(d_share * share, axis=0, keepdims=True))).astype(BF)

    def attend_back(head):
        rows = part(head, HEAD)
        for third in range(3):
            cols = part(third, 128)
            d_scores[head % 2, :, cols] = shares_back(probs[head, :, cols].astype(F32), scores[head % 2, :, cols])
        few = dot(v_t[rows, LONG:TOK], d_ctx[rows, LONG:TOK], 0, 0)
        d_few[head % 2] = shares_back(probs_small[head].astype(F32), few)

    def mix_back(head):
        rows = part(head, HEAD)
        g, at = head // 3, HEAD * (head % 3)
        for cols, share, d_score in (
            (slice(0, LONG), probs[head], d_scores[head % 2]),
            (slice(LONG, TOK), probs_small[head], d_few[head % 2]),
        ):
            packed_t[g, 3 * DG + at : 3 * DG + at + HEAD, cols] = dot(d_ctx[rows, cols], share, 1, 1).astype(BF)
            packed_t[g, DG + at : DG + at + HEAD, cols] = (0.125 * dot(k_t[rows, cols], d_score, 1, 0)).astype(BF)
            packed_t[g, at : at + HEAD, cols] = dot(q_t[rows, cols], d_score, 1, 1).astype(BF)
        side_sums(head)
        tile_feed(head)

    def project_in_back(g):
        rows = part(g, DG)
        packed_t[g, WIDE : 3 * DG, :] = jnp.zeros((DG, TOK), BF)
        g_qkv[rows, 0:WIDE] = dot(x_t[rows, :], packed_t[g, 0:WIDE, :], 1, 1).astype(BF)
        g_qkv[rows, 512:768] = dot(x_t[rows, :], packed_t[g, 512:768, :], 1, 1).astype(BF)
        g_side[rows, 0:1] = lane_sum(packed_t[g, DG:WIDE, :].astype(F32))
        g_side[rows, 1:2] = lane_sum(packed_t[g, 3 * DG :, :].astype(F32))
        tile_feed(12 + g)

    def tile_attention(i):
        here, units, rows = part(i, 48), part(i, 192), part(i, 96)
        hidden = jnp.where(pick_hidden(), up_bias[units, :], 0.0).astype(BF)
        bias = (g_side[here, :] + dot(grow, hidden, 0, 0)).astype(BF)
        blocks = []
        for begin in (0, WIDE):
            mixed_out, mixed_qkv = g_out[here, begin + 128 : begin + 256], g_qkv[here, begin + 128 : begin + 256]
            for odd in range(2):
                first = (g_qkv[here, 0:128] if begin == 0 else bias) if odd else g_out[here, begin : begin + 128]
                left, right = (mixed_qkv, mixed_out) if odd else (mixed_out, mixed_qkv)
                last = (g_out if odd else g_qkv)[here, begin + 256 : begin + 384]
                blocks.append(jnp.concatenate([first, jnp.where(low_lanes(), left, right), last], axis=1))
        placed = dot(unsort, jnp.concatenate(blocks, axis=0), 1, 0).astype(BF)
        mine[rows, 0:WIDE] = placed[0:96]
        send[rows, 0:WIDE] = placed[96:192]

    score_back(0)
    for head in range(HEADS):
        if head + 1 < HEADS:
            score_back(head + 1)
        if head > 0:
            mix_back(head - 1)
            if head % 3 == 0:
                project_in_back(head // 3 - 1)
        attend_back(head)
        if head > 2:
            block = (head // 3 - 1) * 4 + head % 3
            tile_attention(block)
            if head % 3 == 2:
                tile_attention(block + 1)
        if head == 7:
            start_behind(core, *leaving[3:5], *leaving[7:9])
    mix_back(HEADS - 1)
    project_in_back(G - 1)
    start_behind(core, *leaving[5:7], *leaving[9:13])
    each(4, lambda i: tile_attention(12 + i))
    start_behind(core, *leaving[13:15])
    wait(*leaving)


def token_kernel(w_qkv, packed_t, d_sum, turn, result, grad_tokens, output, high, low):
    def total(g):
        rows = part(g, DG)
        back = dot(w_qkv[rows, 0:WIDE], packed_t[g, 0:WIDE, :], 1, 0)
        whole = d_sum[rows, :] + back + dot(w_qkv[rows, 512:768], packed_t[g, 512:768, :], 1, 0)
        high[rows, :] = whole.astype(BF)
        low[rows, :] = (whole - high[rows, :].astype(F32)).astype(BF)

    each(G, total)

    def write(i):
        rows = part(i, 256)
        grad_tokens[:, rows] = dot(turn[...], high[rows, :], 1, 1) + dot(turn[...], low[rows, :], 1, 1)
        output[:, rows] = dot(turn[...], result[rows, :], 1, 1).astype(BF)

    each(3, write)


def add_kernel(left_far, right, total_far, left, total, arrive, leave):
    count = 8
    size = TILES // count
    rows = [part(i, size) for i in range(count)]
    arriving = moves([(left_far.at[span, :], left.at[span, :]) for span in rows], arrive)
    leaving = moves([(total.at[span, :], total_far.at[span, :]) for span in rows], leave)
    start(*arriving)
    for i, span in enumerate(rows):
        wait(arriving[i])
        total[span, :] = (left[span, :].astype(F32) + right[span, :].astype(F32)).astype(BF)
        start(leaving[i])
    wait(*leaving)


def sum_kernel(parts, qkv, out, up, down, qv, outb, upb, gain, shift, square):
    total = jnp.zeros((2 * ROWS, D), F32)
    for pair in range(CHIPS // 2):
        total += parts[part(pair, 2 * ROWS), :].astype(F32)
    total = total[0:ROWS] + total[ROWS:]
    for block in range(4):
        rows, lanes = slice(6 * block, 6 * block + 6), slice(DG * block, DG * block + DG)
        here, there = (slice(0, DG), slice(DG, WIDE))[:: 1 - 2 * (block % 2)]
        out[:, lanes] = total[rows, here]
        if block < 3:
            qkv[:, lanes] = total[rows, there]
        up[:, lanes] = total[rows, WIDE : WIDE + DG]
    down[...] = total[:, WIDE + DG : D]
    square[...] = jnp.zeros_like(square)
    square[0:6, :] = total[SIDE:ROWS, 0:128]
    columns = square[...].T
    for place, rows in enumerate((qv, outb, gain, shift)):
        rows[...] = columns[2 * place : 2 * place + 2, 0:6]
    lanes = (iota((128, ROWS), 0) - 8 == iota((128, ROWS), 1) % 4).astype(F32)
    grown = jnp.dot(square[0:8, :], lanes, preferred_element_type=F32, precision=lax.Precision.HIGHEST)
    grown = jnp.where(iota((8, ROWS), 1) // 4 == iota((8, ROWS), 0), grown, 0.0)
    upb[...] = jnp.sum(grown, axis=0, keepdims=True)


FAR = pl.BlockSpec(memory_space=pl.ANY)
NEAR = pl.BlockSpec(memory_space=pltpu.VMEM)


def call(kernel, shapes, scratch, name, limit, flops=0, near=(), sems=(), aliases=()):
    scratch = [pltpu.VMEM(*shape) for shape in scratch] + [pltpu.SemaphoreType.DMA((count,)) for count in sems]

    def specs(count, base):
        return [NEAR if not sems or base + i in near else FAR for i in range(count)]

    def run(*inputs):
        if sems:
            inputs = [x if i in near else pltpu.with_memory_space_constraint(x, pltpu.HBM) for i, x in enumerate(inputs)]
        return pl.pallas_call(
            kernel,
            in_specs=specs(len(inputs), 0),
            out_specs=specs(len(shapes), len(inputs)),
            out_shape=[
                pltpu.HBM(*shape) if sems and len(inputs) + i not in near else jax.ShapeDtypeStruct(*shape)
                for i, shape in enumerate(shapes)
            ],
            scratch_shapes=scratch,
            input_output_aliases=dict(aliases),
            compiler_params=pltpu.CompilerParams(vmem_limit_bytes=limit * MIB),
            cost_estimate=pl.CostEstimate(flops=flops, bytes_accessed=0, transcendentals=0),
            name=name,
        )(*inputs)

    return run


def exchange(array):
    groups = [[y * 32 + i for y in range(4) for i in range(core, 32, 2)] for core in range(2)]
    return lax.all_to_all(array, AXES, 0, 0, axis_index_groups=groups, tiled=True)


def swap(array):
    return lax.ppermute(array, "fsdp", [(i, i ^ 1) for i in range(32)])


def local(
    tokens, segment_ids, qkv_weight, out_weight, up_weight, down_weight,
    qv_bias, out_bias, up_bias, norm_gain, norm_shift, cotangent,
):
    tile, full, low, square, side = ((TILES, D), BF), ((D, TOK), F32), ((D, TOK), BF), ((D, D), BF), ((D, 128), F32)
    probs, small, packed = ((HEADS, LONG, LONG), BF), ((HEADS, 128, 128), BF), ((G, D, TOK), BF)
    units = ((F, 256), BF)
    shards = (
        qkv_weight, out_weight, up_weight, down_weight, qv_bias, out_bias, up_bias.reshape(1, ROWS),
        norm_gain, norm_shift,
    )
    gathered = call(
        pack_kernel, [tile], [*((x.shape, x.dtype) for x in shards), ((ROWS, D), F32), ((128, 128), F32), ((2 * ROWS, D), BF)],
        "pack", 12, sems=(9, CHIPS // 2),
    )(*shards)[0]
    mine = exchange(gathered)
    turn, x_t, c_t = call(
        turn_kernel, [((TOK, TOK), BF), low, low], [], "turn", 60, flops=2 * 2 * TOK * TOK * D
    )(tokens, segment_ids, cotangent)
    mine, x_t = lax.optimization_barrier((mine, x_t))
    w_qkv, result, d_sum, d_packed, keep, send = call(
        layer_kernel,
        [square, low, full, packed, tile, tile],
        [tile, tile, low, low, square, square, square, units, side, ((F, 1), F32), low, low, low, low, probs, small,
         low, full, full, ((F, TOK), BF), ((F, TOK), F32), full, full, ((F, TOK), BF), low, low, low,
         ((G, 256, TOK), BF), packed,
         square, square, square, units, side, ((2, LONG, LONG), F32), ((2, LONG, LONG), BF),
         ((2, 128, 128), BF), ((2, 256, TOK), F32)],
        "layer", 56, flops=40 * 10**9, near=(0, 2), sems=(6, 15),
    )(segment_ids, mine, pltpu.with_memory_space_constraint(swap(mine), pltpu.VMEM), x_t, c_t)
    chip = call(add_kernel, [tile], [tile, tile], "chip_sum", 20, near=(1,), sems=(8, 8))(keep, swap(send))[0]
    chip, d_packed = lax.optimization_barrier((chip, d_packed))
    parts = exchange(chip)
    grad_tokens, output = call(
        token_kernel, [((TOK, D), F32), ((TOK, D), BF)], [low, low], "token_gradient", 60,
        flops=4 * 2 * TOK * TOK * D,
    )(w_qkv, d_packed, d_sum, turn, result)
    qkv, out, up, down, qv, outb, upb, gain, shift = call(
        sum_kernel,
        [((6, QKV), F32), ((6, D), F32), ((6, D), F32), ((ROWS, DG), F32), ((2, 6), F32), ((2, 6), F32),
         ((1, ROWS), F32), ((2, 6), F32), ((2, 6), F32)],
        [((128, 128), F32)], "slice_sum", 12,
    )(parts)
    return output, grad_tokens, qkv, out, up, down, qv, outb, upb.reshape(ROWS), gain, shift


def solution(mesh):
    rows, columns, flat = P(AXES, None), P(None, AXES), P(AXES)
    in_specs = (rows, rows, rows, rows, rows, rows, columns, columns, flat, columns, columns, rows)
    out_specs = (rows, rows, rows, rows, rows, rows, columns, columns, flat, columns, columns)
    return jax.shard_map(local, mesh=mesh, in_specs=in_specs, out_specs=out_specs, check_vma=False)
```

```python
import jax
import jax.numpy as jnp
from jax import lax
from jax.experimental import pallas as pl
from jax.experimental.pallas import tpu as pltpu
from jax.sharding import PartitionSpec as P

AXES = ("dp", "fsdp")
D = 768
F = 3072
G = 4
DG = 192
QKV = 3 * DG
HEADS = 12
HEAD = 64
TOK = 512
LONG = 384
CHIPS = 64
ROWS = 24
EPS = 1e-05
BAND = 64
BANDS = D // BAND
BF = jnp.bfloat16
F32 = jnp.float32
MIB = 1 << 20

SIDE = 18
WIDE = 2 * DG
TILES = CHIPS * ROWS


def dot(left, right, over_left, over_right):
    return lax.dot_general(
        left, right, (((over_left,), (over_right,)), ((), ())), preferred_element_type=F32
    )


def iota(shape, axis):
    return lax.broadcasted_iota(jnp.int32, shape, axis)


def each(count, step):
    for i in range(count):
        step(i)


def part(i, size):
    return slice(i * size, (i + 1) * size)


def halves(chunk):
    return jnp.sum(chunk.reshape(chunk.shape[0] // 8, 8, TOK), axis=0)


def means(count, bands):
    sums = [jnp.zeros((8, TOK), F32)] * count
    for i in range(BANDS):
        sums = [kept + halves(chunk) for kept, chunk in zip(sums, bands(part(i, BAND)), strict=True)]
    return [jnp.sum(total, axis=0, keepdims=True) * (1.0 / D) for total in sums]


class Moments:
    def add(self, chunk):
        if not hasattr(self, "near"):
            self.near = jnp.mean(chunk, axis=0, keepdims=True)
            self.sums = [jnp.zeros((8, TOK), F32)] * 2
        off = chunk - self.near
        self.sums = [self.sums[0] + halves(off), self.sums[1] + halves(off * off)]

    def result(self):
        off, square = (jnp.sum(total, axis=0, keepdims=True) * (1.0 / D) for total in self.sums)
        return self.near + off, lax.rsqrt(square - off * off + EPS)


def lane_sum(chunk):
    return jnp.sum(chunk, axis=1, keepdims=True)


def pick_hidden():
    return iota((192, 128), 1) - 8 == (iota((192, 128), 0) & 3)


def arrival(core, by_device, axis):
    sorted_row = iota((192, 1) if axis == 0 else (1, 192), axis)
    if by_device:
        device = (sorted_row * 2731) >> 16
        row = sorted_row - device * ROWS
    else:
        block = (sorted_row * 1366) >> 16
        sixth = (sorted_row * 10923) >> 16
        device = sixth - block * 8
        row = block * 6 + sorted_row - sixth * 6
    return jnp.where((device & 1) == core, 0, 96) + (device >> 1) * ROWS + row


def sorter(core, by_device=False):
    return (arrival(core, by_device, 0) == iota((192, 192), 1)).astype(F32).astype(BF)


def unsorter(core, by_device=False):
    return (arrival(core, by_device, 1) == iota((192, 192), 0)).astype(F32).astype(BF)


def grower():
    return ((iota((192, 48), 0) >> 2) == iota((192, 48), 1)).astype(F32).astype(BF)


def low_lanes():
    return iota((48, 128), 1) < 64


def pack_kernel(*refs):
    far, packed, near, (tile, square, twice, arrive, leave) = refs[:9], refs[9], refs[10:19], refs[19:]
    arriving = moves(zip(far, near, strict=True), arrive)
    start(*arriving)
    wait(*arriving)
    qkv, out, up, down, qv, outb, upb, gain, shift = near
    square[...] = jnp.zeros_like(square)
    for place, rows in enumerate((qv, outb, gain, shift)):
        square[2 * place : 2 * place + 2, 0:6] = rows[...].astype(F32)
    columns = square[...].T
    grown = jnp.where(iota((8, ROWS), 1) // 4 == iota((8, ROWS), 0), upb[...].astype(F32), 0.0)
    lanes = (iota((ROWS, 128), 1) - 8 == iota((ROWS, 128), 0) % 4).astype(F32)
    hidden = jnp.dot(grown, lanes, preferred_element_type=F32)
    tile[...] = jnp.zeros_like(tile)
    for block in range(4):
        rows, lanes = slice(6 * block, 6 * block + 6), slice(DG * block, DG * block + DG)
        here, there = (slice(0, DG), slice(DG, WIDE))[:: 1 - 2 * (block % 2)]
        tile[rows, here] = out[:, lanes].astype(F32)
        if block < 3:
            tile[rows, there] = qkv[:, lanes].astype(F32)
        tile[rows, WIDE : WIDE + DG] = up[:, lanes].astype(F32)
    tile[SIDE:ROWS, 0:128] = (columns[0:8] + hidden)[0:6]
    tile[:, WIDE + DG : D] = down[...].astype(F32)
    twice[0:ROWS, :] = tile[...].astype(BF)
    twice[ROWS:, :] = tile[...].astype(BF)
    pairs = [(twice, packed.at[2 * ROWS * pair : 2 * ROWS * (pair + 1), :]) for pair in range(CHIPS // 2)]
    leaving = moves(pairs, leave)
    start(*leaving)
    wait(*leaving)


def turn_kernel(tokens, segments, cotangent, turn, x_t, c_t):
    ids = segments[...]
    count0 = jnp.sum((ids == 0).astype(jnp.int32))
    count1 = jnp.sum((ids == 1).astype(jnp.int32))
    start = jnp.where(count0 == LONG, 0, jnp.where(count1 == LONG, count0, count0 + count1))

    def turn_rows(i):
        place = iota((64, TOK), 1) + start
        place = jnp.where(place >= TOK, place - TOK, place)
        turn[part(i, 64), :] = jnp.where(iota((64, TOK), 0) + i * 64 == place, 1.0, 0.0).astype(BF)

    each(8, turn_rows)

    def turn_features(i):
        x_t[part(i, 256), :] = dot(tokens[:, part(i, 256)], turn[...], 0, 0).astype(BF)
        c_t[part(i, 256), :] = dot(cotangent[:, part(i, 256)], turn[...], 0, 0).astype(BF)

    each(3, turn_features)


def moves(pairs, sems):
    return [pltpu.make_async_copy(source, target, sems.at[i]) for i, (source, target) in enumerate(pairs)]


def start(*copies):
    for copy in copies:
        copy.start()


def wait(*copies):
    for copy in copies:
        copy.wait()


def start_behind(core, *copies):
    def body(i, nothing):
        start(*copies)
        return nothing

    lax.fori_loop(0, 1 + (core >> 1), body, 0)


def own_core():
    return lax.rem(lax.axis_index("fsdp"), 2)


SPANS = (slice(0, LONG), slice(LONG, TOK))


def layer_kernel(
    segments, mine_far, other, x_far, c_far,
    w_qkv_far, result_far, d_sum_far, packed_far, keep, send,
    mine, x_t, c_t, w_qkv, w_out, w_up, w_down, side, up_bias, q_t, k_t, v_t, ctx_t, probs, probs_small,
    first_low, hat, hat_two, active, slope, stream, d_first, d_upper, d_ctx, result, low_t, branch_pad, packed_t,
    g_qkv, g_out, g_up, g_down, g_side, scores, d_scores, d_few, work, arrive, leave,
):
    core = own_core()
    quarters = [slice(TILES // 4 * i, TILES // 4 * (i + 1)) for i in range(4)]
    arriving = moves(
        [(mine_far.at[rows, :], mine.at[rows, :]) for rows in quarters] + [(x_far, x_t), (c_far, c_t)],
        arrive,
    )
    leaving = moves(
        [(w_qkv, w_qkv_far), (result, result_far), (stream, d_sum_far)]
        + [(packed_t.at[g], packed_far.at[g]) for g in range(G)],
        leave,
    )
    start(*arriving)
    sort, sort_devices, grow = sorter(core), sorter(core, True), grower()

    def both(i, lanes):
        rows = part(i, 96)
        return jnp.concatenate([mine[rows, lanes], other[rows, lanes]], axis=0)

    def place_attention(i):
        here = part(i, 48)
        placed = jnp.dot(sort, both(i, slice(0, WIDE)), preferred_element_type=F32).astype(BF)
        blocks = [placed[48 * block : 48 * block + 48] for block in range(4)]
        for begin, target, left, right in (
            (0, w_out, 0, 1), (WIDE, w_out, 2, 3), (0, w_qkv, 1, 0), (WIDE, w_qkv, 3, 2),
        ):
            target[here, begin : begin + 128] = blocks[left][:, 0:128]
            target[here, begin + 128 : begin + 256] = jnp.where(
                low_lanes(), blocks[left][:, 128:256], blocks[right][:, 128:256]
            )
            target[here, begin + 256 : begin + 384] = blocks[right][:, 256:384]
        side[here, :] = blocks[3][:, 0:128].astype(F32)

    def place_feed(i):
        here, units = part(i, 48), part(i, 192)
        placed = jnp.dot(sort, both(i, slice(WIDE, WIDE + 256)), preferred_element_type=F32).astype(BF)
        for block in range(4):
            w_up[here, DG * block : DG * block + DG] = placed[48 * block : 48 * block + 48, 0:DG]
        rows = jnp.dot(sort_devices, both(i, slice(512, 768)), preferred_element_type=F32)
        w_down[units, :] = rows.astype(BF)
        hidden = jnp.dot(grow, side[here, :].astype(BF), preferred_element_type=F32)
        up_bias[units, :] = lane_sum(jnp.where(pick_hidden(), hidden, 0.0))

    wait(arriving[0])
    each(4, place_attention)
    wait(arriving[4])

    ids = segments[...]
    count0 = jnp.sum((ids == 0).astype(jnp.int32))
    count1 = jnp.sum((ids == 1).astype(jnp.int32))
    count2 = TOK - count0 - count1
    border = jnp.where(count0 == LONG, count1, jnp.where(count1 == LONG, count2, count0))
    together = (iota((128, 128), 0) < border) == (iota((128, 128), 1) < border)

    def project_in(g):
        rows = part(g, DG)
        packed = dot(w_qkv[rows, 0:WIDE], x_t[rows, :], 0, 0)
        k_t[rows, :] = packed[0:DG].astype(BF)
        q_t[rows, :] = ((packed[DG:WIDE] + side[rows, 0:1]).astype(BF).astype(F32) * 0.125).astype(BF)
        packed = dot(w_qkv[rows, 512:768], x_t[rows, :], 0, 0)
        v_t[rows, :] = (packed[64:256] + side[rows, 1:2]).astype(BF)

    def score(head):
        if head % 3 == 0:
            project_in(head // 3)
        rows = part(head, HEAD)
        scores[head % 2] = dot(k_t[rows, 0:LONG], q_t[rows, 0:LONG], 0, 0)

    def shares(logits):
        power = jnp.exp(logits - jnp.max(logits, axis=0, keepdims=True))
        return (power * (1.0 / jnp.sum(power, axis=0, keepdims=True))).astype(BF)

    def attend(head):
        for third in range(3):
            cols = part(third, 128)
            probs[head, :, cols] = shares(scores[head % 2, :, cols])
        rows = part(head, HEAD)
        few = dot(k_t[rows, LONG:TOK], q_t[rows, LONG:TOK], 0, 0)
        probs_small[head] = shares(jnp.where(together, few, -1000000000.0))

    def mix(head):
        rows = part(head, HEAD)
        ctx_t[rows, 0:LONG] = dot(v_t[rows, 0:LONG], probs[head], 1, 0).astype(BF)
        ctx_t[rows, LONG:TOK] = dot(v_t[rows, LONG:TOK], probs_small[head], 1, 0).astype(BF)

    meanwhile = ((4, 5), (6, 7), (8,), (9,), (10, 11), (12,), (13,), (14, 15), (), (), (), ())
    score(0)
    for head in range(HEADS):
        if head > 0:
            mix(head - 1)
        attend(head)
        if head + 1 < HEADS:
            score(head + 1)
        if head in (0, 2, 5):
            wait(arriving[(head + 4) // 3])
        if head >= 8:
            each(4, lambda i, head=head: place_feed(4 * (head - 8) + i))
        each(len(meanwhile[head]), lambda i, blocks=meanwhile[head]: place_attention(blocks[i]))
    mix(HEADS - 1)

    moments_one = Moments()

    def project(i):
        rows = part(i, 128)
        attended = dot(w_out[:, rows], ctx_t[...], 0, 0) + side[rows, 2:3]
        total = x_t[rows, :].astype(F32) + attended
        stream[rows, :] = total
        moments_one.add(total)

    each(6, project)
    mean_one, scale_one = moments_one.result()

    def norm_one(i):
        rows = part(i, BAND)
        hats = (stream[rows, :] - mean_one) * scale_one
        hat[rows, :] = hats
        first = hats * side[rows, 4:5] + side[rows, 6:7]
        stream[rows, :] = first
        first_low[rows, :] = first.astype(BF)

    each(BANDS, norm_one)

    def raise_up(i):
        g, third = i // 3, i % 3
        rows = part(g, DG)
        work[i % 2] = dot(w_up[rows, 256 * third : 256 * third + 256], first_low[rows, :], 0, 0)

    def activate(i):
        for quarter in range(4):
            units = part(4 * i + quarter, 64)
            upper = work[i % 2, part(quarter, 64), :] + up_bias[units, :]
            below = 0.5 + 0.5 * lax.erf(upper * 0.7071067811865476)
            density = jnp.exp(-0.5 * upper * upper) * 0.3989422804014327
            active[units, :] = (upper * below).astype(BF)
            slope[units, :] = below + upper * density

    def bring_down(g):
        rows, units = part(g, DG), part(g, D)
        branch = dot(w_down[units, :], active[units, :], 0, 0)[64:256]
        total = stream[rows, :] + branch + side[rows, 3:4]
        stream[rows, :] = total
        moments_two.add(total)

    moments_two = Moments()
    raise_up(0)
    for i in range(12):
        if i + 1 < 12:
            raise_up(i + 1)
        if i % 3 == 0 and i > 0:
            bring_down(i // 3 - 1)
        activate(i)
    bring_down(3)
    wait(arriving[5])

    mean_two, scale_two = moments_two.result()

    def norm_two(rows):
        hats = (stream[rows, :] - mean_two) * scale_two
        hat_two[rows, :] = hats
        result[rows, :] = (hats * side[rows, 5:6] + side[rows, 7:8]).astype(BF)
        slopes = c_t[rows, :].astype(F32) * side[rows, 5:6]
        return slopes, slopes * hats

    lean_two, tilt_two = means(2, norm_two)
    for g in range(G):
        branch_pad[g, 0:64, :] = jnp.zeros((64, TOK), BF)

    def norm_two_back(i):
        rows = part(i, BAND)
        slopes = c_t[rows, :].astype(F32) * side[rows, 5:6]
        back = scale_two * (slopes - lean_two - hat_two[rows, :] * tilt_two)
        stream[rows, :] = back
        branch_pad[i // 3, 64 + BAND * (i % 3) : 128 + BAND * (i % 3), :] = back.astype(BF)

    each(BANDS, norm_two_back)

    def raise_back(i):
        work[i % 2] = dot(w_down[part(i, 256), :], branch_pad[i // 3], 1, 0)

    def activate_back(i):
        for quarter in range(4):
            units = part(4 * i + quarter, 64)
            d_upper[units, :] = (work[i % 2, part(quarter, 64), :] * slope[units, :]).astype(BF)

    def bring_back(g):
        rows = part(g, DG)
        slopes = stream[rows, :] + dot(w_up[rows, :], d_upper[part(g, D), :], 1, 0)
        d_first[rows, :] = slopes
        slopes = slopes * side[rows, 4:5]
        sums_one[:] = [sums_one[0] + halves(slopes), sums_one[1] + halves(slopes * hat[rows, :])]

    sums_one = [jnp.zeros((8, TOK), F32)] * 2
    raise_back(0)
    for i in range(12):
        if i + 1 < 12:
            raise_back(i + 1)
        if i % 3 == 0 and i > 0:
            bring_back(i // 3 - 1)
        activate_back(i)
    bring_back(3)

    lean_one, tilt_one = (jnp.sum(total, axis=0, keepdims=True) * (1.0 / D) for total in sums_one)

    def norm_one_back(i):
        rows, units = part(i, BAND), part(i, 256)
        back = scale_one * (d_first[rows, :] * side[rows, 4:5] - lean_one - hat[rows, :] * tilt_one)
        stream[rows, :] = back
        low_t[rows, :] = back.astype(BF)
        span = slice(256 * (i % 3), 256 * (i % 3) + 256)
        g_up[part(i // 3, DG), span] = dot(first_low[part(i // 3, DG), :], d_upper[units, :], 1, 1).astype(BF)
        g_down[units, :] = dot(active[units, :], branch_pad[i // 3], 1, 1).astype(BF)

    each(BANDS, norm_one_back)
    start_behind(core, *leaving[0:3])

    def project_back(i):
        rows = part(i, 128)
        d_ctx[rows, :] = dot(w_out[rows, :], low_t[...], 1, 0).astype(BF)
        g_out[rows, :] = dot(ctx_t[rows, :], low_t[...], 1, 1).astype(BF)

    each(6, project_back)

    unsort, unsort_devices = unsorter(core), unsorter(core, True)

    def side_sums(i):
        rows = part(i, BAND)
        g_side[rows, :] = jnp.zeros((BAND, 128), F32)
        slopes = c_t[rows, :].astype(F32)
        g_side[rows, 5:6] = lane_sum(slopes * hat_two[rows, :])
        g_side[rows, 7:8] = lane_sum(slopes)
        slopes = d_first[rows, :]
        g_side[rows, 4:5] = lane_sum(slopes * hat[rows, :])
        g_side[rows, 6:7] = lane_sum(slopes)
        g_side[rows, 2:3] = lane_sum(low_t[rows, :].astype(F32))
        branch = branch_pad[i // 3, 64 + BAND * (i % 3) : 128 + BAND * (i % 3), :]
        g_side[rows, 3:4] = lane_sum(branch.astype(F32))
        units = part(i, 256)
        up_bias[units, :] = lane_sum(d_upper[units, :].astype(F32))

    def tile_feed(i):
        here, units, rows = part(i, 48), part(i, 192), part(i, 96)
        zero = jnp.zeros((48, 64), BF)
        ups = [jnp.concatenate([g_up[here, DG * block : DG * block + DG], zero], axis=1) for block in range(4)]
        placed = dot(unsort, jnp.concatenate(ups, axis=0), 1, 0)
        downs = dot(unsort_devices, g_down[units, :], 1, 0)
        for target, begin in ((keep, 0), (send, 96)):
            span = slice(begin, begin + 96)
            target[rows, 384:512] = placed[span, 0:128].astype(BF)
            target[rows, 512:640] = (placed[span, 128:256] + downs[span, 0:128]).astype(BF)
            target[rows, 640:768] = downs[span, 128:256].astype(BF)

    def score_back(head):
        rows = part(head, HEAD)
        scores[head % 2] = dot(v_t[rows, 0:LONG], d_ctx[rows, 0:LONG], 0, 0)

    def shares_back(share, d_share):
        return (share * (d_share - jnp.sum(d_share * share, axis=0, keepdims=True))).astype(BF)

    def attend_back(head):
        rows = part(head, HEAD)
        for third in range(3):
            cols = part(third, 128)
            d_scores[head % 2, :, cols] = shares_back(probs[head, :, cols].astype(F32), scores[head % 2, :, cols])
        few = dot(v_t[rows, LONG:TOK], d_ctx[rows, LONG:TOK], 0, 0)
        d_few[head % 2] = shares_back(probs_small[head].astype(F32), few)

    def mix_back(head):
        rows = part(head, HEAD)
        g, at = head // 3, HEAD * (head % 3)
        for cols, share, d_score in (
            (slice(0, LONG), probs[head], d_scores[head % 2]),
            (slice(LONG, TOK), probs_small[head], d_few[head % 2]),
        ):
            packed_t[g, 3 * DG + at : 3 * DG + at + HEAD, cols] = dot(d_ctx[rows, cols], share, 1, 1).astype(BF)
            packed_t[g, DG + at : DG + at + HEAD, cols] = (0.125 * dot(k_t[rows, cols], d_score, 1, 0)).astype(BF)
            packed_t[g, at : at + HEAD, cols] = dot(q_t[rows, cols], d_score, 1, 1).astype(BF)
        side_sums(head)
        tile_feed(head)

    def project_in_back(g):
        rows = part(g, DG)
        packed_t[g, WIDE : 3 * DG, :] = jnp.zeros((DG, TOK), BF)
        g_qkv[rows, 0:WIDE] = dot(x_t[rows, :], packed_t[g, 0:WIDE, :], 1, 1).astype(BF)
        g_qkv[rows, 512:768] = dot(x_t[rows, :], packed_t[g, 512:768, :], 1, 1).astype(BF)
        g_side[rows, 0:1] = lane_sum(packed_t[g, DG:WIDE, :].astype(F32))
        g_side[rows, 1:2] = lane_sum(packed_t[g, 3 * DG :, :].astype(F32))
        tile_feed(12 + g)

    def tile_attention(i):
        here, units, rows = part(i, 48), part(i, 192), part(i, 96)
        hidden = jnp.where(pick_hidden(), up_bias[units, :], 0.0).astype(BF)
        bias = (g_side[here, :] + dot(grow, hidden, 0, 0)).astype(BF)
        blocks = []
        for begin in (0, WIDE):
            mixed_out, mixed_qkv = g_out[here, begin + 128 : begin + 256], g_qkv[here, begin + 128 : begin + 256]
            for odd in range(2):
                first = (g_qkv[here, 0:128] if begin == 0 else bias) if odd else g_out[here, begin : begin + 128]
                left, right = (mixed_qkv, mixed_out) if odd else (mixed_out, mixed_qkv)
                last = (g_out if odd else g_qkv)[here, begin + 256 : begin + 384]
                blocks.append(jnp.concatenate([first, jnp.where(low_lanes(), left, right), last], axis=1))
        placed = dot(unsort, jnp.concatenate(blocks, axis=0), 1, 0).astype(BF)
        keep[rows, 0:WIDE] = placed[0:96]
        send[rows, 0:WIDE] = placed[96:192]

    score_back(0)
    for head in range(HEADS):
        if head + 1 < HEADS:
            score_back(head + 1)
        if head > 0:
            mix_back(head - 1)
            if head % 3 == 0:
                project_in_back(head // 3 - 1)
        attend_back(head)
        if head > 2:
            block = (head // 3 - 1) * 4 + head % 3
            tile_attention(block)
            if head % 3 == 2:
                tile_attention(block + 1)
        if head == 7:
            start_behind(core, *leaving[3:5])
    mix_back(HEADS - 1)
    project_in_back(G - 1)
    start_behind(core, *leaving[5:7])
    each(4, lambda i: tile_attention(12 + i))
    wait(*leaving)


def token_kernel(w_qkv, packed_t, d_sum, turn, result, grad_tokens, output, high, low):
    def total(g):
        rows = part(g, DG)
        back = dot(w_qkv[rows, 0:WIDE], packed_t[g, 0:WIDE, :], 1, 0)
        whole = d_sum[rows, :] + back + dot(w_qkv[rows, 512:768], packed_t[g, 512:768, :], 1, 0)
        high[rows, :] = whole.astype(BF)
        low[rows, :] = (whole - high[rows, :].astype(F32)).astype(BF)

    each(G, total)

    def write(i):
        rows = part(i, 256)
        grad_tokens[:, rows] = dot(turn[...], high[rows, :], 1, 1) + dot(turn[...], low[rows, :], 1, 1)
        output[:, rows] = dot(turn[...], result[rows, :], 1, 1).astype(BF)

    each(3, write)


def add_kernel(left, right, total_far, total, leave):
    rows = [part(i, TILES // 4) for i in range(4)]
    leaving = moves([(total.at[span, :], total_far.at[span, :]) for span in rows], leave)
    for i, span in enumerate(rows):
        total[span, :] = (left[span, :].astype(F32) + right[span, :].astype(F32)).astype(BF)
        start_behind(own_core(), leaving[i])
    wait(*leaving)


def sum_kernel(parts, qkv, out, up, down, qv, outb, upb, gain, shift, square):
    total = jnp.zeros((2 * ROWS, D), F32)
    for pair in range(CHIPS // 2):
        total += parts[part(pair, 2 * ROWS), :].astype(F32)
    total = total[0:ROWS] + total[ROWS:]
    for block in range(4):
        rows, lanes = slice(6 * block, 6 * block + 6), slice(DG * block, DG * block + DG)
        here, there = (slice(0, DG), slice(DG, WIDE))[:: 1 - 2 * (block % 2)]
        out[:, lanes] = total[rows, here]
        if block < 3:
            qkv[:, lanes] = total[rows, there]
        up[:, lanes] = total[rows, WIDE : WIDE + DG]
    down[...] = total[:, WIDE + DG : D]
    square[...] = jnp.zeros_like(square)
    square[0:6, :] = total[SIDE:ROWS, 0:128]
    columns = square[...].T
    for place, rows in enumerate((qv, outb, gain, shift)):
        rows[...] = columns[2 * place : 2 * place + 2, 0:6]
    lanes = (iota((128, ROWS), 0) - 8 == iota((128, ROWS), 1) % 4).astype(F32)
    grown = jnp.dot(square[0:8, :], lanes, preferred_element_type=F32, precision=lax.Precision.HIGHEST)
    grown = jnp.where(iota((8, ROWS), 1) // 4 == iota((8, ROWS), 0), grown, 0.0)
    upb[...] = jnp.sum(grown, axis=0, keepdims=True)


FAR = pl.BlockSpec(memory_space=pl.ANY)
NEAR = pl.BlockSpec(memory_space=pltpu.VMEM)


def call(kernel, shapes, scratch, name, limit, flops=0, near=(), held=(), sems=()):
    scratch = [pltpu.VMEM(*shape) for shape in scratch] + [pltpu.SemaphoreType.DMA((count,)) for count in sems]

    def specs(count, base):
        return [NEAR if not sems or base + i in near else FAR for i in range(count)]

    def run(*inputs):
        if sems:
            inputs = [x if i in near else pltpu.with_memory_space_constraint(x, pltpu.HBM) for i, x in enumerate(inputs)]
        return pl.pallas_call(
            kernel,
            in_specs=specs(len(inputs), 0),
            out_specs=specs(len(shapes), len(inputs)),
            out_shape=[
                (pltpu.VMEM if len(inputs) + i in held else pltpu.HBM)(*shape)
                if sems and (len(inputs) + i in held or len(inputs) + i not in near)
                else jax.ShapeDtypeStruct(*shape)
                for i, shape in enumerate(shapes)
            ],
            scratch_shapes=scratch,
            compiler_params=pltpu.CompilerParams(vmem_limit_bytes=limit * MIB),
            cost_estimate=pl.CostEstimate(flops=flops, bytes_accessed=0, transcendentals=0),
            name=name,
        )(*inputs)

    return run


def exchange(array):
    groups = [[y * 32 + i for y in range(4) for i in range(core, 32, 2)] for core in range(2)]
    return lax.all_to_all(array, AXES, 0, 0, axis_index_groups=groups, tiled=True)


def swap(array):
    return lax.ppermute(array, "fsdp", [(i, i ^ 1) for i in range(32)])


def local(
    tokens, segment_ids, qkv_weight, out_weight, up_weight, down_weight,
    qv_bias, out_bias, up_bias, norm_gain, norm_shift, cotangent,
):
    tile, full, low, square, side = ((TILES, D), BF), ((D, TOK), F32), ((D, TOK), BF), ((D, D), BF), ((D, 128), F32)
    probs, small, packed = ((HEADS, LONG, LONG), BF), ((HEADS, 128, 128), BF), ((G, D, TOK), BF)
    units = ((F, 256), BF)
    shards = (
        qkv_weight, out_weight, up_weight, down_weight, qv_bias, out_bias, up_bias.reshape(1, ROWS),
        norm_gain, norm_shift,
    )
    gathered = call(
        pack_kernel, [tile], [*((x.shape, x.dtype) for x in shards), ((ROWS, D), F32), ((128, 128), F32), ((2 * ROWS, D), BF)],
        "pack", 12, sems=(9, CHIPS // 2),
    )(*shards)[0]
    mine = exchange(gathered)
    turn, x_t, c_t = call(
        turn_kernel, [((TOK, TOK), BF), low, low], [], "turn", 60, flops=2 * 2 * TOK * TOK * D
    )(tokens, segment_ids, cotangent)
    mine, x_t = lax.optimization_barrier((mine, x_t))
    w_qkv, result, d_sum, d_packed, keep, send = call(
        layer_kernel,
        [square, low, full, packed, tile, tile],
        [tile, low, low, square, square, square, units, side, ((F, 1), F32), low, low, low, low, probs, small,
         low, full, full, ((F, TOK), BF), ((F, TOK), F32), full, full, ((F, TOK), BF), low, low, low,
         ((G, 256, TOK), BF), packed,
         square, square, square, units, side, ((2, LONG, LONG), F32), ((2, LONG, LONG), BF),
         ((2, 128, 128), BF), ((2, 256, TOK), F32)],
        "layer", 53, flops=40 * 10**9, near=(0, 2, 9, 10), held=(9, 10), sems=(6, 7),
    )(segment_ids, mine, pltpu.with_memory_space_constraint(swap(mine), pltpu.VMEM), x_t, c_t)
    chip = call(add_kernel, [tile], [tile], "chip_sum", 20, near=(0, 1), sems=(4,))(keep, swap(send))[0]
    chip, d_packed = lax.optimization_barrier((chip, d_packed))
    parts = exchange(chip)
    grad_tokens, output = call(
        token_kernel, [((TOK, D), F32), ((TOK, D), BF)], [low, low], "token_gradient", 60,
        flops=4 * 2 * TOK * TOK * D,
    )(w_qkv, d_packed, d_sum, turn, result)
    qkv, out, up, down, qv, outb, upb, gain, shift = call(
        sum_kernel,
        [((6, QKV), F32), ((6, D), F32), ((6, D), F32), ((ROWS, DG), F32), ((2, 6), F32), ((2, 6), F32),
         ((1, ROWS), F32), ((2, 6), F32), ((2, 6), F32)],
        [((128, 128), F32)], "slice_sum", 12,
    )(parts)
    return output, grad_tokens, qkv, out, up, down, qv, outb, upb.reshape(ROWS), gain, shift


def solution(mesh):
    rows, columns, flat = P(AXES, None), P(None, AXES), P(AXES)
    in_specs = (rows, rows, rows, rows, rows, rows, columns, columns, flat, columns, columns, rows)
    out_specs = (rows, rows, rows, rows, rows, rows, columns, columns, flat, columns, columns)
    return jax.shard_map(local, mesh=mesh, in_specs=in_specs, out_specs=out_specs, check_vma=False)
```

```python
import jax
import jax.numpy as jnp
from jax import lax
from jax.experimental import pallas as pl
from jax.experimental.pallas import tpu as pltpu
from jax.sharding import PartitionSpec as P

AXES = ("dp", "fsdp")
D = 768
F = 3072
G = 4
DG = 192
QKV = 3 * DG
HEADS = 12
HEAD = 64
TOK = 512
LONG = 384
CHIPS = 64
ROWS = 24
EPS = 1e-05
BAND = 64
BANDS = D // BAND
BF = jnp.bfloat16
F32 = jnp.float32
MIB = 1 << 20

SIDE = 18
WIDE = 2 * DG
TILES = CHIPS * ROWS


def dot(left, right, over_left, over_right):
    return lax.dot_general(
        left, right, (((over_left,), (over_right,)), ((), ())), preferred_element_type=F32
    )


def iota(shape, axis):
    return lax.broadcasted_iota(jnp.int32, shape, axis)


def each(count, step):
    for i in range(count):
        step(i)


def part(i, size):
    return slice(i * size, (i + 1) * size)


def halves(chunk):
    return jnp.sum(chunk.reshape(chunk.shape[0] // 8, 8, TOK), axis=0)


def means(count, bands):
    sums = [jnp.zeros((8, TOK), F32)] * count
    for i in range(BANDS):
        sums = [kept + halves(chunk) for kept, chunk in zip(sums, bands(part(i, BAND)), strict=True)]
    return [jnp.sum(total, axis=0, keepdims=True) * (1.0 / D) for total in sums]


class Moments:
    def add(self, chunk):
        if not hasattr(self, "near"):
            self.near = jnp.mean(chunk, axis=0, keepdims=True)
            self.sums = [jnp.zeros((8, TOK), F32)] * 2
        off = chunk - self.near
        self.sums = [self.sums[0] + halves(off), self.sums[1] + halves(off * off)]

    def result(self):
        off, square = (jnp.sum(total, axis=0, keepdims=True) * (1.0 / D) for total in self.sums)
        return self.near + off, lax.rsqrt(square - off * off + EPS)


def lane_sum(chunk):
    return jnp.sum(chunk, axis=1, keepdims=True)


def pick_hidden():
    return iota((192, 128), 1) - 8 == (iota((192, 128), 0) & 3)


def arrival(core, by_device, axis):
    sorted_row = iota((192, 1) if axis == 0 else (1, 192), axis)
    if by_device:
        device = (sorted_row * 2731) >> 16
        row = sorted_row - device * ROWS
    else:
        block = (sorted_row * 1366) >> 16
        sixth = (sorted_row * 10923) >> 16
        device = sixth - block * 8
        row = block * 6 + sorted_row - sixth * 6
    return jnp.where((device & 1) == core, 0, 96) + (device >> 1) * ROWS + row


def sorter(core, by_device=False):
    return (arrival(core, by_device, 0) == iota((192, 192), 1)).astype(F32).astype(BF)


def unsorter(core, by_device=False):
    return (arrival(core, by_device, 1) == iota((192, 192), 0)).astype(F32).astype(BF)


def grower():
    return ((iota((192, 48), 0) >> 2) == iota((192, 48), 1)).astype(F32).astype(BF)


def low_lanes():
    return iota((48, 128), 1) < 64


def pack_kernel(*refs):
    far, packed, near, (tile, square, twice, arrive, leave) = refs[:9], refs[9], refs[10:19], refs[19:]
    arriving = moves(zip(far, near, strict=True), arrive)
    start(*arriving)
    wait(*arriving)
    qkv, out, up, down, qv, outb, upb, gain, shift = near
    square[...] = jnp.zeros_like(square)
    for place, rows in enumerate((qv, outb, gain, shift)):
        square[2 * place : 2 * place + 2, 0:6] = rows[...].astype(F32)
    columns = square[...].T
    grown = jnp.where(iota((8, ROWS), 1) // 4 == iota((8, ROWS), 0), upb[...].astype(F32), 0.0)
    lanes = (iota((ROWS, 128), 1) - 8 == iota((ROWS, 128), 0) % 4).astype(F32)
    hidden = jnp.dot(grown, lanes, preferred_element_type=F32)
    tile[...] = jnp.zeros_like(tile)
    for block in range(4):
        rows, lanes = slice(6 * block, 6 * block + 6), slice(DG * block, DG * block + DG)
        here, there = (slice(0, DG), slice(DG, WIDE))[:: 1 - 2 * (block % 2)]
        tile[rows, here] = out[:, lanes].astype(F32)
        if block < 3:
            tile[rows, there] = qkv[:, lanes].astype(F32)
        tile[rows, WIDE : WIDE + DG] = up[:, lanes].astype(F32)
    tile[SIDE:ROWS, 0:128] = (columns[0:8] + hidden)[0:6]
    tile[:, WIDE + DG : D] = down[...].astype(F32)
    twice[0:ROWS, :] = tile[...].astype(BF)
    twice[ROWS:, :] = tile[...].astype(BF)
    pairs = [(twice, packed.at[2 * ROWS * pair : 2 * ROWS * (pair + 1), :]) for pair in range(CHIPS // 2)]
    leaving = moves(pairs, leave)
    start_behind(own_core(), *leaving)
    wait(*leaving)


def turn_kernel(tokens, segments, cotangent, turn, x_t, c_t):
    ids = segments[...]
    count0 = jnp.sum((ids == 0).astype(jnp.int32))
    count1 = jnp.sum((ids == 1).astype(jnp.int32))
    start = jnp.where(count0 == LONG, 0, jnp.where(count1 == LONG, count0, count0 + count1))

    def turn_rows(i):
        place = iota((64, TOK), 1) + start
        place = jnp.where(place >= TOK, place - TOK, place)
        turn[part(i, 64), :] = jnp.where(iota((64, TOK), 0) + i * 64 == place, 1.0, 0.0).astype(BF)

    each(8, turn_rows)

    def turn_features(i):
        x_t[part(i, 256), :] = dot(tokens[:, part(i, 256)], turn[...], 0, 0).astype(BF)
        c_t[part(i, 256), :] = dot(cotangent[:, part(i, 256)], turn[...], 0, 0).astype(BF)

    each(3, turn_features)


def moves(pairs, sems):
    return [pltpu.make_async_copy(source, target, sems.at[i]) for i, (source, target) in enumerate(pairs)]


def start(*copies):
    for copy in copies:
        copy.start()


def wait(*copies):
    for copy in copies:
        copy.wait()


def start_behind(core, *copies):
    def body(i, nothing):
        start(*copies)
        return nothing

    lax.fori_loop(0, 1 + (core >> 1), body, 0)


def own_core():
    return lax.rem(lax.axis_index("fsdp"), 2)


SPANS = (slice(0, LONG), slice(LONG, TOK))


def layer_kernel(
    segments, mine_far, other, x_far, c_far,
    w_qkv_far, result_far, d_sum_far, packed_far, keep, send,
    mine, x_t, c_t, w_qkv, w_out, w_up, w_down, side, up_bias, q_t, k_t, v_t, ctx_t, probs, probs_small,
    first_low, hat, hat_two, active, slope, stream, d_first, d_upper, d_ctx, result, low_t, branch_pad, packed_t,
    g_qkv, g_out, g_up, g_down, g_side, scores, d_scores, d_few, work, arrive, leave,
):
    core = own_core()
    quarters = [slice(TILES // 4 * i, TILES // 4 * (i + 1)) for i in range(4)]
    arriving = moves(
        [(mine_far.at[rows, :], mine.at[rows, :]) for rows in quarters] + [(x_far, x_t), (c_far, c_t)],
        arrive,
    )
    leaving = moves(
        [(w_qkv, w_qkv_far), (result, result_far), (stream, d_sum_far)]
        + [(packed_t.at[g], packed_far.at[g]) for g in range(G)],
        leave,
    )
    start(*arriving)
    sort, sort_devices, grow = sorter(core), sorter(core, True), grower()

    def both(i, lanes):
        rows = part(i, 96)
        return jnp.concatenate([mine[rows, lanes], other[rows, lanes]], axis=0)

    def place_attention(i):
        here = part(i, 48)
        placed = jnp.dot(sort, both(i, slice(0, WIDE)), preferred_element_type=F32).astype(BF)
        blocks = [placed[48 * block : 48 * block + 48] for block in range(4)]
        for begin, target, left, right in (
            (0, w_out, 0, 1), (WIDE, w_out, 2, 3), (0, w_qkv, 1, 0), (WIDE, w_qkv, 3, 2),
        ):
            target[here, begin : begin + 128] = blocks[left][:, 0:128]
            target[here, begin + 128 : begin + 256] = jnp.where(
                low_lanes(), blocks[left][:, 128:256], blocks[right][:, 128:256]
            )
            target[here, begin + 256 : begin + 384] = blocks[right][:, 256:384]
        side[here, :] = blocks[3][:, 0:128].astype(F32)

    def place_feed(i):
        here, units = part(i, 48), part(i, 192)
        placed = jnp.dot(sort, both(i, slice(WIDE, WIDE + 256)), preferred_element_type=F32).astype(BF)
        for block in range(4):
            w_up[here, DG * block : DG * block + DG] = placed[48 * block : 48 * block + 48, 0:DG]
        rows = jnp.dot(sort_devices, both(i, slice(512, 768)), preferred_element_type=F32)
        w_down[units, :] = rows.astype(BF)
        hidden = jnp.dot(grow, side[here, :].astype(BF), preferred_element_type=F32)
        up_bias[units, :] = lane_sum(jnp.where(pick_hidden(), hidden, 0.0))

    wait(arriving[0])
    each(4, place_attention)
    wait(arriving[4])

    ids = segments[...]
    count0 = jnp.sum((ids == 0).astype(jnp.int32))
    count1 = jnp.sum((ids == 1).astype(jnp.int32))
    count2 = TOK - count0 - count1
    border = jnp.where(count0 == LONG, count1, jnp.where(count1 == LONG, count2, count0))
    together = (iota((128, 128), 0) < border) == (iota((128, 128), 1) < border)

    def project_in(g):
        rows = part(g, DG)
        packed = dot(w_qkv[rows, 0:WIDE], x_t[rows, :], 0, 0)
        k_t[rows, :] = packed[0:DG].astype(BF)
        q_t[rows, :] = ((packed[DG:WIDE] + side[rows, 0:1]).astype(BF).astype(F32) * 0.125).astype(BF)
        packed = dot(w_qkv[rows, 512:768], x_t[rows, :], 0, 0)
        v_t[rows, :] = (packed[64:256] + side[rows, 1:2]).astype(BF)

    def score(head):
        if head % 3 == 0:
            project_in(head // 3)
        rows = part(head, HEAD)
        scores[head % 2] = dot(k_t[rows, 0:LONG], q_t[rows, 0:LONG], 0, 0)

    def shares(logits):
        power = jnp.exp(logits - jnp.max(logits, axis=0, keepdims=True))
        return (power * (1.0 / jnp.sum(power, axis=0, keepdims=True))).astype(BF)

    def attend(head):
        for third in range(3):
            cols = part(third, 128)
            probs[head, :, cols] = shares(scores[head % 2, :, cols])
        rows = part(head, HEAD)
        few = dot(k_t[rows, LONG:TOK], q_t[rows, LONG:TOK], 0, 0)
        probs_small[head] = shares(jnp.where(together, few, -1000000000.0))

    def mix(head):
        rows = part(head, HEAD)
        ctx_t[rows, 0:LONG] = dot(v_t[rows, 0:LONG], probs[head], 1, 0).astype(BF)
        ctx_t[rows, LONG:TOK] = dot(v_t[rows, LONG:TOK], probs_small[head], 1, 0).astype(BF)

    meanwhile = ((4, 5), (6, 7), (8,), (9,), (10, 11), (12,), (13,), (14, 15), (), (), (), ())
    score(0)
    for head in range(HEADS):
        if head > 0:
            mix(head - 1)
        attend(head)
        if head + 1 < HEADS:
            score(head + 1)
        if head in (0, 2, 5):
            wait(arriving[(head + 4) // 3])
        if head >= 8:
            each(4, lambda i, head=head: place_feed(4 * (head - 8) + i))
        each(len(meanwhile[head]), lambda i, blocks=meanwhile[head]: place_attention(blocks[i]))
    mix(HEADS - 1)

    moments_one = Moments()

    def project(i):
        rows = part(i, 128)
        attended = dot(w_out[:, rows], ctx_t[...], 0, 0) + side[rows, 2:3]
        total = x_t[rows, :].astype(F32) + attended
        stream[rows, :] = total
        moments_one.add(total)

    each(6, project)
    mean_one, scale_one = moments_one.result()

    def norm_one(i):
        rows = part(i, BAND)
        hats = (stream[rows, :] - mean_one) * scale_one
        hat[rows, :] = hats
        first = hats * side[rows, 4:5] + side[rows, 6:7]
        stream[rows, :] = first
        first_low[rows, :] = first.astype(BF)

    each(BANDS, norm_one)

    def raise_up(i):
        g, third = i // 3, i % 3
        rows = part(g, DG)
        work[i % 2] = dot(w_up[rows, 256 * third : 256 * third + 256], first_low[rows, :], 0, 0)

    def activate(i):
        for quarter in range(4):
            units = part(4 * i + quarter, 64)
            upper = work[i % 2, part(quarter, 64), :] + up_bias[units, :]
            below = 0.5 + 0.5 * lax.erf(upper * 0.7071067811865476)
            density = jnp.exp(-0.5 * upper * upper) * 0.3989422804014327
            active[units, :] = (upper * below).astype(BF)
            slope[units, :] = below + upper * density

    def bring_down(g):
        rows, units = part(g, DG), part(g, D)
        branch = dot(w_down[units, :], active[units, :], 0, 0)[64:256]
        total = stream[rows, :] + branch + side[rows, 3:4]
        stream[rows, :] = total
        moments_two.add(total)

    moments_two = Moments()
    raise_up(0)
    for i in range(12):
        if i + 1 < 12:
            raise_up(i + 1)
        if i % 3 == 0 and i > 0:
            bring_down(i // 3 - 1)
        activate(i)
    bring_down(3)
    wait(arriving[5])

    mean_two, scale_two = moments_two.result()

    def norm_two(rows):
        hats = (stream[rows, :] - mean_two) * scale_two
        hat_two[rows, :] = hats
        result[rows, :] = (hats * side[rows, 5:6] + side[rows, 7:8]).astype(BF)
        slopes = c_t[rows, :].astype(F32) * side[rows, 5:6]
        return slopes, slopes * hats

    lean_two, tilt_two = means(2, norm_two)
    for g in range(G):
        branch_pad[g, 0:64, :] = jnp.zeros((64, TOK), BF)

    def norm_two_back(i):
        rows = part(i, BAND)
        slopes = c_t[rows, :].astype(F32) * side[rows, 5:6]
        back = scale_two * (slopes - lean_two - hat_two[rows, :] * tilt_two)
        stream[rows, :] = back
        branch_pad[i // 3, 64 + BAND * (i % 3) : 128 + BAND * (i % 3), :] = back.astype(BF)

    each(BANDS, norm_two_back)

    def raise_back(i):
        work[i % 2] = dot(w_down[part(i, 256), :], branch_pad[i // 3], 1, 0)

    def activate_back(i):
        for quarter in range(4):
            units = part(4 * i + quarter, 64)
            d_upper[units, :] = (work[i % 2, part(quarter, 64), :] * slope[units, :]).astype(BF)

    def bring_back(g):
        rows = part(g, DG)
        slopes = stream[rows, :] + dot(w_up[rows, :], d_upper[part(g, D), :], 1, 0)
        d_first[rows, :] = slopes
        slopes = slopes * side[rows, 4:5]
        sums_one[:] = [sums_one[0] + halves(slopes), sums_one[1] + halves(slopes * hat[rows, :])]

    sums_one = [jnp.zeros((8, TOK), F32)] * 2
    raise_back(0)
    for i in range(12):
        if i + 1 < 12:
            raise_back(i + 1)
        if i % 3 == 0 and i > 0:
            bring_back(i // 3 - 1)
        activate_back(i)
    bring_back(3)

    lean_one, tilt_one = (jnp.sum(total, axis=0, keepdims=True) * (1.0 / D) for total in sums_one)

    def norm_one_back(i):
        rows, units = part(i, BAND), part(i, 256)
        back = scale_one * (d_first[rows, :] * side[rows, 4:5] - lean_one - hat[rows, :] * tilt_one)
        stream[rows, :] = back
        low_t[rows, :] = back.astype(BF)
        span = slice(256 * (i % 3), 256 * (i % 3) + 256)
        g_up[part(i // 3, DG), span] = dot(first_low[part(i // 3, DG), :], d_upper[units, :], 1, 1).astype(BF)
        g_down[units, :] = dot(active[units, :], branch_pad[i // 3], 1, 1).astype(BF)

    each(BANDS, norm_one_back)
    start_behind(core, *leaving[0:3])

    def project_back(i):
        rows = part(i, 128)
        d_ctx[rows, :] = dot(w_out[rows, :], low_t[...], 1, 0).astype(BF)

    def out_gradient(i):
        rows = part(i, 128)
        g_out[rows, :] = dot(ctx_t[rows, :], low_t[...], 1, 1).astype(BF)

    each(6, project_back)

    unsort, unsort_devices = unsorter(core), unsorter(core, True)

    def side_sums(i):
        rows = part(i, BAND)
        g_side[rows, :] = jnp.zeros((BAND, 128), F32)
        slopes = c_t[rows, :].astype(F32)
        g_side[rows, 5:6] = lane_sum(slopes * hat_two[rows, :])
        g_side[rows, 7:8] = lane_sum(slopes)
        slopes = d_first[rows, :]
        g_side[rows, 4:5] = lane_sum(slopes * hat[rows, :])
        g_side[rows, 6:7] = lane_sum(slopes)
        g_side[rows, 2:3] = lane_sum(low_t[rows, :].astype(F32))
        branch = branch_pad[i // 3, 64 + BAND * (i % 3) : 128 + BAND * (i % 3), :]
        g_side[rows, 3:4] = lane_sum(branch.astype(F32))
        units = part(i, 256)
        up_bias[units, :] = lane_sum(d_upper[units, :].astype(F32))

    def tile_feed(i):
        here, units, rows = part(i, 48), part(i, 192), part(i, 96)
        zero = jnp.zeros((48, 64), BF)
        ups = [jnp.concatenate([g_up[here, DG * block : DG * block + DG], zero], axis=1) for block in range(4)]
        placed = dot(unsort, jnp.concatenate(ups, axis=0), 1, 0)
        downs = dot(unsort_devices, g_down[units, :], 1, 0)
        for target, begin in ((keep, 0), (send, 96)):
            span = slice(begin, begin + 96)
            target[rows, 384:512] = placed[span, 0:128].astype(BF)
            target[rows, 512:640] = (placed[span, 128:256] + downs[span, 0:128]).astype(BF)
            target[rows, 640:768] = downs[span, 128:256].astype(BF)

    def score_back(head):
        rows = part(head, HEAD)
        scores[head % 2] = dot(v_t[rows, 0:LONG], d_ctx[rows, 0:LONG], 0, 0)

    def shares_back(share, d_share):
        return (share * (d_share - jnp.sum(d_share * share, axis=0, keepdims=True))).astype(BF)

    def attend_back(head):
        rows = part(head, HEAD)
        for third in range(3):
            cols = part(third, 128)
            d_scores[head % 2, :, cols] = shares_back(probs[head, :, cols].astype(F32), scores[head % 2, :, cols])
        few = dot(v_t[rows, LONG:TOK], d_ctx[rows, LONG:TOK], 0, 0)
        d_few[head % 2] = shares_back(probs_small[head].astype(F32), few)

    def mix_back(head):
        rows = part(head, HEAD)
        g, at = head // 3, HEAD * (head % 3)
        for cols, share, d_score in (
            (slice(0, LONG), probs[head], d_scores[head % 2]),
            (slice(LONG, TOK), probs_small[head], d_few[head % 2]),
        ):
            packed_t[g, 3 * DG + at : 3 * DG + at + HEAD, cols] = dot(d_ctx[rows, cols], share, 1, 1).astype(BF)
            packed_t[g, DG + at : DG + at + HEAD, cols] = (0.125 * dot(k_t[rows, cols], d_score, 1, 0)).astype(BF)
            packed_t[g, at : at + HEAD, cols] = dot(q_t[rows, cols], d_score, 1, 1).astype(BF)
        side_sums(head)
        tile_feed(head)

    def project_in_back(g):
        rows = part(g, DG)
        packed_t[g, WIDE : 3 * DG, :] = jnp.zeros((DG, TOK), BF)
        g_qkv[rows, 0:WIDE] = dot(x_t[rows, :], packed_t[g, 0:WIDE, :], 1, 1).astype(BF)
        g_qkv[rows, 512:768] = dot(x_t[rows, :], packed_t[g, 512:768, :], 1, 1).astype(BF)
        g_side[rows, 0:1] = lane_sum(packed_t[g, DG:WIDE, :].astype(F32))
        g_side[rows, 1:2] = lane_sum(packed_t[g, 3 * DG :, :].astype(F32))
        tile_feed(12 + g)

    def tile_attention(i):
        here, units, rows = part(i, 48), part(i, 192), part(i, 96)
        hidden = jnp.where(pick_hidden(), up_bias[units, :], 0.0).astype(BF)
        bias = (g_side[here, :] + dot(grow, hidden, 0, 0)).astype(BF)
        blocks = []
        for begin in (0, WIDE):
            mixed_out, mixed_qkv = g_out[here, begin + 128 : begin + 256], g_qkv[here, begin + 128 : begin + 256]
            for odd in range(2):
                first = (g_qkv[here, 0:128] if begin == 0 else bias) if odd else g_out[here, begin : begin + 128]
                left, right = (mixed_qkv, mixed_out) if odd else (mixed_out, mixed_qkv)
                last = (g_out if odd else g_qkv)[here, begin + 256 : begin + 384]
                blocks.append(jnp.concatenate([first, jnp.where(low_lanes(), left, right), last], axis=1))
        placed = dot(unsort, jnp.concatenate(blocks, axis=0), 1, 0).astype(BF)
        keep[rows, 0:WIDE] = placed[0:96]
        send[rows, 0:WIDE] = placed[96:192]

    score_back(0)
    for head in range(HEADS):
        if head + 1 < HEADS:
            score_back(head + 1)
        if head > 0:
            mix_back(head - 1)
            if head % 3 == 0:
                project_in_back(head // 3 - 1)
        attend_back(head)
        if head < 3:
            each(2, lambda i, head=head: out_gradient(2 * head + i))
        if head > 2:
            block = (head // 3 - 1) * 4 + head % 3
            tile_attention(block)
            if head % 3 == 2:
                tile_attention(block + 1)
        if head == 7:
            start_behind(core, *leaving[3:5])
    mix_back(HEADS - 1)
    project_in_back(G - 1)
    start_behind(core, *leaving[5:7])
    each(4, lambda i: tile_attention(12 + i))
    wait(*leaving)


def token_kernel(w_qkv, packed_t, d_sum, turn, result, grad_tokens, output, high, low):
    def total(g):
        rows = part(g, DG)
        back = dot(w_qkv[rows, 0:WIDE], packed_t[g, 0:WIDE, :], 1, 0)
        whole = d_sum[rows, :] + back + dot(w_qkv[rows, 512:768], packed_t[g, 512:768, :], 1, 0)
        high[rows, :] = whole.astype(BF)
        low[rows, :] = (whole - high[rows, :].astype(F32)).astype(BF)

    each(G, total)

    def write(i):
        rows = part(i, 256)
        grad_tokens[:, rows] = dot(turn[...], high[rows, :], 1, 1) + dot(turn[...], low[rows, :], 1, 1)
        output[:, rows] = dot(turn[...], result[rows, :], 1, 1).astype(BF)

    each(3, write)


def add_kernel(left, right, total_far, total, leave):
    rows = [part(i, TILES // 4) for i in range(4)]
    leaving = moves([(total.at[span, :], total_far.at[span, :]) for span in rows], leave)
    for i, span in enumerate(rows):
        total[span, :] = (left[span, :].astype(F32) + right[span, :].astype(F32)).astype(BF)
        start_behind(own_core(), leaving[i])
    wait(*leaving)


def sum_kernel(parts, qkv, out, up, down, qv, outb, upb, gain, shift, square):
    total = jnp.zeros((2 * ROWS, D), F32)
    for pair in range(CHIPS // 2):
        total += parts[part(pair, 2 * ROWS), :].astype(F32)
    total = total[0:ROWS] + total[ROWS:]
    for block in range(4):
        rows, lanes = slice(6 * block, 6 * block + 6), slice(DG * block, DG * block + DG)
        here, there = (slice(0, DG), slice(DG, WIDE))[:: 1 - 2 * (block % 2)]
        out[:, lanes] = total[rows, here]
        if block < 3:
            qkv[:, lanes] = total[rows, there]
        up[:, lanes] = total[rows, WIDE : WIDE + DG]
    down[...] = total[:, WIDE + DG : D]
    square[...] = jnp.zeros_like(square)
    square[0:6, :] = total[SIDE:ROWS, 0:128]
    columns = square[...].T
    for place, rows in enumerate((qv, outb, gain, shift)):
        rows[...] = columns[2 * place : 2 * place + 2, 0:6]
    lanes = (iota((128, ROWS), 0) - 8 == iota((128, ROWS), 1) % 4).astype(F32)
    grown = jnp.dot(square[0:8, :], lanes, preferred_element_type=F32, precision=lax.Precision.HIGHEST)
    grown = jnp.where(iota((8, ROWS), 1) // 4 == iota((8, ROWS), 0), grown, 0.0)
    upb[...] = jnp.sum(grown, axis=0, keepdims=True)


FAR = pl.BlockSpec(memory_space=pl.ANY)
NEAR = pl.BlockSpec(memory_space=pltpu.VMEM)


def call(kernel, shapes, scratch, name, limit, flops=0, near=(), held=(), sems=()):
    scratch = [pltpu.VMEM(*shape) for shape in scratch] + [pltpu.SemaphoreType.DMA((count,)) for count in sems]

    def specs(count, base):
        return [NEAR if not sems or base + i in near else FAR for i in range(count)]

    def run(*inputs):
        if sems:
            inputs = [x if i in near else pltpu.with_memory_space_constraint(x, pltpu.HBM) for i, x in enumerate(inputs)]
        return pl.pallas_call(
            kernel,
            in_specs=specs(len(inputs), 0),
            out_specs=specs(len(shapes), len(inputs)),
            out_shape=[
                (pltpu.VMEM if len(inputs) + i in held else pltpu.HBM)(*shape)
                if sems and (len(inputs) + i in held or len(inputs) + i not in near)
                else jax.ShapeDtypeStruct(*shape)
                for i, shape in enumerate(shapes)
            ],
            scratch_shapes=scratch,
            compiler_params=pltpu.CompilerParams(vmem_limit_bytes=limit * MIB),
            cost_estimate=pl.CostEstimate(flops=flops, bytes_accessed=0, transcendentals=0),
            name=name,
        )(*inputs)

    return run


def exchange(array):
    groups = [[y * 32 + i for y in range(4) for i in range(core, 32, 2)] for core in range(2)]
    return lax.all_to_all(array, AXES, 0, 0, axis_index_groups=groups, tiled=True)


def swap(array):
    return lax.ppermute(array, "fsdp", [(i, i ^ 1) for i in range(32)])


def local(
    tokens, segment_ids, qkv_weight, out_weight, up_weight, down_weight,
    qv_bias, out_bias, up_bias, norm_gain, norm_shift, cotangent,
):
    tile, full, low, square, side = ((TILES, D), BF), ((D, TOK), F32), ((D, TOK), BF), ((D, D), BF), ((D, 128), F32)
    probs, small, packed = ((HEADS, LONG, LONG), BF), ((HEADS, 128, 128), BF), ((G, D, TOK), BF)
    units = ((F, 256), BF)
    shards = (
        qkv_weight, out_weight, up_weight, down_weight, qv_bias, out_bias, up_bias.reshape(1, ROWS),
        norm_gain, norm_shift,
    )
    gathered = call(
        pack_kernel, [tile], [*((x.shape, x.dtype) for x in shards), ((ROWS, D), F32), ((128, 128), F32), ((2 * ROWS, D), BF)],
        "pack", 12, sems=(9, CHIPS // 2),
    )(*shards)[0]
    mine = exchange(gathered)
    turn, x_t, c_t = call(
        turn_kernel, [((TOK, TOK), BF), low, low], [], "turn", 60, flops=2 * 2 * TOK * TOK * D
    )(tokens, segment_ids, cotangent)
    mine, x_t = lax.optimization_barrier((mine, x_t))
    w_qkv, result, d_sum, d_packed, keep, send = call(
        layer_kernel,
        [square, low, full, packed, tile, tile],
        [tile, low, low, square, square, square, units, side, ((F, 1), F32), low, low, low, low, probs, small,
         low, full, full, ((F, TOK), BF), ((F, TOK), F32), full, full, ((F, TOK), BF), low, low, low,
         ((G, 256, TOK), BF), packed,
         square, square, square, units, side, ((2, LONG, LONG), F32), ((2, LONG, LONG), BF),
         ((2, 128, 128), BF), ((2, 256, TOK), F32)],
        "layer", 53, flops=40 * 10**9, near=(0, 2, 9, 10), held=(9, 10), sems=(6, 7),
    )(segment_ids, mine, pltpu.with_memory_space_constraint(swap(mine), pltpu.VMEM), x_t, c_t)
    chip = call(add_kernel, [tile], [tile], "chip_sum", 20, near=(0, 1), sems=(4,))(keep, swap(send))[0]
    chip, d_packed = lax.optimization_barrier((chip, d_packed))
    parts = exchange(chip)
    grad_tokens, output = call(
        token_kernel, [((TOK, D), F32), ((TOK, D), BF)], [low, low], "token_gradient", 60,
        flops=4 * 2 * TOK * TOK * D,
    )(w_qkv, d_packed, d_sum, turn, result)
    qkv, out, up, down, qv, outb, upb, gain, shift = call(
        sum_kernel,
        [((6, QKV), F32), ((6, D), F32), ((6, D), F32), ((ROWS, DG), F32), ((2, 6), F32), ((2, 6), F32),
         ((1, ROWS), F32), ((2, 6), F32), ((2, 6), F32)],
        [((128, 128), F32)], "slice_sum", 12,
    )(parts)
    return output, grad_tokens, qkv, out, up, down, qv, outb, upb.reshape(ROWS), gain, shift


def solution(mesh):
    rows, columns, flat = P(AXES, None), P(None, AXES), P(AXES)
    in_specs = (rows, rows, rows, rows, rows, rows, columns, columns, flat, columns, columns, rows)
    out_specs = (rows, rows, rows, rows, rows, rows, columns, columns, flat, columns, columns)
    return jax.shard_map(local, mesh=mesh, in_specs=in_specs, out_specs=out_specs, check_vma=False)
```

```python
import jax
import jax.numpy as jnp
from jax import lax
from jax.experimental import pallas as pl
from jax.experimental.pallas import tpu as pltpu
from jax.sharding import PartitionSpec as P

AXES = ("dp", "fsdp")
D = 768
F = 3072
G = 4
DG = 192
QKV = 3 * DG
HEADS = 12
HEAD = 64
TOK = 512
LONG = 384
CHIPS = 64
ROWS = 24
EPS = 1e-05
BAND = 64
BANDS = D // BAND
BF = jnp.bfloat16
F32 = jnp.float32
MIB = 1 << 20

SIDE = 18
WIDE = 2 * DG
TILES = CHIPS * ROWS


def dot(left, right, over_left, over_right):
    return lax.dot_general(
        left, right, (((over_left,), (over_right,)), ((), ())), preferred_element_type=F32
    )


def iota(shape, axis):
    return lax.broadcasted_iota(jnp.int32, shape, axis)


def each(count, step):
    for i in range(count):
        step(i)


def part(i, size):
    return slice(i * size, (i + 1) * size)


def halves(chunk):
    return jnp.sum(chunk.reshape(chunk.shape[0] // 8, 8, TOK), axis=0)


def means(count, bands):
    sums = [jnp.zeros((8, TOK), F32)] * count
    for i in range(BANDS):
        sums = [kept + halves(chunk) for kept, chunk in zip(sums, bands(part(i, BAND)), strict=True)]
    return [jnp.sum(total, axis=0, keepdims=True) * (1.0 / D) for total in sums]


class Moments:
    def add(self, chunk):
        if not hasattr(self, "near"):
            self.near = jnp.mean(chunk, axis=0, keepdims=True)
            self.sums = [jnp.zeros((8, TOK), F32)] * 2
        off = chunk - self.near
        self.sums = [self.sums[0] + halves(off), self.sums[1] + halves(off * off)]

    def result(self):
        off, square = (jnp.sum(total, axis=0, keepdims=True) * (1.0 / D) for total in self.sums)
        return self.near + off, lax.rsqrt(square - off * off + EPS)


def lane_sum(chunk):
    return jnp.sum(chunk, axis=1, keepdims=True)


def pick_hidden():
    return iota((192, 128), 1) - 8 == (iota((192, 128), 0) & 3)


def arrival(core, by_device, axis):
    sorted_row = iota((192, 1) if axis == 0 else (1, 192), axis)
    if by_device:
        device = (sorted_row * 2731) >> 16
        row = sorted_row - device * ROWS
    else:
        block = (sorted_row * 1366) >> 16
        sixth = (sorted_row * 10923) >> 16
        device = sixth - block * 8
        row = block * 6 + sorted_row - sixth * 6
    return jnp.where((device & 1) == core, 0, 96) + (device >> 1) * ROWS + row


def sorter(core, by_device=False):
    return (arrival(core, by_device, 0) == iota((192, 192), 1)).astype(F32).astype(BF)


def unsorter(core, by_device=False):
    return (arrival(core, by_device, 1) == iota((192, 192), 0)).astype(F32).astype(BF)


def grower():
    return ((iota((192, 48), 0) >> 2) == iota((192, 48), 1)).astype(F32).astype(BF)


def low_lanes():
    return iota((48, 128), 1) < 64


def pack_kernel(*refs):
    far, packed, near, (tile, square, twice, arrive, leave) = refs[:9], refs[9], refs[10:19], refs[19:]
    arriving = moves(zip(far, near, strict=True), arrive)
    start(*arriving)
    wait(*arriving)
    qkv, out, up, down, qv, outb, upb, gain, shift = near
    square[...] = jnp.zeros_like(square)
    for place, rows in enumerate((qv, outb, gain, shift)):
        square[2 * place : 2 * place + 2, 0:6] = rows[...].astype(F32)
    columns = square[...].T
    grown = jnp.where(iota((8, ROWS), 1) // 4 == iota((8, ROWS), 0), upb[...].astype(F32), 0.0)
    lanes = (iota((ROWS, 128), 1) - 8 == iota((ROWS, 128), 0) % 4).astype(F32)
    hidden = jnp.dot(grown, lanes, preferred_element_type=F32)
    tile[...] = jnp.zeros_like(tile)
    for block in range(4):
        rows, lanes = slice(6 * block, 6 * block + 6), slice(DG * block, DG * block + DG)
        here, there = (slice(0, DG), slice(DG, WIDE))[:: 1 - 2 * (block % 2)]
        tile[rows, here] = out[:, lanes].astype(F32)
        if block < 3:
            tile[rows, there] = qkv[:, lanes].astype(F32)
        tile[rows, WIDE : WIDE + DG] = up[:, lanes].astype(F32)
    tile[SIDE:ROWS, 0:128] = (columns[0:8] + hidden)[0:6]
    tile[:, WIDE + DG : D] = down[...].astype(F32)
    twice[0:ROWS, :] = tile[...].astype(BF)
    twice[ROWS:, :] = tile[...].astype(BF)
    pairs = [(twice, packed.at[2 * ROWS * pair : 2 * ROWS * (pair + 1), :]) for pair in range(CHIPS // 2)]
    leaving = moves(pairs, leave)
    start_behind(own_core(), *leaving)
    wait(*leaving)


def turn_kernel(tokens, segments, cotangent, turn, x_t, c_t):
    ids = segments[...]
    count0 = jnp.sum((ids == 0).astype(jnp.int32))
    count1 = jnp.sum((ids == 1).astype(jnp.int32))
    start = jnp.where(count0 == LONG, 0, jnp.where(count1 == LONG, count0, count0 + count1))

    def turn_rows(i):
        place = iota((64, TOK), 1) + start
        place = jnp.where(place >= TOK, place - TOK, place)
        turn[part(i, 64), :] = jnp.where(iota((64, TOK), 0) + i * 64 == place, 1.0, 0.0).astype(BF)

    each(8, turn_rows)

    def turn_features(i):
        x_t[part(i, 256), :] = dot(tokens[:, part(i, 256)], turn[...], 0, 0).astype(BF)
        c_t[part(i, 256), :] = dot(cotangent[:, part(i, 256)], turn[...], 0, 0).astype(BF)

    each(3, turn_features)


def moves(pairs, sems):
    return [pltpu.make_async_copy(source, target, sems.at[i]) for i, (source, target) in enumerate(pairs)]


def start(*copies):
    for copy in copies:
        copy.start()


def wait(*copies):
    for copy in copies:
        copy.wait()


def start_behind(core, *copies):
    def body(i, nothing):
        start(*copies)
        return nothing

    lax.fori_loop(0, 1 + (core >> 1), body, 0)


def own_core():
    return lax.rem(lax.axis_index("fsdp"), 2)


SPANS = (slice(0, LONG), slice(LONG, TOK))


def layer_kernel(
    segments, mine, other, x_far, c_far,
    w_qkv_far, result_far, d_sum_far, packed_far, keep, send,
    x_t, c_t, w_qkv, w_out, w_up, w_down, side, up_bias, q_t, k_t, v_t, ctx_t, probs, probs_small,
    first_low, hat, hat_two, active, slope, stream, d_first, d_upper, d_ctx, result, low_t, branch_pad, packed_t,
    g_qkv, g_out, g_up, g_down, g_side, scores, d_scores, d_few, work, arrive, leave,
):
    core = own_core()
    arriving = moves(
        [(x_far, x_t), (c_far, c_t)],
        arrive,
    )
    leaving = moves(
        [(w_qkv, w_qkv_far), (result, result_far), (stream, d_sum_far)]
        + [(packed_t.at[g], packed_far.at[g]) for g in range(G)],
        leave,
    )
    start(*arriving)
    sort, sort_devices, grow = sorter(core), sorter(core, True), grower()

    def both(i, lanes):
        rows = part(i, 96)
        return jnp.concatenate([mine[rows, lanes], other[rows, lanes]], axis=0)

    def place_attention(i):
        here = part(i, 48)
        placed = jnp.dot(sort, both(i, slice(0, WIDE)), preferred_element_type=F32).astype(BF)
        blocks = [placed[48 * block : 48 * block + 48] for block in range(4)]
        for begin, target, left, right in (
            (0, w_out, 0, 1), (WIDE, w_out, 2, 3), (0, w_qkv, 1, 0), (WIDE, w_qkv, 3, 2),
        ):
            target[here, begin : begin + 128] = blocks[left][:, 0:128]
            target[here, begin + 128 : begin + 256] = jnp.where(
                low_lanes(), blocks[left][:, 128:256], blocks[right][:, 128:256]
            )
            target[here, begin + 256 : begin + 384] = blocks[right][:, 256:384]
        side[here, :] = blocks[3][:, 0:128].astype(F32)

    def place_feed(i):
        here, units = part(i, 48), part(i, 192)
        placed = jnp.dot(sort, both(i, slice(WIDE, WIDE + 256)), preferred_element_type=F32).astype(BF)
        for block in range(4):
            w_up[here, DG * block : DG * block + DG] = placed[48 * block : 48 * block + 48, 0:DG]
        rows = jnp.dot(sort_devices, both(i, slice(512, 768)), preferred_element_type=F32)
        w_down[units, :] = rows.astype(BF)
        hidden = jnp.dot(grow, side[here, :].astype(BF), preferred_element_type=F32)
        up_bias[units, :] = lane_sum(jnp.where(pick_hidden(), hidden, 0.0))

    each(4, place_attention)
    wait(arriving[0])

    ids = segments[...]
    count0 = jnp.sum((ids == 0).astype(jnp.int32))
    count1 = jnp.sum((ids == 1).astype(jnp.int32))
    count2 = TOK - count0 - count1
    border = jnp.where(count0 == LONG, count1, jnp.where(count1 == LONG, count2, count0))
    together = (iota((128, 128), 0) < border) == (iota((128, 128), 1) < border)

    def project_in(g):
        rows = part(g, DG)
        packed = dot(w_qkv[rows, 0:WIDE], x_t[rows, :], 0, 0)
        k_t[rows, :] = packed[0:DG].astype(BF)
        q_t[rows, :] = ((packed[DG:WIDE] + side[rows, 0:1]).astype(BF).astype(F32) * 0.125).astype(BF)
        packed = dot(w_qkv[rows, 512:768], x_t[rows, :], 0, 0)
        v_t[rows, :] = (packed[64:256] + side[rows, 1:2]).astype(BF)

    def score(head):
        if head % 3 == 0:
            project_in(head // 3)
        rows = part(head, HEAD)
        scores[head % 2] = dot(k_t[rows, 0:LONG], q_t[rows, 0:LONG], 0, 0)

    def shares(logits):
        power = jnp.exp(logits - jnp.max(logits, axis=0, keepdims=True))
        return (power * (1.0 / jnp.sum(power, axis=0, keepdims=True))).astype(BF)

    def attend(head):
        for third in range(3):
            cols = part(third, 128)
            probs[head, :, cols] = shares(scores[head % 2, :, cols])
        rows = part(head, HEAD)
        few = dot(k_t[rows, LONG:TOK], q_t[rows, LONG:TOK], 0, 0)
        probs_small[head] = shares(jnp.where(together, few, -1000000000.0))

    def mix(head):
        rows = part(head, HEAD)
        ctx_t[rows, 0:LONG] = dot(v_t[rows, 0:LONG], probs[head], 1, 0).astype(BF)
        ctx_t[rows, LONG:TOK] = dot(v_t[rows, LONG:TOK], probs_small[head], 1, 0).astype(BF)

    meanwhile = ((4, 5), (6, 7), (8,), (9,), (10, 11), (12,), (13,), (14, 15), (), (), (), ())
    score(0)
    for head in range(HEADS):
        if head > 0:
            mix(head - 1)
        attend(head)
        if head + 1 < HEADS:
            score(head + 1)
        if head >= 8:
            each(4, lambda i, head=head: place_feed(4 * (head - 8) + i))
        each(len(meanwhile[head]), lambda i, blocks=meanwhile[head]: place_attention(blocks[i]))
    mix(HEADS - 1)

    moments_one = Moments()

    def project(i):
        rows = part(i, 128)
        attended = dot(w_out[:, rows], ctx_t[...], 0, 0) + side[rows, 2:3]
        total = x_t[rows, :].astype(F32) + attended
        stream[rows, :] = total
        moments_one.add(total)

    each(6, project)
    mean_one, scale_one = moments_one.result()

    def norm_one(i):
        rows = part(i, BAND)
        hats = (stream[rows, :] - mean_one) * scale_one
        hat[rows, :] = hats
        first = hats * side[rows, 4:5] + side[rows, 6:7]
        stream[rows, :] = first
        first_low[rows, :] = first.astype(BF)

    each(BANDS, norm_one)

    def raise_up(i):
        g, third = i // 3, i % 3
        rows = part(g, DG)
        work[i % 2] = dot(w_up[rows, 256 * third : 256 * third + 256], first_low[rows, :], 0, 0)

    def activate(i):
        for quarter in range(4):
            units = part(4 * i + quarter, 64)
            upper = work[i % 2, part(quarter, 64), :] + up_bias[units, :]
            below = 0.5 + 0.5 * lax.erf(upper * 0.7071067811865476)
            density = jnp.exp(-0.5 * upper * upper) * 0.3989422804014327
            active[units, :] = (upper * below).astype(BF)
            slope[units, :] = below + upper * density

    def bring_down(g):
        rows, units = part(g, DG), part(g, D)
        branch = dot(w_down[units, :], active[units, :], 0, 0)[64:256]
        total = stream[rows, :] + branch + side[rows, 3:4]
        stream[rows, :] = total
        moments_two.add(total)

    moments_two = Moments()
    raise_up(0)
    for i in range(12):
        if i + 1 < 12:
            raise_up(i + 1)
        if i % 3 == 0 and i > 0:
            bring_down(i // 3 - 1)
        activate(i)
    bring_down(3)
    wait(arriving[1])

    mean_two, scale_two = moments_two.result()

    def norm_two(rows):
        hats = (stream[rows, :] - mean_two) * scale_two
        hat_two[rows, :] = hats
        result[rows, :] = (hats * side[rows, 5:6] + side[rows, 7:8]).astype(BF)
        slopes = c_t[rows, :].astype(F32) * side[rows, 5:6]
        return slopes, slopes * hats

    lean_two, tilt_two = means(2, norm_two)
    for g in range(G):
        branch_pad[g, 0:64, :] = jnp.zeros((64, TOK), BF)

    def norm_two_back(i):
        rows = part(i, BAND)
        slopes = c_t[rows, :].astype(F32) * side[rows, 5:6]
        back = scale_two * (slopes - lean_two - hat_two[rows, :] * tilt_two)
        stream[rows, :] = back
        branch_pad[i // 3, 64 + BAND * (i % 3) : 128 + BAND * (i % 3), :] = back.astype(BF)

    each(BANDS, norm_two_back)

    def raise_back(i):
        work[i % 2] = dot(w_down[part(i, 256), :], branch_pad[i // 3], 1, 0)

    def activate_back(i):
        for quarter in range(4):
            units = part(4 * i + quarter, 64)
            d_upper[units, :] = (work[i % 2, part(quarter, 64), :] * slope[units, :]).astype(BF)

    def bring_back(g):
        rows = part(g, DG)
        slopes = stream[rows, :] + dot(w_up[rows, :], d_upper[part(g, D), :], 1, 0)
        d_first[rows, :] = slopes
        slopes = slopes * side[rows, 4:5]
        sums_one[:] = [sums_one[0] + halves(slopes), sums_one[1] + halves(slopes * hat[rows, :])]

    sums_one = [jnp.zeros((8, TOK), F32)] * 2
    raise_back(0)
    for i in range(12):
        if i + 1 < 12:
            raise_back(i + 1)
        if i % 3 == 0 and i > 0:
            bring_back(i // 3 - 1)
        activate_back(i)
    bring_back(3)

    lean_one, tilt_one = (jnp.sum(total, axis=0, keepdims=True) * (1.0 / D) for total in sums_one)

    def norm_one_back(i):
        rows, units = part(i, BAND), part(i, 256)
        back = scale_one * (d_first[rows, :] * side[rows, 4:5] - lean_one - hat[rows, :] * tilt_one)
        stream[rows, :] = back
        low_t[rows, :] = back.astype(BF)
        span = slice(256 * (i % 3), 256 * (i % 3) + 256)
        g_up[part(i // 3, DG), span] = dot(first_low[part(i // 3, DG), :], d_upper[units, :], 1, 1).astype(BF)
        g_down[units, :] = dot(active[units, :], branch_pad[i // 3], 1, 1).astype(BF)

    each(BANDS, norm_one_back)
    start_behind(core, *leaving[0:3])

    def project_back(i):
        rows = part(i, 128)
        d_ctx[rows, :] = dot(w_out[rows, :], low_t[...], 1, 0).astype(BF)

    def out_gradient(i):
        rows = part(i, 128)
        g_out[rows, :] = dot(ctx_t[rows, :], low_t[...], 1, 1).astype(BF)

    each(6, project_back)

    unsort, unsort_devices = unsorter(core), unsorter(core, True)

    def side_sums(i):
        rows = part(i, BAND)
        g_side[rows, :] = jnp.zeros((BAND, 128), F32)
        slopes = c_t[rows, :].astype(F32)
        g_side[rows, 5:6] = lane_sum(slopes * hat_two[rows, :])
        g_side[rows, 7:8] = lane_sum(slopes)
        slopes = d_first[rows, :]
        g_side[rows, 4:5] = lane_sum(slopes * hat[rows, :])
        g_side[rows, 6:7] = lane_sum(slopes)
        g_side[rows, 2:3] = lane_sum(low_t[rows, :].astype(F32))
        branch = branch_pad[i // 3, 64 + BAND * (i % 3) : 128 + BAND * (i % 3), :]
        g_side[rows, 3:4] = lane_sum(branch.astype(F32))
        units = part(i, 256)
        up_bias[units, :] = lane_sum(d_upper[units, :].astype(F32))

    def tile_feed(i):
        here, units, rows = part(i, 48), part(i, 192), part(i, 96)
        zero = jnp.zeros((48, 64), BF)
        ups = [jnp.concatenate([g_up[here, DG * block : DG * block + DG], zero], axis=1) for block in range(4)]
        placed = dot(unsort, jnp.concatenate(ups, axis=0), 1, 0)
        downs = dot(unsort_devices, g_down[units, :], 1, 0)
        for target, begin in ((keep, 0), (send, 96)):
            span = slice(begin, begin + 96)
            target[rows, 384:512] = placed[span, 0:128].astype(BF)
            target[rows, 512:640] = (placed[span, 128:256] + downs[span, 0:128]).astype(BF)
            target[rows, 640:768] = downs[span, 128:256].astype(BF)

    def score_back(head):
        rows = part(head, HEAD)
        scores[head % 2] = dot(v_t[rows, 0:LONG], d_ctx[rows, 0:LONG], 0, 0)

    def shares_back(share, d_share):
        return (share * (d_share - jnp.sum(d_share * share, axis=0, keepdims=True))).astype(BF)

    def attend_back(head):
        rows = part(head, HEAD)
        for third in range(3):
            cols = part(third, 128)
            d_scores[head % 2, :, cols] = shares_back(probs[head, :, cols].astype(F32), scores[head % 2, :, cols])
        few = dot(v_t[rows, LONG:TOK], d_ctx[rows, LONG:TOK], 0, 0)
        d_few[head % 2] = shares_back(probs_small[head].astype(F32), few)

    def mix_back(head):
        rows = part(head, HEAD)
        g, at = head // 3, HEAD * (head % 3)
        for cols, share, d_score in (
            (slice(0, LONG), probs[head], d_scores[head % 2]),
            (slice(LONG, TOK), probs_small[head], d_few[head % 2]),
        ):
            packed_t[g, 3 * DG + at : 3 * DG + at + HEAD, cols] = dot(d_ctx[rows, cols], share, 1, 1).astype(BF)
            packed_t[g, DG + at : DG + at + HEAD, cols] = (0.125 * dot(k_t[rows, cols], d_score, 1, 0)).astype(BF)
            packed_t[g, at : at + HEAD, cols] = dot(q_t[rows, cols], d_score, 1, 1).astype(BF)
        side_sums(head)
        tile_feed(head)

    def project_in_back(g):
        rows = part(g, DG)
        packed_t[g, WIDE : 3 * DG, :] = jnp.zeros((DG, TOK), BF)
        g_qkv[rows, 0:WIDE] = dot(x_t[rows, :], packed_t[g, 0:WIDE, :], 1, 1).astype(BF)
        g_qkv[rows, 512:768] = dot(x_t[rows, :], packed_t[g, 512:768, :], 1, 1).astype(BF)
        g_side[rows, 0:1] = lane_sum(packed_t[g, DG:WIDE, :].astype(F32))
        g_side[rows, 1:2] = lane_sum(packed_t[g, 3 * DG :, :].astype(F32))
        tile_feed(12 + g)

    def tile_attention(i):
        here, units, rows = part(i, 48), part(i, 192), part(i, 96)
        hidden = jnp.where(pick_hidden(), up_bias[units, :], 0.0).astype(BF)
        bias = (g_side[here, :] + dot(grow, hidden, 0, 0)).astype(BF)
        blocks = []
        for begin in (0, WIDE):
            mixed_out, mixed_qkv = g_out[here, begin + 128 : begin + 256], g_qkv[here, begin + 128 : begin + 256]
            for odd in range(2):
                first = (g_qkv[here, 0:128] if begin == 0 else bias) if odd else g_out[here, begin : begin + 128]
                left, right = (mixed_qkv, mixed_out) if odd else (mixed_out, mixed_qkv)
                last = (g_out if odd else g_qkv)[here, begin + 256 : begin + 384]
                blocks.append(jnp.concatenate([first, jnp.where(low_lanes(), left, right), last], axis=1))
        placed = dot(unsort, jnp.concatenate(blocks, axis=0), 1, 0).astype(BF)
        keep[rows, 0:WIDE] = placed[0:96]
        send[rows, 0:WIDE] = placed[96:192]

    score_back(0)
    for head in range(HEADS):
        if head + 1 < HEADS:
            score_back(head + 1)
        if head > 0:
            mix_back(head - 1)
            if head % 3 == 0:
                project_in_back(head // 3 - 1)
        attend_back(head)
        if head < 3:
            each(2, lambda i, head=head: out_gradient(2 * head + i))
        if head > 2:
            block = (head // 3 - 1) * 4 + head % 3
            tile_attention(block)
            if head % 3 == 2:
                tile_attention(block + 1)
        if head == 7:
            start_behind(core, *leaving[3:5])
    mix_back(HEADS - 1)
    project_in_back(G - 1)
    start_behind(core, *leaving[5:7])
    each(4, lambda i: tile_attention(12 + i))
    wait(*leaving)


def token_kernel(w_qkv, packed_t, d_sum, turn, result, grad_tokens, output, high, low):
    def total(g):
        rows = part(g, DG)
        back = dot(w_qkv[rows, 0:WIDE], packed_t[g, 0:WIDE, :], 1, 0)
        whole = d_sum[rows, :] + back + dot(w_qkv[rows, 512:768], packed_t[g, 512:768, :], 1, 0)
        high[rows, :] = whole.astype(BF)
        low[rows, :] = (whole - high[rows, :].astype(F32)).astype(BF)

    each(G, total)

    def write(i):
        rows = part(i, 256)
        grad_tokens[:, rows] = dot(turn[...], high[rows, :], 1, 1) + dot(turn[...], low[rows, :], 1, 1)
        output[:, rows] = dot(turn[...], result[rows, :], 1, 1).astype(BF)

    each(3, write)


def add_kernel(left, right, total_far, total, leave):
    rows = [part(i, TILES // 4) for i in range(4)]
    leaving = moves([(total.at[span, :], total_far.at[span, :]) for span in rows], leave)
    for i, span in enumerate(rows):
        total[span, :] = (left[span, :].astype(F32) + right[span, :].astype(F32)).astype(BF)
        start_behind(own_core(), leaving[i])
    wait(*leaving)


def sum_kernel(parts, qkv, out, up, down, qv, outb, upb, gain, shift, square):
    total = jnp.zeros((2 * ROWS, D), F32)
    for pair in range(CHIPS // 2):
        total += parts[part(pair, 2 * ROWS), :].astype(F32)
    total = total[0:ROWS] + total[ROWS:]
    for block in range(4):
        rows, lanes = slice(6 * block, 6 * block + 6), slice(DG * block, DG * block + DG)
        here, there = (slice(0, DG), slice(DG, WIDE))[:: 1 - 2 * (block % 2)]
        out[:, lanes] = total[rows, here]
        if block < 3:
            qkv[:, lanes] = total[rows, there]
        up[:, lanes] = total[rows, WIDE : WIDE + DG]
    down[...] = total[:, WIDE + DG : D]
    square[...] = jnp.zeros_like(square)
    square[0:6, :] = total[SIDE:ROWS, 0:128]
    columns = square[...].T
    for place, rows in enumerate((qv, outb, gain, shift)):
        rows[...] = columns[2 * place : 2 * place + 2, 0:6]
    lanes = (iota((128, ROWS), 0) - 8 == iota((128, ROWS), 1) % 4).astype(F32)
    grown = jnp.dot(square[0:8, :], lanes, preferred_element_type=F32, precision=lax.Precision.HIGHEST)
    grown = jnp.where(iota((8, ROWS), 1) // 4 == iota((8, ROWS), 0), grown, 0.0)
    upb[...] = jnp.sum(grown, axis=0, keepdims=True)


FAR = pl.BlockSpec(memory_space=pl.ANY)
NEAR = pl.BlockSpec(memory_space=pltpu.VMEM)


def call(kernel, shapes, scratch, name, limit, flops=0, near=(), held=(), sems=()):
    scratch = [pltpu.VMEM(*shape) for shape in scratch] + [pltpu.SemaphoreType.DMA((count,)) for count in sems]

    def specs(count, base):
        return [NEAR if not sems or base + i in near else FAR for i in range(count)]

    def run(*inputs):
        if sems:
            inputs = [x if i in near else pltpu.with_memory_space_constraint(x, pltpu.HBM) for i, x in enumerate(inputs)]
        return pl.pallas_call(
            kernel,
            in_specs=specs(len(inputs), 0),
            out_specs=specs(len(shapes), len(inputs)),
            out_shape=[
                (pltpu.VMEM if len(inputs) + i in held else pltpu.HBM)(*shape)
                if sems and (len(inputs) + i in held or len(inputs) + i not in near)
                else jax.ShapeDtypeStruct(*shape)
                for i, shape in enumerate(shapes)
            ],
            scratch_shapes=scratch,
            compiler_params=pltpu.CompilerParams(vmem_limit_bytes=limit * MIB),
            cost_estimate=pl.CostEstimate(flops=flops, bytes_accessed=0, transcendentals=0),
            name=name,
        )(*inputs)

    return run


def exchange(array):
    groups = [[y * 32 + i for y in range(4) for i in range(core, 32, 2)] for core in range(2)]
    return lax.all_to_all(array, AXES, 0, 0, axis_index_groups=groups, tiled=True)


def swap(array):
    return lax.ppermute(array, "fsdp", [(i, i ^ 1) for i in range(32)])


def local(
    tokens, segment_ids, qkv_weight, out_weight, up_weight, down_weight,
    qv_bias, out_bias, up_bias, norm_gain, norm_shift, cotangent,
):
    tile, full, low, square, side = ((TILES, D), BF), ((D, TOK), F32), ((D, TOK), BF), ((D, D), BF), ((D, 128), F32)
    probs, small, packed = ((HEADS, LONG, LONG), BF), ((HEADS, 128, 128), BF), ((G, D, TOK), BF)
    units = ((F, 256), BF)
    shards = (
        qkv_weight, out_weight, up_weight, down_weight, qv_bias, out_bias, up_bias.reshape(1, ROWS),
        norm_gain, norm_shift,
    )
    gathered = call(
        pack_kernel, [tile], [*((x.shape, x.dtype) for x in shards), ((ROWS, D), F32), ((128, 128), F32), ((2 * ROWS, D), BF)],
        "pack", 12, sems=(9, CHIPS // 2),
    )(*shards)[0]
    mine = exchange(gathered)
    turn, x_t, c_t = call(
        turn_kernel, [((TOK, TOK), BF), low, low], [], "turn", 60, flops=2 * 2 * TOK * TOK * D
    )(tokens, segment_ids, cotangent)
    mine, x_t = lax.optimization_barrier((mine, x_t))
    w_qkv, result, d_sum, d_packed, keep, send = call(
        layer_kernel,
        [square, low, full, packed, tile, tile],
        [low, low, square, square, square, units, side, ((F, 1), F32), low, low, low, low, probs, small,
         low, full, full, ((F, TOK), BF), ((F, TOK), F32), full, full, ((F, TOK), BF), low, low, low,
         ((G, 256, TOK), BF), packed,
         square, square, square, units, side, ((2, LONG, LONG), F32), ((2, LONG, LONG), BF),
         ((2, 128, 128), BF), ((2, 256, TOK), F32)],
        "layer", 51, flops=40 * 10**9, near=(0, 1, 2, 9, 10), held=(9, 10), sems=(2, 7),
    )(segment_ids, *(pltpu.with_memory_space_constraint(x, pltpu.VMEM) for x in (mine, swap(mine))), x_t, c_t)
    chip = call(add_kernel, [tile], [tile], "chip_sum", 20, near=(0, 1), sems=(4,))(keep, swap(send))[0]
    chip, d_packed = lax.optimization_barrier((chip, d_packed))
    parts = exchange(chip)
    grad_tokens, output = call(
        token_kernel, [((TOK, D), F32), ((TOK, D), BF)], [low, low], "token_gradient", 60,
        flops=4 * 2 * TOK * TOK * D,
    )(w_qkv, d_packed, d_sum, turn, result)
    qkv, out, up, down, qv, outb, upb, gain, shift = call(
        sum_kernel,
        [((6, QKV), F32), ((6, D), F32), ((6, D), F32), ((ROWS, DG), F32), ((2, 6), F32), ((2, 6), F32),
         ((1, ROWS), F32), ((2, 6), F32), ((2, 6), F32)],
        [((128, 128), F32)], "slice_sum", 12,
    )(parts)
    return output, grad_tokens, qkv, out, up, down, qv, outb, upb.reshape(ROWS), gain, shift


def solution(mesh):
    rows, columns, flat = P(AXES, None), P(None, AXES), P(AXES)
    in_specs = (rows, rows, rows, rows, rows, rows, columns, columns, flat, columns, columns, rows)
    out_specs = (rows, rows, rows, rows, rows, rows, columns, columns, flat, columns, columns)
    return jax.shard_map(local, mesh=mesh, in_specs=in_specs, out_specs=out_specs, check_vma=False)
```
